32 devices in a mesh: groups: 2 (over x), river: 8 (over z, y), hand: 2 (over core).
Axes of the slice: x: 2, y: 2, z: 4, core: 2. Of those that a mesh axis runs over, the one named last changes fastest.
Arguments:
- hand_rank: int32 [192, 1326], P(('groups', 'river'), 'hand'), parts along dimension 0, may hold values from -1 to 7461, as said below
- loads: int32 [16], P('groups'), parts along dimension 0, may hold values from 3 to 12, as said below
- turn_cards: int32 [8], P('groups'), parts along dimension 0, may hold values from 0 to 51, as said below
- turn_children: int32 [6, 16], replicated, may hold values from 0 to 1, as said below
- turn_parents: int32 [6, 16], replicated, may hold values from 0 to 1, as said below
- river_children: int32 [16, 64], replicated, may hold values from 0 to 1, as said below
- river_parents: int32 [16, 80], replicated, may hold values from 0 to 1, as said below
- showdown_pot: float32 [64, 64], replicated, may hold values from 0 to 0.0625
- river_fold: float32 [64, 64], replicated, may hold values from -0.75 to 0.75
- turn_fold: float32 [16, 16], replicated, may hold values from -1.5 to 1.5
- mover_turn: float32 [32, 1326], P('groups', 'hand'), parts along dimension 0, may hold values from 0 to 2
- mover_river: float32 [192, 64, 1326], P(('groups', 'river'), None, 'hand'), parts along dimension 0, may hold values from 0 to 120
- mover_turn_price: float32 [12, 1326], P('groups', 'hand'), parts along dimension 0, may hold values from -6 to 6
- mover_river_price: float32 [192, 16, 1326], P(('groups', 'river'), None, 'hand'), parts along dimension 0, may hold values from -120 to 120
- rival_turn: float32 [32, 1326], P('groups', 'hand'), parts along dimension 0, may hold values from 0 to 2
- rival_river: float32 [192, 64, 1326], P(('groups', 'river'), None, 'hand'), parts along dimension 0, may hold values from 0 to 120
- rival_turn_price: float32 [12, 1326], P('groups', 'hand'), parts along dimension 0, may hold values from -6 to 6
- rival_river_price: float32 [192, 16, 1326], P(('groups', 'river'), None, 'hand'), parts along dimension 0, may hold values from -120 to 120
Outputs:
- next_mover_turn: float32 [32, 1326], P('groups', 'hand'), parts along dimension 0
- next_mover_river: float32 [192, 64, 1326], P(('groups', 'river'), None, 'hand'), parts along dimension 0
- next_mover_turn_price: float32 [12, 1326], P('groups', 'hand'), parts along dimension 0
- next_mover_river_price: float32 [192, 16, 1326], P(('groups', 'river'), None, 'hand'), parts along dimension 0
- next_rival_turn: float32 [32, 1326], P('groups', 'hand'), parts along dimension 0
- next_rival_river: float32 [192, 64, 1326], P(('groups', 'river'), None, 'hand'), parts along dimension 0
- next_rival_turn_price: float32 [12, 1326], P('groups', 'hand'), parts along dimension 0
- next_rival_river_price: float32 [192, 16, 1326], P(('groups', 'river'), None, 'hand'), parts along dimension 0
The draws below stay inside these ranges and needn't reach their ends.
There are 2 independent parts, one for each index of `groups`. The reference program is written for one: setup_inputs(seed, part) draws one part's arguments, and reference() takes and returns one part's arrays. A program takes and returns all parts, laid end to end along the dimension named above; an argument that names none is the same for every part. Nothing has to cross between parts.
Inputs may be any that keep to these rules, and one draw needn't show every extreme that they name: hand_rank is -1 exactly where a hand holds one of turn_cards or the slot's river card, and on every hand of an unused slot; the used slots of the river devices, taken in order, hold the 48 cards not in turn_cards, once each. The loads sum to 48; some river device holds 12. `turn_cards`: four different cards. `turn_children`: each turn sequence starts at exactly one decision point; each decision point starts one or more sequences, in a run of consecutive indices, the runs in order of the decision points. `turn_parents`: decision point 0 has no parent sequence; every other one has exactly one, a sequence starting at an earlier decision point. `river_children`: each river sequence starts at exactly one decision point; each decision point starts one or more sequences, in a run of consecutive indices, the runs in order of the decision points. `river_parents`: every river decision point has exactly one parent: a river sequence starting at an earlier decision point, or a turn sequence (the last 16 columns); decision point 0 has a turn sequence.
All inputs are finite; a program needn't handle non-finite values.
Results may differ from the reference program's by a relative error of at most 0.0003.
Values sent between devices are 32-bit elements; how exact they have to be, the bound alone decides.
No kernel may reach another device: no remote copies, remote signals or barrier semaphores. Data moves between devices by JAX's collectives and lax.ppermute only.
A program may use at most 192 MiB of HBM per device.

```python
import math
import jax
import jax.numpy as jnp
import numpy as np
from jax import lax

CARDS = 52
H = 1326
BOARDS = 48
RS = 64
QR = 16
TS = 16
QT = 6
RANKS = 7462
ITERS = 2
BASE = 3
SLOTS = 12
N_RIVER = 8


def deal_cards(key):
    key = jax.random.fold_in(key, 101)
    return jax.random.permutation(key, CARDS).astype(jnp.int32)


def spread_loads(key):
    key = jax.random.fold_in(key, 202)
    first_key, second_key = jax.random.split(key)
    room = SLOTS - BASE
    total = N_RIVER * room
    owner = jnp.arange(total, dtype=jnp.int32) // room
    busiest = jax.random.randint(first_key, (), 0, N_RIVER)
    order = jax.random.permutation(second_key, total).astype(jnp.int32)
    score = order - jnp.where(owner == busiest, total, 0)
    place = jnp.argsort(jnp.argsort(score))
    chosen = place < BOARDS - BASE * N_RIVER
    hits = (owner[None, :] == jnp.arange(N_RIVER, dtype=jnp.int32)[:, None]) & chosen[None, :]
    return (BASE + jnp.sum(hits.astype(jnp.int32), axis=1)).astype(jnp.int32)


def split_sequences(key, sequences, points):
    cuts = jnp.sort(jax.random.permutation(key, sequences - 1)[:points - 1] + 1).astype(jnp.int32)
    starts = jnp.concatenate([jnp.zeros((1,), jnp.int32), cuts])
    member = jnp.sum((jnp.arange(sequences, dtype=jnp.int32)[:, None] >= starts[None, :]).astype(jnp.int32), axis=1) - 1
    children = (member[None, :] == jnp.arange(points, dtype=jnp.int32)[:, None]).astype(jnp.int32)
    return (starts, children)


def river_tree(key):
    key = jax.random.fold_in(key, 303)
    first_key, second_key = jax.random.split(key)
    starts, children = split_sequences(first_key, RS, QR)
    pick = jax.random.randint(second_key, (QR,), 0, 1 << 20) % (starts + TS)
    column = jnp.where(pick < starts, pick, RS + pick - starts)
    parents = (jnp.arange(RS + TS, dtype=jnp.int32)[None, :] == column[:, None]).astype(jnp.int32)
    return (children, parents)


def turn_tree(key):
    key = jax.random.fold_in(key, 404)
    first_key, second_key = jax.random.split(key)
    starts, children = split_sequences(first_key, TS, QT)
    pick = jax.random.randint(second_key, (QT,), 0, 1 << 20) % jnp.maximum(starts, 1)
    parents = (jnp.arange(TS, dtype=jnp.int32)[None, :] == pick[:, None]) & (jnp.arange(QT, dtype=jnp.int32)[:, None] > 0)
    return (children, parents.astype(jnp.int32))


def spread_field(key, values):
    row_key, col_key = jax.random.split(key)
    rows = values.shape[1]
    row_scale = jnp.exp(jax.random.uniform(row_key, (N_RIVER * SLOTS, rows, 1), minval=0.0, maxval=math.log(10.0)))
    col_scale = jnp.exp(jax.random.uniform(col_key, (N_RIVER * SLOTS, 1, H), minval=0.0, maxval=math.log(10.0)))
    device = (jnp.arange(N_RIVER * SLOTS) // SLOTS).astype(jnp.float32)
    rise = 1.0 + 2.0 * device / (N_RIVER - 1)
    return (values * row_scale * col_scale * rise[:, None, None] / 20.0).astype(jnp.float32)


def draw_loads(key, part):
    return spread_loads(key)


def draw_turn_cards(key, part):
    return deal_cards(key)[:4]


def draw_hand_rank(key, part):
    cards = deal_cards(key)
    loads = spread_loads(key)
    key = jax.random.fold_in(key, 5)
    slot_ids = jnp.arange(N_RIVER * SLOTS, dtype=jnp.int32)
    device = slot_ids // SLOTS
    within = slot_ids % SLOTS
    used = within < loads[device]
    board = (jnp.cumsum(loads) - loads)[device] + within
    river = cards[4 + jnp.clip(board, 0, BOARDS - 1)]
    pairs = np.triu_indices(CARDS, 1)
    card_one = jnp.asarray(pairs[0].astype(np.int32))
    card_two = jnp.asarray(pairs[1].astype(np.int32))
    turn = cards[:4]
    held_turn = ((card_one[:, None] == turn[None, :]) | (card_two[:, None] == turn[None, :])).any(axis=1)
    held_river = (card_one[None, :] == river[:, None]) | (card_two[None, :] == river[:, None])
    ranks = jax.random.randint(key, (N_RIVER * SLOTS, H), 0, RANKS)
    dead = held_turn[None, :] | held_river | jnp.logical_not(used)[:, None]
    return jnp.where(dead, -1, ranks).astype(jnp.int32)


def draw_turn_children(key, part):
    return turn_tree(key)[0]


def draw_turn_parents(key, part):
    return turn_tree(key)[1]


def draw_river_children(key, part):
    return river_tree(key)[0]


def draw_river_parents(key, part):
    return river_tree(key)[1]


def draw_mover_river(key, part):
    key = jax.random.fold_in(key, 11)
    second_key = jax.random.fold_in(key, 1)
    third_key = jax.random.fold_in(key, 2)
    values = jnp.abs(jax.random.normal(second_key, (N_RIVER * SLOTS, RS, H)))
    return spread_field(third_key, values)


def draw_rival_river(key, part):
    key = jax.random.fold_in(key, 12)
    second_key = jax.random.fold_in(key, 1)
    third_key = jax.random.fold_in(key, 2)
    values = jnp.abs(jax.random.normal(second_key, (N_RIVER * SLOTS, RS, H)))
    return spread_field(third_key, values)


def draw_mover_river_price(key, part):
    key = jax.random.fold_in(key, 13)
    second_key = jax.random.fold_in(key, 1)
    third_key = jax.random.fold_in(key, 2)
    values = jax.random.normal(second_key, (N_RIVER * SLOTS, QR, H))
    return spread_field(third_key, values)


def draw_rival_river_price(key, part):
    key = jax.random.fold_in(key, 14)
    second_key = jax.random.fold_in(key, 1)
    third_key = jax.random.fold_in(key, 2)
    values = jax.random.normal(second_key, (N_RIVER * SLOTS, QR, H))
    return spread_field(third_key, values)


def levels(rng, shape, cuts, low, top_value):
    def one(axis_at, parts):
        heights = jax.random.uniform(jax.random.fold_in(jax.random.fold_in(rng, 6), axis_at), (parts,), jnp.float32, low / len(cuts), top_value / len(cuts))
        return jnp.repeat(jnp.exp(heights), shape[axis_at] // parts).reshape((-1,) + (1,) * (len(shape) - axis_at - 1))

    loudness = one(*cuts[0])
    for cut in cuts[1:]:
        loudness = loudness * one(*cut)
    return loudness


def bell_draw(stream_key, shape, width, limit, shards=(), kind=jnp.bfloat16):
    gain = levels(stream_key, shape, shards, -0.22, 0.18) if shards else 1.0
    drawn = jax.random.normal(stream_key, shape, jnp.float32) * width * gain
    return jnp.minimum(jnp.maximum(drawn, -limit), limit).astype(kind)


def setup_inputs(seed: int = 0, part: int = 0) -> dict:
    keys = jax.random.split(jax.random.key(seed), 19)
    own_keys = jax.random.split(jax.random.fold_in(keys[18], part), 19)
    return {
        "hand_rank": draw_hand_rank(jax.random.fold_in(jax.random.fold_in(keys[18], part), 71), part),
        "loads": draw_loads(jax.random.fold_in(jax.random.fold_in(keys[18], part), 71), part),
        "turn_cards": draw_turn_cards(jax.random.fold_in(jax.random.fold_in(keys[18], part), 71), part),
        "turn_children": draw_turn_children(jax.random.fold_in(keys[18], 71), part),
        "turn_parents": draw_turn_parents(jax.random.fold_in(keys[18], 71), part),
        "river_children": draw_river_children(jax.random.fold_in(keys[18], 71), part),
        "river_parents": draw_river_parents(jax.random.fold_in(keys[18], 71), part),
        "showdown_pot": jnp.clip(jax.random.uniform(keys[7], (RS, RS), jnp.float32, 0.0, 0.0625), 0.0, 0.0625),
        "river_fold": bell_draw(keys[8], (RS, RS), RS ** -0.5, 0.75, (), jnp.float32),
        "turn_fold": bell_draw(keys[9], (TS, TS), TS ** -0.5, 1.5, (), jnp.float32),
        "mover_turn": jnp.clip(2.0 * jax.random.uniform(own_keys[10], (TS, H), jnp.float32) ** levels(own_keys[10], (TS, H), ((1, 2),), -0.2, 0.2), 0.0, 2.0),
        "mover_river": draw_mover_river(jax.random.fold_in(jax.random.fold_in(keys[18], part), 71), part),
        "mover_turn_price": bell_draw(own_keys[12], (QT, H), 1.0, 6.0, ((1, 2),), jnp.float32),
        "mover_river_price": draw_mover_river_price(jax.random.fold_in(jax.random.fold_in(keys[18], part), 71), part),
        "rival_turn": jnp.clip(2.0 * jax.random.uniform(own_keys[14], (TS, H), jnp.float32) ** levels(own_keys[14], (TS, H), ((1, 2),), -0.2, 0.2), 0.0, 2.0),
        "rival_river": draw_rival_river(jax.random.fold_in(jax.random.fold_in(keys[18], part), 71), part),
        "rival_turn_price": bell_draw(own_keys[16], (QT, H), 1.0, 6.0, ((1, 2),), jnp.float32),
        "rival_river_price": draw_rival_river_price(jax.random.fold_in(jax.random.fold_in(keys[18], part), 71), part),
    }


HIGH = lax.Precision.HIGHEST
STEP_SCALE = 0.25
EPSILON = 1e-06

def card_tables():
    pairs = np.triu_indices(CARDS, 1)
    return (jnp.asarray(pairs[0].astype(np.int32)), jnp.asarray(pairs[1].astype(np.int32)))

def reference(hand_rank, loads, turn_cards, turn_children, turn_parents, river_children, river_parents, showdown_pot, river_fold, turn_fold, mover_turn, mover_river, mover_turn_price, mover_river_price, rival_turn, rival_river, rival_turn_price, rival_river_price):
    card_one, card_two = card_tables()
    deck = jnp.arange(CARDS, dtype=jnp.int32)
    incidence = ((card_one[:, None] == deck[None, :]) | (card_two[:, None] == deck[None, :])).astype(jnp.float32)
    held = ((card_one[:, None] == turn_cards[None, :]) | (card_two[:, None] == turn_cards[None, :])).any(axis=1)
    turn_live = 1.0 - held.astype(jnp.float32)
    shared = (card_one[:, None] == card_one[None, :]) | (card_one[:, None] == card_two[None, :]) | (card_two[:, None] == card_one[None, :]) | (card_two[:, None] == card_two[None, :])
    compat = 1.0 - shared.astype(jnp.float32)
    slot_ids = jnp.arange(N_RIVER * SLOTS, dtype=jnp.int32)
    slot_used = (slot_ids % SLOTS < loads[slot_ids // SLOTS]).astype(jnp.float32)
    live = (hand_rank >= 0).astype(jnp.float32) * slot_used[:, None] * turn_live[None, :]
    live_three = live[:, None, :]
    turn_step = (turn_children - turn_parents).astype(jnp.float32)
    turn_root = 1.0 - lax.optimization_barrier(jnp.sum(turn_parents, axis=1)).astype(jnp.float32)
    river_step = (river_children - river_parents[:, :RS]).astype(jnp.float32)
    river_link = river_parents[:, RS:].astype(jnp.float32)
    total_count = (TS + QT) * H + N_RIVER * SLOTS * (RS + QR) * H

    def turn_mix(plan):
        weighted = turn_live[None, :] * plan
        card_sums = jnp.dot(weighted, incidence, precision=HIGH)
        totals = lax.optimization_barrier(jnp.sum(weighted, axis=1))
        near = jnp.dot(card_sums, incidence.T, precision=HIGH)
        return turn_live[None, :] * (totals[:, None] - near + turn_live[None, :] * plan)

    def river_mix(plans, direction, pot_matrix, fold_matrix):

        def one_board(args):
            plan, rank, alive = args
            indicator = compat * alive[:, None] * alive[None, :]
            signs = jnp.sign(rank[None, :] - rank[:, None]).astype(jnp.float32) * direction
            blocks = jnp.stack([signs * indicator, indicator])
            mixed = jnp.einsum('tb,kab->kta', plan, blocks, precision=HIGH)
            return (jnp.dot(pot_matrix, mixed[0], precision=HIGH) + jnp.dot(fold_matrix, mixed[1], precision=HIGH)) / H
        return lax.map(one_board, (plans, hand_rank, live))

    def link_sum(mult):
        return jnp.einsum('qt,bqh->th', river_link, live_three * mult, precision=HIGH)

    def squares(*arrays):
        return sum((jnp.sum(item * item) for item in arrays))
    mover_turn = turn_live[None, :] * mover_turn
    mover_turn_price = turn_live[None, :] * mover_turn_price
    rival_turn = turn_live[None, :] * rival_turn
    rival_turn_price = turn_live[None, :] * rival_turn_price
    mover_river = live_three * mover_river
    mover_river_price = live_three * mover_river_price
    rival_river = live_three * rival_river
    rival_river_price = live_three * rival_river_price
    for step in range(ITERS):
        norm_mover = squares(mover_turn, mover_turn_price, mover_river, mover_river_price)
        norm_rival = squares(rival_turn, rival_turn_price, rival_river, rival_river_price)
        weight = jnp.sqrt((norm_rival / total_count + EPSILON) / (norm_mover / total_count + EPSILON))
        primal_step = STEP_SCALE / weight
        dual_step = STEP_SCALE * weight
        grad_turn = jnp.dot(turn_fold, turn_mix(rival_turn), precision=HIGH) / H + turn_live[None, :] * (jnp.dot(turn_step.T, rival_turn_price, precision=HIGH) - link_sum(rival_river_price))
        grad_river = river_mix(rival_river, 1.0, showdown_pot, river_fold) + live_three * jnp.einsum('qs,bqh->bsh', river_step, rival_river_price, precision=HIGH)
        new_turn = turn_live[None, :] * jnp.maximum(mover_turn - primal_step * grad_turn, 0.0)
        new_river = live_three * jnp.maximum(mover_river - primal_step * grad_river, 0.0)
        new_turn_price = mover_turn_price + primal_step * turn_live[None, :] * (jnp.dot(turn_step, rival_turn, precision=HIGH) - turn_root[:, None])
        new_river_price = mover_river_price + primal_step * live_three * (jnp.einsum('qs,bsh->bqh', river_step, rival_river, precision=HIGH) - jnp.dot(river_link, rival_turn, precision=HIGH)[None])
        turn_bar = 2.0 * new_turn - mover_turn
        river_bar = 2.0 * new_river - mover_river
        turn_price_bar = 2.0 * new_turn_price - mover_turn_price
        river_price_bar = 2.0 * new_river_price - mover_river_price
        mover_turn, mover_river, mover_turn_price, mover_river_price = (new_turn, new_river, new_turn_price, new_river_price)
        rise_turn = jnp.dot(turn_fold.T, turn_mix(turn_bar), precision=HIGH) / H - turn_live[None, :] * (jnp.dot(turn_step.T, turn_price_bar, precision=HIGH) - link_sum(river_price_bar))
        rise_river = river_mix(river_bar, -1.0, showdown_pot.T, river_fold.T) - live_three * jnp.einsum('qs,bqh->bsh', river_step, river_price_bar, precision=HIGH)
        new_rival_turn = turn_live[None, :] * jnp.maximum(rival_turn + dual_step * rise_turn, 0.0)
        new_rival_river = live_three * jnp.maximum(rival_river + dual_step * rise_river, 0.0)
        rival_turn_price = rival_turn_price + dual_step * turn_live[None, :] * (jnp.dot(turn_step, turn_bar, precision=HIGH) - turn_root[:, None])
        rival_river_price = rival_river_price + dual_step * live_three * (jnp.einsum('qs,bsh->bqh', river_step, river_bar, precision=HIGH) - jnp.dot(river_link, turn_bar, precision=HIGH)[None])
        rival_turn, rival_river = (new_rival_turn, new_rival_river)
    return (mover_turn, mover_river, mover_turn_price, mover_river_price, rival_turn, rival_river, rival_turn_price, rival_river_price)
```

```python
import functools

import jax
import jax.numpy as jnp
import ml_dtypes
import numpy as np
from jax import lax
from jax.experimental import pallas as pl
from jax.experimental.pallas import tpu as pltpu
from jax.sharding import PartitionSpec as P

CARDS = 52
H = 1326
ITERS = 2
STEP_SCALE = 0.25
EPSILON = 1e-06
HIGH = lax.Precision.HIGHEST
LANES = 128
TILE = 256
VMEM_BYTES = 56 * 2**20
F32 = jnp.float32
BF16 = jnp.bfloat16


def round_up(value, unit):
    return -(-value // unit) * unit


def halves(width, padded):
    pairs = np.stack(np.triu_indices(CARDS, 1)).astype(np.int32)
    deck = np.arange(CARDS)
    incidence = (pairs[0][:, None] == deck) | (pairs[1][:, None] == deck)
    parts = pairs.shape[1] // width
    cards = np.full((parts, 8, 2 * padded), -1, np.int32)
    compat = np.zeros((parts, 2 * padded, padded), np.float32)
    gather = np.zeros((parts, 2 * padded, LANES), np.float32)
    spread = np.zeros((parts, LANES, 2 * padded), np.float32)
    for part in range(parts):
        own = slice(part * width, (part + 1) * width)
        for place, half in enumerate((part, 1 - part)):
            far = slice(half * width, (half + 1) * width)
            rows = slice(place * padded, place * padded + width)
            cards[part, :2, rows] = pairs[:, far]
            shared = incidence[far].astype(np.int32) @ incidence[own].T.astype(np.int32)
            compat[part, rows, :width] = shared == 0
            compat[part, rows, width:width + CARDS] = incidence[far]
            compat[part, rows, width + CARDS] = 1.0
            gather[part, rows, :CARDS] = incidence[far]
            gather[part, rows, CARDS] = 1.0
            spread[part, :CARDS, rows] = -incidence[far].T.astype(np.float32)
            spread[part, CARDS, rows] = 1.0
    near = np.zeros((parts, LANES, padded), np.float32)
    first = width - (padded - LANES)
    near[:, first:first + CARDS + 1] = spread[:, :CARDS + 1, :padded]
    exact = ml_dtypes.bfloat16
    return (cards, compat.astype(exact), gather.astype(exact), spread.astype(exact), near.astype(exact))


def split_two(value):
    high = value.astype(BF16)
    return high, (value - high.astype(F32)).astype(BF16)


def exact_right(value, matrix):
    rows = value.shape[0]
    first = value.astype(BF16)
    rest = value - first.astype(F32)
    second = rest.astype(BF16)
    third = (rest - second.astype(F32)).astype(BF16)
    total = jnp.dot(jnp.concatenate([first, second, third], axis=0), matrix, preferred_element_type=F32)
    return total[:rows] + total[rows:2 * rows] + total[2 * rows:]


def full_dot(left, right):
    return jnp.dot(left, right, precision=HIGH, preferred_element_type=F32)


def alive_rows(card_rows, turn_cards):
    one, two = card_rows[0:1], card_rows[1:2]
    held = one < 0
    for place in range(4):
        card = turn_cards[place]
        held = held | (one == card) | (two == card)
    return jnp.where(held, 0.0, 1.0).astype(F32)


def lane_sums(value):
    total = jnp.sum(value, axis=0, keepdims=True)
    parts = [total[:, at:at + LANES] for at in range(0, total.shape[1], LANES)]
    return functools.reduce(jnp.add, parts)


def steps_from(norms, count):
    totals = jnp.sum(norms, axis=1, keepdims=True)
    weight = jnp.sqrt((totals[1:2] / count + EPSILON) / (totals[0:1] / count + EPSILON))
    return STEP_SCALE / weight, STEP_SCALE * weight


def fetch_steps(norms_ref, count, step_scratch):
    primal, dual = steps_from(norms_ref[...], count)
    step_scratch[0:1, :] = jnp.broadcast_to(primal, (1, LANES))
    step_scratch[1:2, :] = jnp.broadcast_to(dual, (1, LANES))


def river_steps(children_ref, parents_ref):
    sequences = children_ref.shape[1]
    step = (children_ref[...] - parents_ref[:, :sequences]).astype(F32)
    return step, parents_ref[:, sequences:].astype(F32)


def stats_kernel(slots, group, river_axis, loads_ref, cards_now_ref, card_ref, rank_ref, x_ref, v_ref, y_ref, u_ref,
                 xt_ref, vt_ref, yt_ref, ut_ref, children_ref, parents_ref,
                 sums_ref, pack_ref, norms_ref, live_scratch, plan_scratch):
    at = pl.program_id(0)
    padded = live_scratch.shape[2]
    prices = v_ref.shape[1]
    river_here = lax.axis_index(river_axis)

    @pl.when(at == 0)
    def _():
        turn = alive_rows(card_ref[0, :, :padded], cards_now_ref)
        slot = lax.broadcasted_iota(jnp.int32, (slots, padded), 0)
        rank = rank_ref[...]
        live = jnp.where((rank >= 0) & (slot < loads_ref[river_here]) & (turn > 0), 1.0, 0.0)
        for board in range(slots):
            live_scratch[board] = live[board:board + 1]
        sums_ref[...] = jnp.zeros_like(sums_ref)
        plan_scratch[...] = jnp.zeros_like(plan_scratch)
        pack_ref[...] = jnp.zeros_like(pack_ref)
        norms_ref[...] = jnp.zeros_like(norms_ref)
        first = jnp.where(river_here == 0, 1.0, 0.0)
        base = 0
        for rows, row in ((xt_ref, 0), (vt_ref, 0), (yt_ref, 1), (ut_ref, 1)):
            value = jnp.where(turn > 0, rows[...], 0.0)
            pack_ref[base:base + value.shape[0]] = value
            base += round_up(value.shape[0], 8)
            norms_ref[row:row + 1] += first * lane_sums(value * value)

    nx = jnp.zeros((1, LANES), F32)
    ny = jnp.zeros((1, LANES), F32)
    for inner in range(group):
        live = live_scratch[at * group + inner] > 0
        x = jnp.where(live, x_ref[inner], 0.0)
        v = jnp.where(live, v_ref[inner], 0.0)
        y = jnp.where(live, y_ref[inner], 0.0)
        u = jnp.where(live, u_ref[inner], 0.0)
        nx = nx + lane_sums(x * x) + lane_sums(v * v)
        ny = ny + lane_sums(y * y) + lane_sums(u * u)
        sums_ref[0:prices] += u
        sums_ref[prices:2 * prices] += v
        plan_scratch[...] += y
    norms_ref[0:1] += nx
    norms_ref[1:2] += ny

    @pl.when(at == pl.num_programs(0) - 1)
    def _():
        step, _ = river_steps(children_ref, parents_ref)
        sums_ref[2 * prices:3 * prices] = full_dot(step, plan_scratch[...])


def rank_kernel(slots, group, river_axis, loads_ref, cards_now_ref, card_ref, own_ref, far_ref, live_ref, row_ref, col_ref):
    padded = row_ref.shape[2]
    rank = jnp.concatenate([own_ref[...], far_ref[...]], axis=1)
    turn = alive_rows(card_ref[0], cards_now_ref)
    slot = lax.broadcasted_iota(jnp.int32, rank.shape, 0)
    live = jnp.where((rank >= 0) & (slot < loads_ref[lax.axis_index(river_axis)]) & (turn > 0), 1.0, 0.0)
    safe = jnp.where(live > 0, rank, 0)
    code = (128 + (safe & 127)).astype(F32)
    high = safe >> 7
    for bit in range(6):
        code = code * jnp.where((high >> bit) & 1 == 1, float(2.0 ** (1 << bit)), 1.0)
    lane = lax.broadcasted_iota(jnp.int32, rank.shape, 1)
    width = H // (2 * padded // padded)
    own_code = jnp.where(lane[:, :padded] < width, code[:, :padded], 0.0)
    for board in range(slots):
        live_ref[board] = live[board:board + 1]
        row_ref[board] = own_code[board:board + 1].astype(BF16)
    depth = round_up(slots, 8)
    if depth > slots:
        code = jnp.concatenate([code, jnp.zeros((depth - slots, code.shape[1]), F32)], axis=0)
    turned = code.T
    for place in range(slots // group):
        col_ref[place] = turned[:, place * group:(place + 1) * group]


def set_operators(transposed, pot_ref, fold_ref, children_ref, parents_ref, main_scratch, fold_scratch, back_scratch):
    pot = pot_ref[...] / H
    fold = fold_ref[...] / H
    if transposed:
        pot, fold = -pot.T, fold.T
    step, _ = river_steps(children_ref, parents_ref)
    sequences = pot.shape[0]
    infosets = step.shape[0]
    pot_high, pot_low = split_two(pot)
    fold_high, fold_low = split_two(fold)
    main_scratch[:sequences] = jnp.concatenate([pot_high, pot_high, fold_high, fold_high], axis=1)
    main_scratch[sequences:2 * sequences] = jnp.concatenate([pot_low, pot_low, fold_low, fold_low], axis=1)
    exact = step.astype(BF16)
    main_scratch[2 * sequences:2 * sequences + infosets] = jnp.concatenate(
        [jnp.zeros((infosets, 2 * sequences), BF16), exact, exact], axis=1)
    fold_scratch[:sequences] = jnp.concatenate([fold_high, fold_high], axis=1)
    fold_scratch[sequences:] = jnp.concatenate([fold_low, fold_low], axis=1)
    turned = step.T
    if transposed:
        turned = -turned
    turned = turned.astype(BF16)
    back_scratch[...] = jnp.concatenate([turned, turned], axis=1)


def payoffs(own_plans, far_plans, prices, col_ref, row_ref, compat_ref, near_ref, main_scratch, fold_scratch, back_scratch):
    sequences, padded = own_plans[0].shape
    tiles = padded // TILE
    results = []
    cards = []
    for inner in range(len(own_plans)):
        own_high, own_low = split_two(own_plans[inner])
        far_high, far_low = split_two(far_plans[inner])
        left = (jnp.concatenate([own_high, own_low], axis=0), jnp.concatenate([far_high, far_low], axis=0))
        row = row_ref[inner]
        sums = [None] * tiles
        for place in range(2 * tiles):
            rows = slice(place * TILE, (place + 1) * TILE)
            column = jnp.broadcast_to(col_ref[0, rows, inner:inner + 1], (TILE, LANES)).astype(BF16)
            column = jnp.concatenate([column, column], axis=1)
            piece = left[place // tiles][:, (place % tiles) * TILE:(place % tiles + 1) * TILE]
            for across in range(tiles):
                lanes = slice(across * TILE, (across + 1) * TILE)
                bound = compat_ref[0, rows, lanes]
                signs = jnp.minimum(jnp.maximum(column - row[:, lanes], -bound), bound)
                part = jnp.dot(piece, signs, preferred_element_type=F32)
                sums[across] = part if sums[across] is None else sums[across] + part
        mixed = jnp.concatenate(sums, axis=1)
        mixed = mixed[:sequences] + mixed[sequences:]
        mixed_high, mixed_low = split_two(mixed)
        stacked = jnp.concatenate([mixed_high, mixed_low, own_high, own_low], axis=0)
        main = jnp.dot(main_scratch[...], stacked, preferred_element_type=F32)
        price_high, price_low = split_two(prices[inner])
        back = jnp.dot(back_scratch[...], jnp.concatenate([price_high, price_low], axis=0), preferred_element_type=F32)
        tail = jnp.concatenate([mixed_high[:, padded - LANES:], mixed_low[:, padded - LANES:]], axis=0)
        folded = jnp.dot(fold_scratch[...], tail, preferred_element_type=F32)
        cards.extend(split_two(folded[:sequences] + folded[sequences:]))
        results.append((main[:sequences] + main[sequences:2 * sequences] + back, main[2 * sequences:]))
    nearby = jnp.dot(jnp.concatenate(cards, axis=0), near_ref[0], preferred_element_type=F32)
    done = []
    for inner, (gradient, flow) in enumerate(results):
        base = 2 * inner * sequences
        close = nearby[base:base + sequences] + nearby[base + sequences:base + 2 * sequences]
        done.append((gradient + close, flow))
    return done


def mover_gradient_kernel(group, hand_ref, y_ref, far_ref, u_ref, live_ref, col_ref, row_ref, compat_ref, near_ref,
                          yt_ref, pot_ref, fold_ref, children_ref, parents_ref,
                          grad_ref, flow_ref, main_scratch, fold_scratch, back_scratch, link_scratch):
    padded = grad_ref.shape[2]

    @pl.when(pl.program_id(0) == 0)
    def _():
        set_operators(False, pot_ref, fold_ref, children_ref, parents_ref, main_scratch, fold_scratch, back_scratch)
        _, link = river_steps(children_ref, parents_ref)
        link_scratch[...] = full_dot(link, yt_ref[...])

    own_plans, far_plans, prices, lives = [], [], [], []
    for inner in range(group):
        live = live_ref[inner]
        lives.append(live[:, :padded])
        own_plans.append(jnp.where(live[:, :padded] > 0, y_ref[inner], 0.0))
        far_plans.append(jnp.where(live[:, padded:] > 0, far_ref[inner], 0.0))
        prices.append(jnp.where(live[:, :padded] > 0, u_ref[inner], 0.0))
    done = payoffs(own_plans, far_plans, prices, col_ref, row_ref, compat_ref, near_ref, main_scratch, fold_scratch, back_scratch)
    for inner, (gradient, flow) in enumerate(done):
        grad_ref[inner] = gradient
        flow_ref[inner] = lives[inner] * (flow - link_scratch[...])


def mover_step_kernel(group, count, last, norms_ref, x_ref, v_ref, grad_ref, flow_ref, live_ref, children_ref, parents_ref,
                      new_x_ref, new_v_ref, bar_ref, *rest):
    at = pl.program_id(0)
    padded = bar_ref.shape[2]
    step_scratch = rest[-1]
    if not last:
        sum_ref, out_norms_ref, plan_scratch, _ = rest

    @pl.when(at == 0)
    def _():
        fetch_steps(norms_ref, count, step_scratch)
        if not last:
            plan_scratch[...] = jnp.zeros_like(plan_scratch)
            out_norms_ref[...] = jnp.zeros_like(out_norms_ref)

    primal = step_scratch[0:1, 0:1]
    for inner in range(group):
        live = live_ref[inner][:, :padded]
        x = jnp.where(live > 0, x_ref[inner], 0.0)
        v = jnp.where(live > 0, v_ref[inner], 0.0)
        new_x = live * jnp.maximum(x - primal * grad_ref[inner], 0.0)
        new_v = v + primal * flow_ref[inner]
        bar = 2.0 * new_x - x
        new_x_ref[inner] = new_x
        new_v_ref[inner] = new_v
        bar_ref[inner] = bar
        if not last:
            plan_scratch[...] += bar
            out_norms_ref[0:1] += lane_sums(new_x * new_x) + lane_sums(new_v * new_v)

    if not last:
        @pl.when(at == pl.num_programs(0) - 1)
        def _():
            step, _ = river_steps(children_ref, parents_ref)
            sum_ref[...] = full_dot(step, plan_scratch[...])


def rival_step_kernel(group, count, last, hand_ref, norms_ref, bar_ref, far_ref, y_ref, u_ref, new_v_ref, flow_ref, live_ref,
                      col_ref, row_ref, compat_ref, near_ref, bart_ref, pot_ref, fold_ref, children_ref, parents_ref, *rest):
    at = pl.program_id(0)
    if last:
        new_y_ref, new_u_ref, main_scratch, fold_scratch, back_scratch, link_scratch, step_scratch = rest
    else:
        (part_ref, new_y_ref, new_u_ref, sum_ref, out_norms_ref, main_scratch, fold_scratch, back_scratch, link_scratch,
         step_scratch, plan_scratch) = rest
    padded = live_ref.shape[2] // 2

    @pl.when(at == 0)
    def _():
        fetch_steps(norms_ref, count, step_scratch)
        set_operators(True, pot_ref, fold_ref, children_ref, parents_ref, main_scratch, fold_scratch, back_scratch)
        _, link = river_steps(children_ref, parents_ref)
        link_scratch[...] = full_dot(link, bart_ref[...])
        if not last:
            plan_scratch[...] = jnp.zeros_like(plan_scratch)
            out_norms_ref[...] = part_ref[...]

    primal = step_scratch[0:1, 0:1]
    dual = step_scratch[1:2, 0:1]
    own_plans, far_plans, prices = [], [], []
    for inner in range(group):
        own_plans.append(bar_ref[inner])
        far_plans.append(far_ref[inner])
        prices.append(new_v_ref[inner] + primal * flow_ref[inner])
    done = payoffs(own_plans, far_plans, prices, col_ref, row_ref, compat_ref, near_ref, main_scratch, fold_scratch, back_scratch)
    for inner, (gradient, flow) in enumerate(done):
        live = live_ref[inner][:, :padded]
        y = jnp.where(live > 0, y_ref[inner], 0.0)
        u = jnp.where(live > 0, u_ref[inner], 0.0)
        new_y = live * jnp.maximum(y + dual * gradient, 0.0)
        new_u = u + dual * (live * (flow - link_scratch[...]))
        new_y_ref[inner] = new_y
        new_u_ref[inner] = new_u
        if not last:
            plan_scratch[...] += new_y
            out_norms_ref[1:2] += lane_sums(new_y * new_y) + lane_sums(new_u * new_u)

    if not last:
        @pl.when(at == pl.num_programs(0) - 1)
        def _():
            step, _ = river_steps(children_ref, parents_ref)
            sum_ref[...] = full_dot(step, plan_scratch[...])


def turn_step_kernel(count, first, names, hand_ref, cards_now_ref, card_ref, gather_ref, spread_ref, norms_ref, *rest):
    if first:
        own_ref, far_ref, sums_ref, sums_far_ref = rest[:4]
        rest = rest[4:]
    else:
        pack_ref, kept_ref, old_bar_ref, old_norms_ref, sums_ref, sums_far_ref = rest[:6]
        rest = rest[6:]
    turn_fold_ref, turn_children_ref, turn_parents_ref, children_ref, parents_ref = rest[:5]
    rest = rest[5:]
    primal, dual = steps_from(norms_ref[...], count)
    turn = alive_rows(card_ref[0], cards_now_ref)
    _, link = river_steps(children_ref, parents_ref)
    link_turned = link.T
    parents = turn_parents_ref[...].astype(F32)
    turn_step = turn_children_ref[...].astype(F32) - parents
    turn_root = 1.0 - jnp.sum(parents, axis=1, keepdims=True)
    step_turned = turn_step.T
    fold = turn_fold_ref[...]
    meetings = (CARDS - 6) * turn
    sequences = fold.shape[0]
    points = turn_step.shape[0]
    slab = round_up(points, 8)
    starts = (0, sequences, sequences + slab, 2 * sequences + slab)
    infosets = link.shape[0]
    sums = jnp.concatenate([sums_ref[...], sums_far_ref[...]], axis=1)
    if first:
        pack = jnp.concatenate([own_ref[...], far_ref[...]], axis=1)
        price_sum = sums[:infosets]
        kept = sums[infosets:2 * infosets]
        plan_sum = sums[2 * infosets:]
    else:
        pack = pack_ref[...]
        _, old_dual = steps_from(old_norms_ref[...], count)
        price_sum = kept_ref[:infosets] + old_dual * (
            sums[:infosets] - meetings * full_dot(link, old_bar_ref[...]))
        kept = kept_ref[infosets:]
        plan_sum = sums[infosets:]
    x = pack[starts[0]:starts[0] + sequences]
    v = pack[starts[1]:starts[1] + points]
    y = pack[starts[2]:starts[2] + sequences]
    u = pack[starts[3]:starts[3] + points]

    def mix(plan):
        return turn * (exact_right(exact_right(plan, gather_ref[0]), spread_ref[0]) + plan)

    grad = full_dot(fold, mix(y)) / H + turn * (full_dot(step_turned, u) - full_dot(link_turned, price_sum))
    new_x = turn * jnp.maximum(x - primal * grad, 0.0)
    new_v = v + primal * (turn * (full_dot(turn_step, y) - turn_root))
    bar = 2.0 * new_x - x
    price_bar = 2.0 * new_v - v
    drift = primal * (plan_sum - meetings * full_dot(link, y))
    rise = full_dot(fold.T, mix(bar)) / H - turn * (
        full_dot(step_turned, price_bar) - full_dot(link_turned, kept + 2.0 * drift))
    new_y = turn * jnp.maximum(y + dual * rise, 0.0)
    new_u = u + dual * (turn * (full_dot(turn_step, bar) - turn_root))
    if first:
        out_pack_ref, out_kept_ref, bar_ref, out_norms_ref = rest
        out_pack_ref[...] = jnp.zeros_like(out_pack_ref)
        for start, value in zip(starts, (new_x, new_v, new_y, new_u)):
            out_pack_ref[start:start + value.shape[0]] = value
        out_kept_ref[:infosets] = price_sum
        out_kept_ref[infosets:] = kept + drift
        bar_ref[...] = bar
        river_name, hand_name = names
        flag = jnp.where((lax.axis_index(river_name) == 0) & (hand_ref[0] == 0), 1.0, 0.0)
        out_norms_ref[...] = jnp.zeros_like(out_norms_ref)
        out_norms_ref[0:1] = flag * (lane_sums(new_x * new_x) + lane_sums(new_v * new_v))
        out_norms_ref[1:2] = flag * (lane_sums(new_y * new_y) + lane_sums(new_u * new_u))
    else:
        bar_ref = rest[0]
        bar_ref[...] = bar
        for out_ref, value in zip(rest[1:], (new_x, new_v, new_y, new_u)):
            out_ref[...] = value[:, :out_ref.shape[1]]


def whole(shape):
    return pl.BlockSpec(shape, lambda *at: (0,) * len(shape))


def smem():
    return pl.BlockSpec(memory_space=pltpu.SMEM)


def local(hand_rank, loads, turn_cards, turn_children, turn_parents, river_children, river_parents, showdown_pot, river_fold,
          turn_fold, mover_turn, mover_river, mover_turn_price, mover_river_price, rival_turn, rival_river,
          rival_turn_price, rival_river_price):
    slots, sequences, width = mover_river.shape
    infosets = mover_river_price.shape[1]
    turn_sequences = mover_turn.shape[0]
    points = mover_turn_price.shape[0]
    river_count = lax.axis_size("river")
    padded = round_up(width + CARDS + 1, TILE)
    count = float((turn_sequences + points) * H + river_count * slots * (sequences + infosets) * H)
    group = next(size for size in (3, 2, 1) if slots % size == 0)
    grid = (slots // group,)
    cards, compat, gather, spread, near = (jnp.asarray(table) for table in halves(width, padded))
    hand = lax.axis_index("hand").astype(jnp.int32).reshape(1)
    pack_rows = 2 * (turn_sequences + round_up(points, 8))
    params = pltpu.CompilerParams(vmem_limit_bytes=VMEM_BYTES)

    def shape(*dims, dtype=F32):
        return jax.ShapeDtypeStruct(dims, dtype)

    def swap(value):
        return lax.ppermute(value, "hand", [(0, 1), (1, 0)])

    def river_total(value):
        if river_count & (river_count - 1):
            return lax.psum(value, "river")
        hop = 1
        while hop < river_count:
            value = value + lax.ppermute(value, "river", [(at, at ^ hop) for at in range(river_count)])
            hop *= 2
        return value

    def boards(rows):
        return pl.BlockSpec((group, rows, padded), lambda at, *_: (at, 0, 0))

    live_block = pl.BlockSpec((group, 1, 2 * padded), lambda at, *_: (at, 0, 0))
    col_block = pl.BlockSpec((1, 2 * padded, group), lambda at, *_: (at, 0, 0))
    row_block = pl.BlockSpec((group, 1, padded), lambda at, *_: (at, 0, 0))
    compat_block = pl.BlockSpec((1, 2 * padded, padded), lambda at, ref: (ref[0], 0, 0))
    near_block = pl.BlockSpec((1, LANES, padded), lambda at, ref: (ref[0], 0, 0))
    card_block = pl.BlockSpec((1, 8, 2 * padded), lambda at, ref: (ref[0], 0, 0))
    tree_blocks = [whole(river_children.shape), whole(river_parents.shape)]
    half_block = lambda rows: pl.BlockSpec((rows, padded), lambda at, *_: (0, 0))
    norm_block = whole((8, LANES))
    operator_scratch = [pltpu.VMEM((2 * sequences + infosets, 4 * sequences), BF16),
                        pltpu.VMEM((2 * sequences, 2 * sequences), BF16),
                        pltpu.VMEM((sequences, 2 * infosets), BF16),
                        pltpu.VMEM((infosets, padded), F32)]
    step_scratch = pltpu.VMEM((8, LANES), F32)
    plan_scratch = pltpu.VMEM((sequences, padded), F32)

    rank_far = swap(hand_rank)
    rival_far = swap(rival_river)

    def stats_call(*args):
        def kernel(hand_ref, *refs):
            stats_kernel(slots, group, "river", *refs)
        return pl.pallas_call(
            kernel,
            grid_spec=pltpu.PrefetchScalarGridSpec(
                num_scalar_prefetch=1, grid=grid,
                in_specs=[smem(), smem(), card_block, half_block(slots), boards(sequences), boards(infosets),
                          boards(sequences), boards(infosets), half_block(turn_sequences), half_block(points),
                          half_block(turn_sequences), half_block(points)] + tree_blocks,
                out_specs=[whole((3 * infosets, padded)), whole((pack_rows, padded)), norm_block],
                scratch_shapes=[pltpu.VMEM((slots, 1, padded), F32), plan_scratch]),
            out_shape=[shape(3 * infosets, padded), shape(pack_rows, padded), shape(8, LANES)],
            compiler_params=params, name="stats",
        )(hand, *args)

    sums, pack, norms = stats_call(
        loads, turn_cards, cards, hand_rank, mover_river, mover_river_price, rival_river, rival_river_price,
        mover_turn, mover_turn_price, rival_turn, rival_turn_price, river_children, river_parents)

    norms = norms + swap(norms)
    norms = river_total(norms)
    pack_far = swap(pack)
    sums = river_total(sums)
    sums_far = swap(sums)

    def rank_call(*args):
        def kernel(hand_ref, *refs):
            rank_kernel(slots, group, "river", *refs)
        return pl.pallas_call(
            kernel,
            grid_spec=pltpu.PrefetchScalarGridSpec(
                num_scalar_prefetch=1, grid=(1,),
                in_specs=[smem(), smem(), card_block, half_block(slots), half_block(slots)],
                out_specs=[whole((slots, 1, 2 * padded)), whole((slots, 1, padded)), whole((slots // group, 2 * padded, group))]),
            out_shape=[shape(slots, 1, 2 * padded), shape(slots, 1, padded, dtype=BF16), shape(slots // group, 2 * padded, group)],
            compiler_params=params, name="ranks",
        )(hand, *args)

    live, rows, cols = rank_call(loads, turn_cards, cards, hand_rank, rank_far)
    board_blocks = [live_block, col_block, row_block, compat_block, near_block]
    board_tables = (live, cols, rows, compat, near)
    matrix_blocks = [whole(showdown_pot.shape), whole(river_fold.shape)] + tree_blocks
    matrices = (showdown_pot, river_fold, river_children, river_parents)

    def gradient_call(y, y_far, u, y_turn):
        return pl.pallas_call(
            functools.partial(mover_gradient_kernel, group),
            grid_spec=pltpu.PrefetchScalarGridSpec(
                num_scalar_prefetch=1, grid=grid,
                in_specs=[boards(sequences), boards(sequences), boards(infosets)] + board_blocks
                + [half_block(turn_sequences)] + matrix_blocks,
                out_specs=[boards(sequences), boards(infosets)],
                scratch_shapes=operator_scratch),
            out_shape=[shape(slots, sequences, padded), shape(slots, infosets, padded)],
            compiler_params=params, name="mover_gradient",
        )(hand, y, y_far, u, *board_tables, y_turn, *matrices)

    def mover_call(last, norms, x, v, grad, flow):
        out_width = width if last else padded
        out_specs = [boards(sequences), boards(infosets), boards(sequences)]
        out_shape = [shape(slots, sequences, out_width), shape(slots, infosets, out_width), shape(slots, sequences, padded)]
        scratch = [step_scratch]
        if not last:
            out_specs += [whole((infosets, padded)), norm_block]
            out_shape += [shape(infosets, padded), shape(8, LANES)]
            scratch = [plan_scratch, step_scratch]
        return pl.pallas_call(
            functools.partial(mover_step_kernel, group, count, last),
            grid_spec=pltpu.PrefetchScalarGridSpec(
                num_scalar_prefetch=0, grid=grid,
                in_specs=[norm_block, boards(sequences), boards(infosets), boards(sequences), boards(infosets), live_block] + tree_blocks,
                out_specs=out_specs, scratch_shapes=scratch),
            out_shape=out_shape, compiler_params=params, name="mover_step",
        )(norms, x, v, grad, flow, live, river_children, river_parents)

    def rival_call(last, norms, bar, bar_far, y, u, new_v, flow, bar_turn, part):
        out_width = width if last else padded
        in_specs = [norm_block, boards(sequences), boards(sequences), boards(sequences), boards(infosets), boards(infosets),
                    boards(infosets)] + board_blocks + [half_block(turn_sequences)] + matrix_blocks
        out_specs = [boards(sequences), boards(infosets)]
        out_shape = [shape(slots, sequences, out_width), shape(slots, infosets, out_width)]
        scratch = operator_scratch + [step_scratch]
        args = (hand, norms, bar, bar_far, y, u, new_v, flow, *board_tables, bar_turn, *matrices)
        if not last:
            in_specs.append(norm_block)
            out_specs += [whole((infosets, padded)), norm_block]
            out_shape += [shape(infosets, padded), shape(8, LANES)]
            scratch = scratch + [plan_scratch]
            args = args + (part,)
        return pl.pallas_call(
            functools.partial(rival_step_kernel, group, count, last),
            grid_spec=pltpu.PrefetchScalarGridSpec(
                num_scalar_prefetch=1, grid=grid, in_specs=in_specs, out_specs=out_specs, scratch_shapes=scratch),
            out_shape=out_shape, compiler_params=params, name="rival_step",
        )(*args)

    both = 2 * padded
    turn_blocks = [smem(), card_block, pl.BlockSpec((1, both, LANES), lambda at, ref: (ref[0], 0, 0)),
                   pl.BlockSpec((1, LANES, both), lambda at, ref: (ref[0], 0, 0)), norm_block]
    turn_tables = (turn_cards, cards, gather, spread)
    turn_matrix_blocks = [whole(turn_fold.shape), whole(turn_children.shape), whole(turn_parents.shape)] + tree_blocks
    turn_matrices = (turn_fold, turn_children, turn_parents, river_children, river_parents)

    def turn_call(first, norms, data):
        if first:
            in_data = [whole((pack_rows, padded))] * 2 + [whole((3 * infosets, padded))] * 2
            out_shape = [shape(pack_rows, both), shape(2 * infosets, both), shape(turn_sequences, both), shape(8, LANES)]
        else:
            in_data = [whole((pack_rows, both)), whole((2 * infosets, both)), whole((turn_sequences, both)), norm_block] + [
                whole((2 * infosets, padded))] * 2
            out_shape = [shape(turn_sequences, both), shape(turn_sequences, width), shape(points, width),
                         shape(turn_sequences, width), shape(points, width)]
        return pl.pallas_call(
            functools.partial(turn_step_kernel, count, first, ("river", "hand")),
            grid_spec=pltpu.PrefetchScalarGridSpec(
                num_scalar_prefetch=1, grid=(1,), in_specs=turn_blocks + in_data + turn_matrix_blocks,
                out_specs=[whole(item.shape) for item in out_shape]),
            out_shape=out_shape, compiler_params=params, name="turn_step",
        )(hand, *turn_tables, norms, *data, *turn_matrices)

    y_start = turn_sequences + round_up(points, 8)
    grad, flow = gradient_call(rival_river, rival_far, rival_river_price, lax.slice_in_dim(pack, y_start, y_start + turn_sequences))
    x, v, bar, bar_sum, part = mover_call(False, norms, mover_river, mover_river_price, grad, flow)
    bar_far = swap(bar)
    pack, kept, bar_turn, turn_norms = turn_call(True, norms, (pack, pack_far, sums, sums_far))
    y, u, plan_sum, part = rival_call(False, norms, bar, bar_far, rival_river, rival_river_price, v, flow, bar_turn,
                                      part + turn_norms)
    y_far = swap(y)
    next_norms = river_total(part + swap(part))
    sums = river_total(jnp.concatenate([bar_sum, plan_sum], axis=0))
    sums_far = swap(sums)
    grad, flow = gradient_call(y, y_far, u, lax.slice_in_dim(pack, y_start, y_start + turn_sequences))
    next_x, next_v, bar = mover_call(True, next_norms, x, v, grad, flow)
    bar_far = swap(bar)
    bar_turn, next_xt, next_vt, next_yt, next_ut = turn_call(
        False, next_norms, (pack, kept, bar_turn, norms, sums, sums_far))
    next_y, next_u = rival_call(True, next_norms, bar, bar_far, y, u, next_v, flow, bar_turn, None)
    return (next_xt, next_x, next_vt, next_v, next_yt, next_y, next_ut, next_u)


def solution(mesh):
    river = P(("groups", "river"), None, "hand")
    turn = P("groups", "hand")
    placed = (P(("groups", "river"), "hand"), P("groups"), P("groups"), P(), P(), P(), P(), P(), P(), P(),
              turn, river, turn, river, turn, river, turn, river)
    return jax.shard_map(local, mesh=mesh, in_specs=placed,
                         out_specs=(turn, river, turn, river, turn, river, turn, river), check_vma=False)
```

```python
import functools

import jax
import jax.numpy as jnp
import ml_dtypes
import numpy as np
from jax import lax
from jax.experimental import pallas as pl
from jax.experimental.pallas import tpu as pltpu
from jax.sharding import PartitionSpec as P

CARDS = 52
H = 1326
ITERS = 2
STEP_SCALE = 0.25
EPSILON = 1e-06
HIGH = lax.Precision.HIGHEST
LANES = 128
TILE = 256
VMEM_BYTES = 20 * 2**20
CHUNKS = 4
F32 = jnp.float32
BF16 = jnp.bfloat16


def round_up(value, unit):
    return -(-value // unit) * unit


def halves(width, padded):
    pairs = np.stack(np.triu_indices(CARDS, 1)).astype(np.int32)
    deck = np.arange(CARDS)
    incidence = (pairs[0][:, None] == deck) | (pairs[1][:, None] == deck)
    parts = pairs.shape[1] // width
    cards = np.full((parts, 8, 2 * padded), -1, np.int32)
    compat = np.zeros((parts, 2 * padded, padded), np.float32)
    gather = np.zeros((parts, 2 * padded, LANES), np.float32)
    spread = np.zeros((parts, LANES, 2 * padded), np.float32)
    for part in range(parts):
        own = slice(part * width, (part + 1) * width)
        for place, half in enumerate((part, 1 - part)):
            far = slice(half * width, (half + 1) * width)
            rows = slice(place * padded, place * padded + width)
            cards[part, :2, rows] = pairs[:, far]
            shared = incidence[far].astype(np.int32) @ incidence[own].T.astype(np.int32)
            compat[part, rows, :width] = shared == 0
            compat[part, rows, width:width + CARDS] = incidence[far]
            compat[part, rows, width + CARDS] = 1.0
            gather[part, rows, :CARDS] = incidence[far]
            gather[part, rows, CARDS] = 1.0
            spread[part, :CARDS, rows] = -incidence[far].T.astype(np.float32)
            spread[part, CARDS, rows] = 1.0
    near = np.zeros((parts, LANES, padded), np.float32)
    first = width - (padded - LANES)
    near[:, first:first + CARDS + 1] = spread[:, :CARDS + 1, :padded]
    exact = ml_dtypes.bfloat16
    return (cards, compat.astype(exact), gather.astype(exact), spread.astype(exact), near.astype(exact))


def split_two(value):
    high = value.astype(BF16)
    return high, (value - high.astype(F32)).astype(BF16)


def exact_right(value, matrix):
    rows = value.shape[0]
    first = value.astype(BF16)
    rest = value - first.astype(F32)
    second = rest.astype(BF16)
    third = (rest - second.astype(F32)).astype(BF16)
    total = jnp.dot(jnp.concatenate([first, second, third], axis=0), matrix, preferred_element_type=F32)
    return total[:rows] + total[rows:2 * rows] + total[2 * rows:]


def full_dot(left, right):
    return jnp.dot(left, right, precision=HIGH, preferred_element_type=F32)


def alive_rows(card_rows, turn_cards):
    one, two = card_rows[0:1], card_rows[1:2]
    held = one < 0
    for place in range(4):
        card = turn_cards[place]
        held = held | (one == card) | (two == card)
    return jnp.where(held, 0.0, 1.0).astype(F32)


def row_sums(value):
    return jnp.sum(value, axis=0, keepdims=True)


def steps_from(own_norms, far_norms, count):
    totals = jnp.sum(own_norms + far_norms, axis=1, keepdims=True)
    weight = jnp.sqrt((totals[1:2] / count + EPSILON) / (totals[0:1] / count + EPSILON))
    return STEP_SCALE / weight, STEP_SCALE * weight


def fetch_steps(own_ref, far_ref, count, step_scratch):
    primal, dual = steps_from(own_ref[...], far_ref[...], count)
    step_scratch[0:1, :] = jnp.broadcast_to(primal, (1, LANES))
    step_scratch[1:2, :] = jnp.broadcast_to(dual, (1, LANES))


def river_steps(children_ref, parents_ref):
    sequences = children_ref.shape[1]
    step = (children_ref[...] - parents_ref[:, :sequences]).astype(F32)
    return step, parents_ref[:, sequences:].astype(F32)


def stats_kernel(slots, group, river_axis, loads_ref, cards_now_ref, card_ref, rank_ref, x_ref, v_ref, y_ref, u_ref,
                 xt_ref, vt_ref, yt_ref, ut_ref, children_ref, parents_ref,
                 sums_ref, pack_ref, live_scratch, plan_scratch):
    at = pl.program_id(0)
    padded = live_scratch.shape[2]
    prices = v_ref.shape[1]
    nx, ny = 3 * prices, 3 * prices + 1
    river_here = lax.axis_index(river_axis)

    @pl.when(at == 0)
    def _():
        turn = alive_rows(card_ref[0, :, :padded], cards_now_ref)
        slot = lax.broadcasted_iota(jnp.int32, (slots, padded), 0)
        rank = rank_ref[...]
        live = jnp.where((rank >= 0) & (slot < loads_ref[river_here]) & (turn > 0), 1.0, 0.0)
        for board in range(slots):
            live_scratch[board] = live[board:board + 1]
        sums_ref[...] = jnp.zeros_like(sums_ref)
        plan_scratch[...] = jnp.zeros_like(plan_scratch)
        pack_ref[...] = jnp.zeros_like(pack_ref)
        first = jnp.where(river_here == 0, 1.0, 0.0)
        base = 0
        for rows, row in ((xt_ref, nx), (yt_ref, ny), (vt_ref, nx), (ut_ref, ny)):
            value = jnp.where(turn > 0, rows[...], 0.0)
            pack_ref[base:base + value.shape[0]] = value
            base += round_up(value.shape[0], 8)
            sums_ref[row:row + 1] += first * row_sums(value * value)

    mover = jnp.zeros((1, padded), F32)
    rival = jnp.zeros((1, padded), F32)
    for inner in range(group):
        live = live_scratch[at * group + inner] > 0
        x = jnp.where(live, x_ref[inner], 0.0)
        v = jnp.where(live, v_ref[inner], 0.0)
        y = jnp.where(live, y_ref[inner], 0.0)
        u = jnp.where(live, u_ref[inner], 0.0)
        mover = mover + row_sums(x * x) + row_sums(v * v)
        rival = rival + row_sums(y * y) + row_sums(u * u)
        sums_ref[0:prices] += u
        sums_ref[prices:2 * prices] += v
        plan_scratch[...] += y
    sums_ref[nx:nx + 1] += mover
    sums_ref[ny:ny + 1] += rival

    @pl.when(at == pl.num_programs(0) - 1)
    def _():
        step, _ = river_steps(children_ref, parents_ref)
        sums_ref[2 * prices:3 * prices] = full_dot(step, plan_scratch[...])


def rank_kernel(slots, group, river_axis, loads_ref, cards_now_ref, card_ref, own_ref, far_ref, live_ref, row_ref, col_ref):
    padded = row_ref.shape[2]
    rank = jnp.concatenate([own_ref[...], far_ref[...]], axis=1)
    turn = alive_rows(card_ref[0], cards_now_ref)
    slot = lax.broadcasted_iota(jnp.int32, rank.shape, 0)
    live = jnp.where((rank >= 0) & (slot < loads_ref[lax.axis_index(river_axis)]) & (turn > 0), 1.0, 0.0)
    safe = jnp.where(live > 0, rank, 0)
    code = (128 + (safe & 127)).astype(F32)
    high = safe >> 7
    for bit in range(6):
        code = code * jnp.where((high >> bit) & 1 == 1, float(2.0 ** (1 << bit)), 1.0)
    lane = lax.broadcasted_iota(jnp.int32, rank.shape, 1)
    width = H // 2
    own_code = jnp.where(lane[:, :padded] < width, code[:, :padded], 0.0)
    for board in range(slots):
        live_ref[board] = live[board:board + 1]
        row_ref[board] = own_code[board:board + 1].astype(BF16)
    depth = round_up(slots, 8)
    if depth > slots:
        code = jnp.concatenate([code, jnp.zeros((depth - slots, code.shape[1]), F32)], axis=0)
    turned = code.T
    for place in range(slots // group):
        col_ref[place] = turned[:, place * group:(place + 1) * group]


def set_operators(transposed, pot_ref, fold_ref, children_ref, parents_ref, main_scratch, fold_scratch, back_scratch):
    pot = pot_ref[...] / H
    fold = fold_ref[...] / H
    if transposed:
        pot, fold = -pot.T, fold.T
    step, _ = river_steps(children_ref, parents_ref)
    sequences = pot.shape[0]
    infosets = step.shape[0]
    pot_high, pot_low = split_two(pot)
    fold_high, fold_low = split_two(fold)
    main_scratch[:sequences] = jnp.concatenate([pot_high, pot_high, fold_high, fold_high], axis=1)
    main_scratch[sequences:2 * sequences] = jnp.concatenate([pot_low, pot_low, fold_low, fold_low], axis=1)
    exact = step.astype(BF16)
    main_scratch[2 * sequences:2 * sequences + infosets] = jnp.concatenate(
        [jnp.zeros((infosets, 2 * sequences), BF16), exact, exact], axis=1)
    fold_scratch[:sequences] = jnp.concatenate([fold_high, fold_high], axis=1)
    fold_scratch[sequences:] = jnp.concatenate([fold_low, fold_low], axis=1)
    turned = step.T
    if transposed:
        turned = -turned
    turned = turned.astype(BF16)
    back_scratch[...] = jnp.concatenate([turned, turned], axis=1)


def payoffs(own_plans, far_plans, prices, col_ref, row_ref, compat_ref, near_ref, main_scratch, fold_scratch, back_scratch):
    sequences, padded = own_plans[0].shape
    tiles = padded // TILE
    results = []
    cards = []
    for inner in range(len(own_plans)):
        own_high, own_low = split_two(own_plans[inner])
        far_high, far_low = split_two(far_plans[inner])
        left = (jnp.concatenate([own_high, own_low], axis=0), jnp.concatenate([far_high, far_low], axis=0))
        row = row_ref[inner]
        sums = [None] * tiles
        for place in range(2 * tiles):
            rows = slice(place * TILE, (place + 1) * TILE)
            column = jnp.broadcast_to(col_ref[0, rows, inner:inner + 1], (TILE, LANES)).astype(BF16)
            column = jnp.concatenate([column, column], axis=1)
            piece = left[place // tiles][:, (place % tiles) * TILE:(place % tiles + 1) * TILE]
            for across in range(tiles):
                lanes = slice(across * TILE, (across + 1) * TILE)
                bound = compat_ref[rows, lanes]
                signs = jnp.minimum(jnp.maximum(column - row[:, lanes], -bound), bound)
                part = jnp.dot(piece, signs, preferred_element_type=F32)
                sums[across] = part if sums[across] is None else sums[across] + part
        mixed = jnp.concatenate(sums, axis=1)
        mixed = mixed[:sequences] + mixed[sequences:]
        mixed_high, mixed_low = split_two(mixed)
        stacked = jnp.concatenate([mixed_high, mixed_low, own_high, own_low], axis=0)
        main = jnp.dot(main_scratch[...], stacked, preferred_element_type=F32)
        price_high, price_low = split_two(prices[inner])
        back = jnp.dot(back_scratch[...], jnp.concatenate([price_high, price_low], axis=0), preferred_element_type=F32)
        tail = jnp.concatenate([mixed_high[:, padded - LANES:], mixed_low[:, padded - LANES:]], axis=0)
        folded = jnp.dot(fold_scratch[...], tail, preferred_element_type=F32)
        cards.extend(split_two(folded[:sequences] + folded[sequences:]))
        results.append((main[:sequences] + main[sequences:2 * sequences] + back, main[2 * sequences:]))
    nearby = jnp.dot(jnp.concatenate(cards, axis=0), near_ref[0], preferred_element_type=F32)
    done = []
    for inner, (gradient, flow) in enumerate(results):
        base = 2 * inner * sequences
        close = nearby[base:base + sequences] + nearby[base + sequences:base + 2 * sequences]
        done.append((gradient + close, flow))
    return done


def mover_gradient_kernel(group, hand_ref, y_ref, far_ref, u_ref, live_ref, col_ref, row_ref, compat_ref, near_ref,
                          yt_ref, pot_ref, fold_ref, children_ref, parents_ref,
                          grad_ref, flow_ref, main_scratch, fold_scratch, back_scratch, link_scratch):
    padded = grad_ref.shape[2]

    @pl.when(pl.program_id(0) == 0)
    def _():
        set_operators(False, pot_ref, fold_ref, children_ref, parents_ref, main_scratch, fold_scratch, back_scratch)
        _, link = river_steps(children_ref, parents_ref)
        link_scratch[...] = full_dot(link, yt_ref[...])

    own_plans, far_plans, prices, lives = [], [], [], []
    for inner in range(group):
        live = live_ref[inner]
        lives.append(live[:, :padded])
        own_plans.append(jnp.where(live[:, :padded] > 0, y_ref[inner], 0.0))
        far_plans.append(jnp.where(live[:, padded:] > 0, far_ref[inner], 0.0))
        prices.append(jnp.where(live[:, :padded] > 0, u_ref[inner], 0.0))
    done = payoffs(own_plans, far_plans, prices, col_ref, row_ref, compat_ref, near_ref, main_scratch, fold_scratch, back_scratch)
    for inner, (gradient, flow) in enumerate(done):
        grad_ref[inner] = gradient
        flow_ref[inner] = lives[inner] * (flow - link_scratch[...])


def mover_step_kernel(group, count, first_chunk, last, own_norm_ref, far_norm_ref, x_ref, v_ref, grad_ref, flow_ref,
                      live_ref, *rest):
    at = pl.program_id(0)
    step_scratch = rest[-1]
    rest = rest[:-1]
    if last:
        new_x_ref, new_v_ref, bar_ref = rest[-3:]
    else:
        new_x_ref, new_v_ref, bar_ref, total_ref = rest[-4:]
    padded = bar_ref.shape[2]

    @pl.when(at == 0)
    def _():
        fetch_steps(own_norm_ref, far_norm_ref, count, step_scratch)
        if not last:
            total_ref[...] = jnp.zeros_like(total_ref) if first_chunk else rest[0][...]

    primal = step_scratch[0:1, 0:1]
    for inner in range(group):
        live = live_ref[inner][:, :padded]
        x = jnp.where(live > 0, x_ref[inner], 0.0)
        v = jnp.where(live > 0, v_ref[inner], 0.0)
        new_x = live * jnp.maximum(x - primal * grad_ref[inner], 0.0)
        new_v = v + primal * flow_ref[inner]
        new_x_ref[inner] = new_x
        new_v_ref[inner] = new_v
        bar_ref[inner] = 2.0 * new_x - x
        if not last:
            total_ref[0:1] += row_sums(new_x * new_x) + row_sums(new_v * new_v)


def rival_step_kernel(group, count, first_chunk, last, hand_ref, own_norm_ref, far_norm_ref, bar_ref, far_ref, y_ref, u_ref,
                      new_v_ref, flow_ref, live_ref, col_ref, row_ref, compat_ref, near_ref, bart_ref, pot_ref, fold_ref,
                      children_ref, parents_ref, *rest):
    at = pl.program_id(0)
    if last:
        new_y_ref, new_u_ref, main_scratch, fold_scratch, back_scratch, link_scratch, step_scratch = rest[-7:]
    else:
        (new_y_ref, new_u_ref, total_ref, main_scratch, fold_scratch, back_scratch, link_scratch, step_scratch,
         plan_scratch) = rest[-9:]
    padded = live_ref.shape[2] // 2
    infosets = u_ref.shape[1]
    nx, ny = 2 * infosets, 2 * infosets + 1

    @pl.when(at == 0)
    def _():
        fetch_steps(own_norm_ref, far_norm_ref, count, step_scratch)
        set_operators(True, pot_ref, fold_ref, children_ref, parents_ref, main_scratch, fold_scratch, back_scratch)
        _, link = river_steps(children_ref, parents_ref)
        link_scratch[...] = full_dot(link, bart_ref[...])
        if not last:
            plan_scratch[...] = jnp.zeros_like(plan_scratch)
            if first_chunk:
                total_ref[...] = jnp.zeros_like(total_ref)
                total_ref[nx:ny + 1] = rest[0][0:2] + rest[1][0:2]
            else:
                total_ref[...] = rest[0][...]

    primal = step_scratch[0:1, 0:1]
    dual = step_scratch[1:2, 0:1]
    own_plans, far_plans, prices = [], [], []
    for inner in range(group):
        own_plans.append(bar_ref[inner])
        far_plans.append(far_ref[inner])
        prices.append(new_v_ref[inner] + primal * flow_ref[inner])
    done = payoffs(own_plans, far_plans, prices, col_ref, row_ref, compat_ref, near_ref, main_scratch, fold_scratch, back_scratch)
    for inner, (gradient, flow) in enumerate(done):
        live = live_ref[inner][:, :padded]
        y = jnp.where(live > 0, y_ref[inner], 0.0)
        u = jnp.where(live > 0, u_ref[inner], 0.0)
        flow = live * flow
        new_y = live * jnp.maximum(y + dual * gradient, 0.0)
        new_u = u + dual * (flow - live * link_scratch[...])
        new_y_ref[inner] = new_y
        new_u_ref[inner] = new_u
        if not last:
            plan_scratch[...] += new_y
            total_ref[0:infosets] += flow
            total_ref[ny:ny + 1] += row_sums(new_y * new_y) + row_sums(new_u * new_u)

    if not last:
        @pl.when(at == pl.num_programs(0) - 1)
        def _():
            step, _ = river_steps(children_ref, parents_ref)
            total_ref[infosets:2 * infosets] += full_dot(step, plan_scratch[...])


def turn_step_kernel(count, first, names, hand_ref, cards_now_ref, card_ref, gather_ref, spread_ref, *rest):
    if first:
        own_ref, far_ref, sums_ref, sums_far_ref = rest[:4]
        rest = rest[4:]
    else:
        pack_ref, kept_ref, old_bar_ref, old_steps_ref, sums_ref, sums_far_ref = rest[:6]
        rest = rest[6:]
    turn_fold_ref, turn_children_ref, turn_parents_ref, children_ref, parents_ref = rest[:5]
    rest = rest[5:]
    turn = alive_rows(card_ref[0], cards_now_ref)
    _, link = river_steps(children_ref, parents_ref)
    link_turned = link.T
    parents = turn_parents_ref[...].astype(F32)
    turn_step = turn_children_ref[...].astype(F32) - parents
    turn_root = 1.0 - jnp.sum(parents, axis=1, keepdims=True)
    step_turned = turn_step.T
    fold = turn_fold_ref[...]
    meetings = (CARDS - 6) * turn
    sequences = fold.shape[0]
    points = turn_step.shape[0]
    slab = round_up(points, 8)
    starts = (0, 2 * sequences, sequences, 2 * sequences + slab)
    infosets = link.shape[0]
    norm_row = (3 if first else 2) * infosets
    primal, dual = steps_from(sums_ref[norm_row:norm_row + 8], sums_far_ref[norm_row:norm_row + 8], count)
    sums = jnp.concatenate([sums_ref[:norm_row], sums_far_ref[:norm_row]], axis=1)
    if first:
        pack = jnp.concatenate([own_ref[...], far_ref[...]], axis=1)
        price_sum = sums[:infosets]
        kept = sums[infosets:2 * infosets]
        plan_sum = sums[2 * infosets:]
    else:
        pack = pack_ref[...]
        old_dual = old_steps_ref[1:2, 0:1]
        price_sum = kept_ref[:infosets] + old_dual * (
            sums[:infosets] - meetings * full_dot(link, old_bar_ref[...]))
        kept = kept_ref[infosets:]
        plan_sum = sums[infosets:]
    x = pack[starts[0]:starts[0] + sequences]
    v = pack[starts[1]:starts[1] + points]
    y = pack[starts[2]:starts[2] + sequences]
    u = pack[starts[3]:starts[3] + points]

    def mix(plan):
        return turn * (exact_right(exact_right(plan, gather_ref[0]), spread_ref[0]) + plan)

    grad = full_dot(fold, mix(y)) / H + turn * (full_dot(step_turned, u) - full_dot(link_turned, price_sum))
    new_x = turn * jnp.maximum(x - primal * grad, 0.0)
    new_v = v + primal * (turn * (full_dot(turn_step, y) - turn_root))
    bar = 2.0 * new_x - x
    price_bar = 2.0 * new_v - v
    drift = primal * (plan_sum - meetings * full_dot(link, y))
    rise = full_dot(fold.T, mix(bar)) / H - turn * (
        full_dot(step_turned, price_bar) - full_dot(link_turned, kept + 2.0 * drift))
    new_y = turn * jnp.maximum(y + dual * rise, 0.0)
    new_u = u + dual * (turn * (full_dot(turn_step, bar) - turn_root))
    if first:
        out_pack_ref, out_kept_ref, bar_ref, out_norms_ref, steps_ref = rest
        steps_ref[0:1] = jnp.broadcast_to(primal, (1, LANES))
        steps_ref[1:2] = jnp.broadcast_to(dual, (1, LANES))
        out_pack_ref[...] = jnp.zeros_like(out_pack_ref)
        for start, value in zip(starts, (new_x, new_v, new_y, new_u)):
            out_pack_ref[start:start + value.shape[0]] = value
        out_kept_ref[:infosets] = price_sum
        out_kept_ref[infosets:] = kept + drift
        bar_ref[...] = bar
        river_name, hand_name = names
        flag = jnp.where((lax.axis_index(river_name) == 0) & (hand_ref[0] == 0), 1.0, 0.0)
        out_norms_ref[...] = jnp.zeros_like(out_norms_ref)
        mover = row_sums(new_x * new_x) + row_sums(new_v * new_v)
        rival = row_sums(new_y * new_y) + row_sums(new_u * new_u)
        half = mover.shape[1] // 2
        out_norms_ref[0:1] = flag * (mover[:, :half] + mover[:, half:])
        out_norms_ref[1:2] = flag * (rival[:, :half] + rival[:, half:])
    else:
        bar_ref = rest[0]
        bar_ref[...] = bar
        for out_ref, value in zip(rest[1:], (new_x, new_v, new_y, new_u)):
            out_ref[...] = value[:, :out_ref.shape[1]]


def whole(shape):
    return pl.BlockSpec(shape, lambda *at: (0,) * len(shape))


def smem():
    return pl.BlockSpec(memory_space=pltpu.SMEM)


def local(hand_rank, loads, turn_cards, turn_children, turn_parents, river_children, river_parents, showdown_pot, river_fold,
          turn_fold, mover_turn, mover_river, mover_turn_price, mover_river_price, rival_turn, rival_river,
          rival_turn_price, rival_river_price):
    slots, sequences, width = mover_river.shape
    infosets = mover_river_price.shape[1]
    turn_sequences = mover_turn.shape[0]
    points = mover_turn_price.shape[0]
    river_count = lax.axis_size("river")
    padded = round_up(width + CARDS + 1, TILE)
    both = 2 * padded
    count = float((turn_sequences + points) * H + river_count * slots * (sequences + infosets) * H)
    chunks = CHUNKS if slots % CHUNKS == 0 else 1
    chunk = slots // chunks
    group = next(size for size in (3, 2, 1) if chunk % size == 0)
    grid = (chunk // group,)
    cards, compat, gather, spread, near = (jnp.asarray(table) for table in halves(width, padded))
    hand = lax.axis_index("hand").astype(jnp.int32).reshape(1)
    compat = lax.dynamic_index_in_dim(compat, hand[0], 0, keepdims=False)
    pack_rows = 2 * (turn_sequences + round_up(points, 8))
    stat_rows = 3 * infosets + 8
    total_rows = 2 * infosets + 8

    def shape(*dims, dtype=F32):
        return jax.ShapeDtypeStruct(dims, dtype)

    def swap(value):
        return lax.ppermute(value, "hand", [(0, 1), (1, 0)])

    def hop_total(value, hop, gate):
        came = lax.ppermute(value, "river", [(at, at ^ hop) for at in range(river_count)])
        if gate is not None:
            came, _ = lax.optimization_barrier((came, gate))
        return value + came

    def reduced(value, gates):
        gates = list(gates)
        if river_count & (river_count - 1):
            value = lax.psum(value, "river")
        else:
            hop = 1
            while hop < river_count:
                value = hop_total(value, hop, gates.pop(0) if gates else None)
                hop *= 2
        far = swap(value)
        if gates:
            far, _ = lax.optimization_barrier((far, gates[0]))
        return value, far

    def boards(rows, start=0):
        return pl.BlockSpec((group, rows, padded), lambda at, *_: (at + start, 0, 0))

    def tables(start):
        return [pl.BlockSpec((group, 1, both), lambda at, *_: (at + start, 0, 0)),
                pl.BlockSpec((1, both, group), lambda at, *_: (at + start, 0, 0)),
                pl.BlockSpec((group, 1, padded), lambda at, *_: (at + start, 0, 0)),
                pl.BlockSpec(memory_space=pltpu.VMEM),
                pl.BlockSpec((1, LANES, padded), lambda at, ref: (ref[0], 0, 0))]

    def norm_rows(row):
        return pl.BlockSpec((8, padded), lambda at, *_: (row // 8, 0))

    def call(kernel, name, scalars, steps, in_specs, out_specs, out_shape, scratch, args, micros, aliases=None, vmem=VMEM_BYTES):
        estimate = pl.CostEstimate(flops=int(micros * 1e9), bytes_accessed=0, transcendentals=0)
        return pl.pallas_call(
            kernel,
            grid_spec=pltpu.PrefetchScalarGridSpec(
                num_scalar_prefetch=scalars, grid=steps, in_specs=in_specs, out_specs=out_specs, scratch_shapes=scratch),
            out_shape=out_shape, compiler_params=pltpu.CompilerParams(vmem_limit_bytes=vmem),
            cost_estimate=estimate, input_output_aliases=aliases or {}, name=name,
        )(*args)

    card_block = pl.BlockSpec((1, 8, both), lambda at, ref: (ref[0], 0, 0))
    tree_blocks = [whole(river_children.shape), whole(river_parents.shape)]
    half_block = lambda rows, at_row=0: pl.BlockSpec((rows, padded), lambda at, *_: (at_row, 0))
    operator_scratch = [pltpu.VMEM((2 * sequences + infosets, 4 * sequences), BF16),
                        pltpu.VMEM((2 * sequences, 2 * sequences), BF16),
                        pltpu.VMEM((sequences, 2 * infosets), BF16),
                        pltpu.VMEM((infosets, padded), F32)]
    step_scratch = pltpu.VMEM((8, LANES), F32)
    plan_scratch = pltpu.VMEM((sequences, padded), F32)
    any_block = pl.BlockSpec(memory_space=pl.ANY)

    rank_far = swap(hand_rank)
    rival_far = swap(rival_river)

    def stats_kernel_here(hand_ref, *refs):
        stats_kernel(slots, group, "river", *refs)

    def rank_kernel_here(hand_ref, *refs):
        rank_kernel(slots, group, "river", *refs)

    sums, pack = call(
        stats_kernel_here, "stats", 1, (slots // group,),
        [smem(), smem(), card_block, half_block(slots), boards(sequences), boards(infosets),
         boards(sequences), boards(infosets), half_block(turn_sequences), half_block(points),
         half_block(turn_sequences), half_block(points)] + tree_blocks,
        [whole((stat_rows, padded)), whole((pack_rows, padded))],
        [shape(stat_rows, padded), shape(pack_rows, padded)],
        [pltpu.VMEM((slots, 1, padded), F32), plan_scratch],
        (hand, loads, turn_cards, cards, hand_rank, mover_river, mover_river_price, rival_river, rival_river_price,
         mover_turn, mover_turn_price, rival_turn, rival_turn_price, river_children, river_parents), 5,
        vmem=56 * 2**20)
    live, rows, cols = call(
        rank_kernel_here, "ranks", 1, (1,),
        [smem(), smem(), card_block, half_block(slots), half_block(slots)],
        [whole((slots, 1, both)), whole((slots, 1, padded)), whole((slots // group, both, group))],
        [shape(slots, 1, both), shape(slots, 1, padded, dtype=BF16), shape(slots // group, both, group)], [],
        (hand, loads, turn_cards, cards, hand_rank, rank_far), 2)

    matrix_blocks = [whole(showdown_pot.shape), whole(river_fold.shape)] + tree_blocks
    matrices = (showdown_pot, river_fold, river_children, river_parents)
    payoff_micros = chunk

    def place(item, index):
        if isinstance(item, list):
            return item[index], 0
        return item, index * (chunk // group)

    def gradients(y, y_far, u, pack):
        out = []
        for index in range(chunks):
            start = index * (chunk // group)
            items = [place(item, index) for item in (y, y_far, u)]
            out.append(call(
                functools.partial(mover_gradient_kernel, group), "mover_gradient", 1, grid,
                [boards(size, item[1]) for size, item in zip((sequences, sequences, infosets), items)] + tables(start)
                + [half_block(turn_sequences, 1)] + matrix_blocks,
                [boards(sequences), boards(infosets)],
                [shape(chunk, sequences, padded), shape(chunk, infosets, padded)], operator_scratch,
                (hand, *(item[0] for item in items), live, cols, rows, compat, near, pack, *matrices), payoff_micros))
        return [item[0] for item in out], [item[1] for item in out]

    def mover_steps(last, norms, row, x, v, grad, flow):
        outs = []
        for index in range(chunks):
            start = index * (chunk // group)
            items = [place(item, index) for item in (x, v, grad, flow)]
            in_specs = [norm_rows(row)] * 2 + [
                boards(size, item[1]) for size, item in zip((sequences, infosets) * 2, items)] + tables(start)[:1]
            args = (*norms, *(item[0] for item in items), live)
            aliases = {}
            if last:
                out_specs = [boards(sequences, start), boards(infosets, start), boards(sequences)]
                out_shape = [shape(slots, sequences, width), shape(slots, infosets, width), shape(chunk, sequences, padded)]
                if index:
                    aliases = {len(args): 0, len(args) + 1: 1}
                    in_specs += [any_block] * 2
                    args += tuple(outs[-1][:2])
            else:
                out_specs = [boards(sequences), boards(infosets), boards(sequences), half_block(8)]
                out_shape = [shape(chunk, sequences, padded), shape(chunk, infosets, padded),
                             shape(chunk, sequences, padded), shape(8, padded)]
                if index:
                    in_specs += [half_block(8)]
                    args += (outs[-1][3],)
            outs.append(call(functools.partial(mover_step_kernel, group, count, index == 0, last), "mover_step", 0, grid,
                             in_specs, out_specs, out_shape, [step_scratch], args, 1, aliases))
        if last:
            return outs[-1][0], outs[-1][1], [item[2] for item in outs]
        return [item[0] for item in outs], [item[1] for item in outs], [item[2] for item in outs], outs[-1][3]

    def rival_steps(last, norms, row, bar, bar_far, y, u, new_v, flow, bar_turn, parts):
        outs = []
        for index in range(chunks):
            start = index * (chunk // group)
            items = [place(item, index) for item in (bar, bar_far, y, u, new_v, flow)]
            sizes = (sequences,) * 3 + (infosets,) * 3
            in_specs = [norm_rows(row)] * 2 + [boards(size, item[1]) for size, item in zip(sizes, items)] + tables(start) + [
                half_block(turn_sequences)] + matrix_blocks
            args = (hand, *norms, *(item[0] for item in items), live, cols, rows, compat, near, bar_turn, *matrices)
            aliases = {}
            scratch = operator_scratch + [step_scratch]
            if last:
                out_specs = [boards(sequences, start), boards(infosets, start)]
                out_shape = [shape(slots, sequences, width), shape(slots, infosets, width)]
                if index:
                    aliases = {len(args): 0, len(args) + 1: 1}
                    in_specs += [any_block] * 2
                    args += tuple(outs[-1][:2])
            else:
                out_specs = [boards(sequences), boards(infosets), half_block(total_rows)]
                out_shape = [shape(chunk, sequences, padded), shape(chunk, infosets, padded), shape(total_rows, padded)]
                scratch = scratch + [plan_scratch]
                if index:
                    in_specs += [half_block(total_rows)]
                    args += (outs[-1][2],)
                else:
                    in_specs += [half_block(8)] * 2
                    args += tuple(parts)
            outs.append(call(functools.partial(rival_step_kernel, group, count, index == 0, last), "rival_step", 1, grid,
                             in_specs, out_specs, out_shape, scratch, args, payoff_micros, aliases))
        if last:
            return outs[-1]
        return [item[0] for item in outs], [item[1] for item in outs], outs[-1][2]

    turn_blocks = [smem(), card_block, pl.BlockSpec((1, both, LANES), lambda at, ref: (ref[0], 0, 0)),
                   pl.BlockSpec((1, LANES, both), lambda at, ref: (ref[0], 0, 0))]
    turn_tables = (turn_cards, cards, gather, spread)
    turn_matrices = (turn_fold, turn_children, turn_parents, river_children, river_parents)

    def turn_call(first, data):
        if first:
            out_shape = [shape(pack_rows, both), shape(2 * infosets, both), shape(turn_sequences, both), shape(8, padded),
                         shape(8, LANES)]
        else:
            out_shape = [shape(turn_sequences, both), shape(turn_sequences, width), shape(points, width),
                         shape(turn_sequences, width), shape(points, width)]
        return call(
            functools.partial(turn_step_kernel, count, first, ("river", "hand")), "turn_step", 1, (1,),
            turn_blocks + [whole(item.shape) for item in data + turn_matrices], [whole(item.shape) for item in out_shape],
            out_shape, [], (hand, *turn_tables, *data, *turn_matrices), 3)

    pack_far = swap(pack)
    grad, flow = gradients(rival_river, rival_far, rival_river_price, pack)
    norms = reduced(sums, [cols] + flow[:3])
    x, v, bar, part = mover_steps(False, norms, 3 * infosets, mover_river, mover_river_price, grad, flow)
    bar_far = [swap(item) for item in bar]
    pack, kept, bar_turn, turn_norms, turn_steps = turn_call(True, (pack, pack_far, *norms))
    y, u, total = rival_steps(False, norms, 3 * infosets, bar, bar_far, rival_river, rival_river_price, v, flow, bar_turn,
                              (part, turn_norms))
    y_far = [swap(item) for item in y]
    grad, flow = gradients(y, y_far, u, pack)
    norms = reduced(total, flow)
    next_x, next_v, bar = mover_steps(True, norms, 2 * infosets, x, v, grad, flow)
    bar_far = [swap(item) for item in bar]
    bar_turn, next_xt, next_vt, next_yt, next_ut = turn_call(False, (pack, kept, bar_turn, turn_steps, *norms))
    next_y, next_u = rival_steps(True, norms, 2 * infosets, bar, bar_far, y, u, next_v, flow, bar_turn, None)
    return (next_xt, next_x, next_vt, next_v, next_yt, next_y, next_ut, next_u)


def solution(mesh):
    river = P(("groups", "river"), None, "hand")
    turn = P("groups", "hand")
    placed = (P(("groups", "river"), "hand"), P("groups"), P("groups"), P(), P(), P(), P(), P(), P(), P(),
              turn, river, turn, river, turn, river, turn, river)
    return jax.shard_map(local, mesh=mesh, in_specs=placed,
                         out_specs=(turn, river, turn, river, turn, river, turn, river), check_vma=False)
```

```python
import functools

import jax
import jax.numpy as jnp
import ml_dtypes
import numpy as np
from jax import lax
from jax.experimental import pallas as pl
from jax.experimental.pallas import tpu as pltpu
from jax.sharding import PartitionSpec as P

CARDS = 52
H = 1326
ITERS = 2
STEP_SCALE = 0.25
EPSILON = 1e-06
LANES = 128
TILE = 256
VMEM_BYTES = 20 * 2**20
F32 = jnp.float32
BF16 = jnp.bfloat16


def round_up(value, unit):
    return -(-value // unit) * unit


def halves(width, padded):
    pairs = np.stack(np.triu_indices(CARDS, 1)).astype(np.int32)
    deck = np.arange(CARDS)
    incidence = (pairs[0][:, None] == deck) | (pairs[1][:, None] == deck)
    parts = pairs.shape[1] // width
    cards = np.full((parts, 8, 2 * padded), -1, np.int32)
    gather = np.zeros((parts, 2 * padded, LANES), np.float32)
    spread = np.zeros((parts, LANES, 2 * padded), np.float32)
    for part in range(parts):
        spread[part, np.arange(CARDS + 1), width + np.arange(CARDS + 1)] = 1.0
        for place, half in enumerate((part, 1 - part)):
            far = slice(half * width, (half + 1) * width)
            rows = slice(place * padded, place * padded + width)
            cards[part, :2, rows] = pairs[:, far]
            gather[part, rows, :CARDS] = incidence[far]
            gather[part, rows, CARDS] = 1.0
            spread[part, :CARDS, rows] = -incidence[far].T.astype(np.float32)
            spread[part, CARDS, rows] = 1.0
    near = np.zeros((parts, LANES, padded), np.float32)
    first = width - (padded - LANES)
    near[:, first:first + CARDS + 1, :width] = spread[:, :CARDS + 1, :width]
    exact = ml_dtypes.bfloat16
    return (cards, gather.astype(exact), spread.astype(exact), near.astype(exact))


def split_two(value):
    high = value.astype(BF16)
    return high, (value - high.astype(F32)).astype(BF16)


def exact_right(value, matrix):
    rows = value.shape[0]
    first = value.astype(BF16)
    rest = value - first.astype(F32)
    second = rest.astype(BF16)
    third = (rest - second.astype(F32)).astype(BF16)
    total = jnp.dot(jnp.concatenate([first, second, third], axis=0), matrix, preferred_element_type=F32)
    return total[:rows] + total[rows:2 * rows] + total[2 * rows:]


def exact_left(matrix, value):
    first = value.astype(BF16)
    rest = value - first.astype(F32)
    second = rest.astype(BF16)
    third = (rest - second.astype(F32)).astype(BF16)
    matrix = matrix.astype(BF16)
    return jnp.dot(jnp.concatenate([matrix] * 3, axis=1), jnp.concatenate([first, second, third], axis=0),
                   preferred_element_type=F32)


def pair_dot(left, right):
    rows = left.shape[0]
    left_high, left_low = split_two(left)
    right_high, right_low = split_two(right)
    total = jnp.dot(
        jnp.concatenate([jnp.concatenate([left_high] * 2, axis=1), jnp.concatenate([left_low] * 2, axis=1)], axis=0),
        jnp.concatenate([right_high, right_low], axis=0), preferred_element_type=F32)
    return total[:rows] + total[rows:]


def alive_rows(card_rows, turn_cards):
    one, two = card_rows[0:1], card_rows[1:2]
    held = one < 0
    for place in range(4):
        card = turn_cards[place]
        held = held | (one == card) | (two == card)
    return jnp.where(held, 0.0, 1.0).astype(F32)


def row_sums(value):
    return jnp.sum(value, axis=0, keepdims=True)


def steps_from(own_norms, far_norms, count):
    totals = jnp.sum(own_norms + far_norms, axis=1, keepdims=True)
    weight = jnp.sqrt((totals[1:2] / count + EPSILON) / (totals[0:1] / count + EPSILON))
    return STEP_SCALE / weight, STEP_SCALE * weight


def river_steps(children_ref, parents_ref):
    sequences = children_ref.shape[1]
    step = (children_ref[...] - parents_ref[:, :sequences]).astype(F32)
    return step, parents_ref[:, sequences:].astype(F32)


def river_link(parents_ref, sequences):
    return parents_ref[:, sequences:].astype(F32)


def stats_kernel(slots, group, river_axis, loads_ref, cards_now_ref, card_ref, rank_ref, x_ref, v_ref, y_ref, u_ref,
                 xt_ref, vt_ref, yt_ref, ut_ref, children_ref, parents_ref,
                 sums_ref, pack_ref, live_scratch, plan_scratch):
    at = pl.program_id(0)
    padded = live_scratch.shape[2]
    prices = v_ref.shape[1]
    nx, ny = 3 * prices, 3 * prices + 1
    river_here = lax.axis_index(river_axis)

    @pl.when(at == 0)
    def _():
        turn = alive_rows(card_ref[0, :, :padded], cards_now_ref)
        slot = lax.broadcasted_iota(jnp.int32, (slots, padded), 0)
        rank = rank_ref[...]
        live = jnp.where((rank >= 0) & (slot < loads_ref[river_here]) & (turn > 0), 1.0, 0.0)
        for board in range(slots):
            live_scratch[board] = live[board:board + 1]
        sums_ref[...] = jnp.zeros_like(sums_ref)
        plan_scratch[...] = jnp.zeros_like(plan_scratch)
        pack_ref[...] = jnp.zeros_like(pack_ref)
        first = jnp.where(river_here == 0, 1.0, 0.0)
        base = 0
        for rows, row in ((xt_ref, nx), (yt_ref, ny), (vt_ref, nx), (ut_ref, ny)):
            value = jnp.where(turn > 0, rows[...], 0.0)
            pack_ref[base:base + value.shape[0]] = value
            base += round_up(value.shape[0], 8)
            sums_ref[row:row + 1] += first * row_sums(value * value)

    mover = jnp.zeros((1, padded), F32)
    rival = jnp.zeros((1, padded), F32)
    for inner in range(group):
        live = live_scratch[at * group + inner] > 0
        x = jnp.where(live, x_ref[inner], 0.0)
        v = jnp.where(live, v_ref[inner], 0.0)
        y = jnp.where(live, y_ref[inner], 0.0)
        u = jnp.where(live, u_ref[inner], 0.0)
        mover = mover + row_sums(x * x) + row_sums(v * v)
        rival = rival + row_sums(y * y) + row_sums(u * u)
        sums_ref[0:prices] += u
        sums_ref[prices:2 * prices] += v
        plan_scratch[...] += y
    sums_ref[nx:nx + 1] += mover
    sums_ref[ny:ny + 1] += rival

    @pl.when(at == pl.num_programs(0) - 1)
    def _():
        step, _ = river_steps(children_ref, parents_ref)
        sums_ref[2 * prices:3 * prices] = exact_left(step, plan_scratch[...])


def prepare_kernel(slots, group, river_axis, loads_ref, cards_now_ref, card_ref, gather_ref, spread_ref, own_ref, far_ref,
                   near_table_ref, pot_ref, fold_ref, children_ref, parents_ref,
                   live_ref, row_ref, col_ref, compat_ref, near_ref, main_ref, folds_ref, back_ref):
    padded = row_ref.shape[2]
    rank = jnp.concatenate([own_ref[...], far_ref[...]], axis=1)
    turn = alive_rows(card_ref[0], cards_now_ref)
    slot = lax.broadcasted_iota(jnp.int32, rank.shape, 0)
    live = jnp.where((rank >= 0) & (slot < loads_ref[lax.axis_index(river_axis)]) & (turn > 0), 1.0, 0.0)
    safe = jnp.where(live > 0, rank, 0)
    code = (128 + (safe & 127)).astype(F32)
    high = safe >> 7
    for bit in range(6):
        code = code * jnp.where((high >> bit) & 1 == 1, float(2.0 ** (1 << bit)), 1.0)
    lane = lax.broadcasted_iota(jnp.int32, rank.shape, 1)
    width = H // 2
    own_code = jnp.where(lane[:, :padded] < width, code[:, :padded], 0.0)
    for board in range(slots):
        live_ref[board] = live[board:board + 1]
        row_ref[board] = own_code[board:board + 1].astype(BF16)
    depth = round_up(slots, 8)
    if depth > slots:
        code = jnp.concatenate([code, jnp.zeros((depth - slots, code.shape[1]), F32)], axis=0)
    turned = code.T
    for place in range(slots // group):
        col_ref[place] = turned[:, place * group:(place + 1) * group]
    free = jnp.dot(gather_ref[0], spread_ref[0][:, :padded], preferred_element_type=F32)
    compat_ref[...] = jnp.maximum(free, 0.0).astype(BF16)
    near_ref[...] = near_table_ref[0]
    for place in range(2):
        set_operators(place == 1, pot_ref, fold_ref, children_ref, parents_ref, main_ref.at[place], folds_ref.at[place],
                      back_ref.at[place])


def set_operators(transposed, pot_ref, fold_ref, children_ref, parents_ref, main_scratch, fold_scratch, back_scratch):
    pot = pot_ref[...] / H
    fold = fold_ref[...] / H
    if transposed:
        pot, fold = -pot.T, fold.T
    step, _ = river_steps(children_ref, parents_ref)
    sequences = pot.shape[0]
    infosets = step.shape[0]
    pot_high, pot_low = split_two(pot)
    fold_high, fold_low = split_two(fold)
    main_scratch[:sequences] = jnp.concatenate([pot_high, pot_high, fold_high, fold_high], axis=1)
    main_scratch[sequences:2 * sequences] = jnp.concatenate([pot_low, pot_low, fold_low, fold_low], axis=1)
    exact = step.astype(BF16)
    main_scratch[2 * sequences:2 * sequences + infosets] = jnp.concatenate(
        [jnp.zeros((infosets, 2 * sequences), BF16), exact, exact], axis=1)
    fold_scratch[:sequences] = jnp.concatenate([fold_high, fold_high], axis=1)
    fold_scratch[sequences:] = jnp.concatenate([fold_low, fold_low], axis=1)
    turned = step.T
    if transposed:
        turned = -turned
    turned = turned.astype(BF16)
    back_scratch[...] = jnp.concatenate([turned, turned], axis=1)


def payoffs(own_plans, far_plans, prices, columns, strengths, compat_ref, near_ref, main, folds, back_step):
    sequences, padded = own_plans[0].shape
    tiles = padded // TILE
    width = H // 2
    depths = [min(TILE, round_up(width - at, 16)) for at in range(0, width, TILE)]
    boards = range(len(own_plans))
    owns = [split_two(plan) for plan in own_plans]
    fars = [split_two(plan) for plan in far_plans]
    price_parts = [split_two(price) for price in prices]
    mixes = []
    for inner in boards:
        left = (jnp.concatenate(owns[inner], axis=0), jnp.concatenate(fars[inner], axis=0))
        row = strengths[inner]
        sums = [None] * tiles
        for place in range(2 * tiles):
            depth = depths[place % tiles]
            rows = slice(place * TILE, place * TILE + depth)
            column = jnp.broadcast_to(columns(rows, inner), (depth, LANES)).astype(BF16)
            column = jnp.concatenate([column, column], axis=1)
            piece = left[place // tiles][:, (place % tiles) * TILE:(place % tiles) * TILE + depth]
            for across in range(tiles):
                lanes = slice(across * TILE, (across + 1) * TILE)
                bound = compat_ref[rows, lanes]
                signs = jnp.minimum(jnp.maximum(column - row[:, lanes], -bound), bound)
                part = jnp.dot(piece, signs, preferred_element_type=F32)
                sums[across] = part if sums[across] is None else sums[across] + part
        mixes.append(split_two(jnp.concatenate([item[:sequences] + item[sequences:] for item in sums], axis=1)))
    cards = []
    for inner in boards:
        tail = jnp.concatenate([item[:, padded - LANES:] for item in mixes[inner]], axis=0)
        folded = jnp.dot(folds, tail, preferred_element_type=F32)
        cards.extend(split_two(folded[:sequences] + folded[sequences:]))
    backs = [jnp.dot(back_step, jnp.concatenate(price_parts[inner], axis=0), preferred_element_type=F32) for inner in boards]
    products = [jnp.dot(main, jnp.concatenate(mixes[inner] + owns[inner], axis=0), preferred_element_type=F32)
                for inner in boards]
    nearby = jnp.dot(jnp.concatenate(cards, axis=0), near_ref[...], preferred_element_type=F32)
    done = []
    for inner in boards:
        base = 2 * inner * sequences
        close = nearby[base:base + sequences] + nearby[base + sequences:base + 2 * sequences]
        product = products[inner]
        done.append((product[:sequences] + product[sequences:2 * sequences] + backs[inner] + close, product[2 * sequences:]))
    return done


def pick(ref, base, at, inner, group):
    return ref[inner] if base is None else ref[base + at * group + inner]


def group_payoffs(group, start, side, at, plans, fars, prices, live_ref, row_ref, col_ref, compat_ref, near_ref,
                  main_ref, folds_ref, back_ref):
    strengths = [row_ref[start + at * group + inner] for inner in range(group)]

    def columns(rows, inner):
        return col_ref[start // group + at, rows, inner:inner + 1]

    return payoffs(plans, fars, prices, columns, strengths, compat_ref, near_ref, main_ref[side], folds_ref[side],
                   back_ref[side])


def mover_gradient_kernel(group, start, bases, turn_row, y_ref, far_ref, u_ref, live_ref, row_ref, col_ref, compat_ref,
                          near_ref, main_ref, folds_ref, back_ref, pack_ref, parents_ref, grad_ref, flow_ref):
    _, sequences, padded = grad_ref.shape
    link = river_link(parents_ref, sequences)
    turn_flow = exact_left(link, pack_ref[turn_row:turn_row + link.shape[1], :padded])
    own_plans, far_plans, prices, lives = [], [], [], []
    for inner in range(group):
        live = live_ref[start + inner]
        near_live = live[:, :padded]
        lives.append(near_live)
        own_plans.append(jnp.where(near_live > 0, pick(y_ref, bases[0], 0, inner, group), 0.0))
        far_plans.append(jnp.where(live[:, padded:] > 0, pick(far_ref, bases[1], 0, inner, group), 0.0))
        prices.append(jnp.where(near_live > 0, pick(u_ref, bases[2], 0, inner, group), 0.0))
    done = group_payoffs(group, start, 0, 0, own_plans, far_plans, prices, live_ref, row_ref, col_ref, compat_ref, near_ref,
                         main_ref, folds_ref, back_ref)
    for inner, (gradient, flow) in enumerate(done):
        grad_ref[inner] = gradient
        flow_ref[inner] = lives[inner] * (flow - turn_flow)


def mover_step_kernel(group, start, bases, count, norm_row, parts, last, own_norm_ref, far_norm_ref, x_ref, v_ref, live_ref,
                      *rest):
    grads, flows = rest[:parts], rest[parts:2 * parts]
    if last:
        new_x_ref, new_v_ref, bar_ref = rest[-3:]
    else:
        new_x_ref, new_v_ref, bar_ref, total_ref = rest[-4:]
        total_ref[...] = rest[2 * parts][...] if start else jnp.zeros_like(total_ref)
    padded = bar_ref.shape[2]
    primal, _ = steps_from(own_norm_ref[norm_row:norm_row + 8], far_norm_ref[norm_row:norm_row + 8], count)
    for board in range(parts * group):
        live = live_ref[start + board][:, :padded]
        x = jnp.where(live > 0, pick(x_ref, bases[0], 0, board, group), 0.0)
        v = jnp.where(live > 0, pick(v_ref, bases[1], 0, board, group), 0.0)
        new_x = live * jnp.maximum(x - primal * grads[board // group][board % group], 0.0)
        new_v = v + primal * flows[board // group][board % group]
        new_x_ref[board] = new_x
        new_v_ref[board] = new_v
        bar_ref[board] = 2.0 * new_x - x
        if not last:
            total_ref[0:1] += row_sums(new_x * new_x) + row_sums(new_v * new_v)


def rival_step_kernel(group, start, bases, count, norm_row, parts, last, own_norm_ref, far_norm_ref, bar_ref, far_ref, y_ref,
                      u_ref, new_v_ref, live_ref, row_ref, col_ref, compat_ref, near_ref, main_ref, folds_ref, back_ref,
                      bart_ref, children_ref, parents_ref, *rest):
    flows = rest[:parts]
    rest = rest[parts:]
    at = pl.program_id(0)
    if last:
        new_y_ref, new_u_ref, link_scratch, flow_scratch, step_scratch = rest[-5:]
    else:
        new_y_ref, new_u_ref, total_ref, link_scratch, flow_scratch, step_scratch, plan_scratch = rest[-7:]
    padded = live_ref.shape[2] // 2
    infosets = u_ref.shape[1]
    nx, ny = 2 * infosets, 2 * infosets + 1

    @pl.when(at == 0)
    def _():
        primal, dual = steps_from(own_norm_ref[norm_row:norm_row + 8], far_norm_ref[norm_row:norm_row + 8], count)
        step_scratch[0:1, :] = jnp.broadcast_to(primal, (1, LANES))
        step_scratch[1:2, :] = jnp.broadcast_to(dual, (1, LANES))
        link_scratch[...] = exact_left(river_link(parents_ref, bar_ref.shape[1]), bart_ref[:, :padded])
        if not last:
            plan_scratch[...] = jnp.zeros_like(plan_scratch)
            if start:
                total_ref[...] = rest[0][...]
            else:
                total_ref[...] = jnp.zeros_like(total_ref)
                total_ref[nx:ny + 1] = rest[0][0:2] + rest[1][0:2]

    for part in range(parts):
        @pl.when(at == part)
        def _():
            flow_scratch[...] = flows[part][...]

    primal = step_scratch[0:1, 0:1]
    dual = step_scratch[1:2, 0:1]
    own_plans, far_plans, prices = [], [], []
    for inner in range(group):
        own_plans.append(pick(bar_ref, bases[0], at, inner, group))
        far_plans.append(pick(far_ref, bases[1], at, inner, group))
        prices.append(pick(new_v_ref, bases[4], at, inner, group) + primal * flow_scratch[inner])
    done = group_payoffs(group, start, 1, at, own_plans, far_plans, prices, live_ref, row_ref, col_ref, compat_ref, near_ref,
                         main_ref, folds_ref, back_ref)
    for inner, (gradient, flow) in enumerate(done):
        live = live_ref[start + at * group + inner][:, :padded]
        y = jnp.where(live > 0, pick(y_ref, bases[2], at, inner, group), 0.0)
        u = jnp.where(live > 0, pick(u_ref, bases[3], at, inner, group), 0.0)
        flow = live * flow
        new_y = live * jnp.maximum(y + dual * gradient, 0.0)
        new_u = u + dual * (flow - live * link_scratch[...])
        place = inner if last else at * group + inner
        new_y_ref[place] = new_y
        new_u_ref[place] = new_u
        if not last:
            plan_scratch[...] += new_y
            total_ref[0:infosets] += flow
            total_ref[ny:ny + 1] += row_sums(new_y * new_y) + row_sums(new_u * new_u)

    if not last:
        @pl.when(at == pl.num_programs(0) - 1)
        def _():
            step, _ = river_steps(children_ref, parents_ref)
            total_ref[infosets:2 * infosets] += exact_left(step, plan_scratch[...])


def turn_step_kernel(count, first, names, hand_ref, cards_now_ref, card_ref, gather_ref, spread_ref, *rest):
    if first:
        own_ref, far_ref, sums_ref, sums_far_ref = rest[:4]
        rest = rest[4:]
    else:
        pack_ref, kept_ref, old_bar_ref, old_steps_ref, sums_ref, sums_far_ref = rest[:6]
        rest = rest[6:]
    turn_fold_ref, turn_children_ref, turn_parents_ref, children_ref, parents_ref = rest[:5]
    rest = rest[5:]
    turn = alive_rows(card_ref[0], cards_now_ref)
    _, link = river_steps(children_ref, parents_ref)
    link_turned = link.T
    parents = turn_parents_ref[...].astype(F32)
    turn_step = turn_children_ref[...].astype(F32) - parents
    turn_root = 1.0 - jnp.sum(parents, axis=1, keepdims=True)
    step_turned = turn_step.T
    fold = turn_fold_ref[...]
    meetings = (CARDS - 6) * turn
    sequences = fold.shape[0]
    points = turn_step.shape[0]
    slab = round_up(points, 8)
    starts = (0, 2 * sequences, sequences, 2 * sequences + slab)
    infosets = link.shape[0]
    norm_row = (3 if first else 2) * infosets
    primal, dual = steps_from(sums_ref[norm_row:norm_row + 8], sums_far_ref[norm_row:norm_row + 8], count)
    sums = jnp.concatenate([sums_ref[:norm_row], sums_far_ref[:norm_row]], axis=1)
    if first:
        pack = jnp.concatenate([own_ref[...], far_ref[...]], axis=1)
        price_sum = sums[:infosets]
        kept = sums[infosets:2 * infosets]
        plan_sum = sums[2 * infosets:]
    else:
        pack = pack_ref[...]
        old_dual = old_steps_ref[1:2, 0:1]
        price_sum = kept_ref[:infosets] + old_dual * (
            sums[:infosets] - meetings * exact_left(link, old_bar_ref[...]))
        kept = kept_ref[infosets:]
        plan_sum = sums[infosets:]
    x = pack[starts[0]:starts[0] + sequences]
    v = pack[starts[1]:starts[1] + points]
    y = pack[starts[2]:starts[2] + sequences]
    u = pack[starts[3]:starts[3] + points]

    def mix(plan):
        return turn * (exact_right(exact_right(plan, gather_ref[0]), spread_ref[0]) + plan)

    grad = pair_dot(fold, mix(y)) / H + turn * (exact_left(step_turned, u) - exact_left(link_turned, price_sum))
    new_x = turn * jnp.maximum(x - primal * grad, 0.0)
    new_v = v + primal * (turn * (exact_left(turn_step, y) - turn_root))
    bar = 2.0 * new_x - x
    price_bar = 2.0 * new_v - v
    drift = primal * (plan_sum - meetings * exact_left(link, y))
    rise = pair_dot(fold.T, mix(bar)) / H - turn * (
        exact_left(step_turned, price_bar) - exact_left(link_turned, kept + 2.0 * drift))
    new_y = turn * jnp.maximum(y + dual * rise, 0.0)
    new_u = u + dual * (turn * (exact_left(turn_step, bar) - turn_root))
    if first:
        out_pack_ref, out_kept_ref, bar_ref, out_norms_ref, steps_ref = rest
        steps_ref[0:1] = jnp.broadcast_to(primal, (1, LANES))
        steps_ref[1:2] = jnp.broadcast_to(dual, (1, LANES))
        out_pack_ref[...] = jnp.zeros_like(out_pack_ref)
        for start, value in zip(starts, (new_x, new_v, new_y, new_u)):
            out_pack_ref[start:start + value.shape[0]] = value
        out_kept_ref[:infosets] = price_sum
        out_kept_ref[infosets:] = kept + drift
        bar_ref[...] = bar
        river_name, hand_name = names
        flag = jnp.where((lax.axis_index(river_name) == 0) & (hand_ref[0] == 0), 1.0, 0.0)
        out_norms_ref[...] = jnp.zeros_like(out_norms_ref)
        mover = row_sums(new_x * new_x) + row_sums(new_v * new_v)
        rival = row_sums(new_y * new_y) + row_sums(new_u * new_u)
        half = mover.shape[1] // 2
        out_norms_ref[0:1] = flag * (mover[:, :half] + mover[:, half:])
        out_norms_ref[1:2] = flag * (rival[:, :half] + rival[:, half:])
    else:
        bar_ref = rest[0]
        bar_ref[...] = bar
        for out_ref, value in zip(rest[1:], (new_x, new_v, new_y, new_u)):
            out_ref[...] = value[:, :out_ref.shape[1]]


def whole(shape):
    return pl.BlockSpec(shape, lambda *at: (0,) * len(shape))


def smem():
    return pl.BlockSpec(memory_space=pltpu.SMEM)


def local(hand_rank, loads, turn_cards, turn_children, turn_parents, river_children, river_parents, showdown_pot, river_fold,
          turn_fold, mover_turn, mover_river, mover_turn_price, mover_river_price, rival_turn, rival_river,
          rival_turn_price, rival_river_price):
    slots, sequences, width = mover_river.shape
    infosets = mover_river_price.shape[1]
    turn_sequences = mover_turn.shape[0]
    points = mover_turn_price.shape[0]
    river_count = lax.axis_size("river")
    padded = round_up(width + CARDS + 1, TILE)
    both = 2 * padded
    count = float((turn_sequences + points) * H + river_count * slots * (sequences + infosets) * H)
    group = next(size for size in (3, 2, 1) if slots % size == 0)
    chunks = slots // group
    parts = 2 if chunks % 2 == 0 else 1
    span = parts * group
    cards, gather, spread, near = (jnp.asarray(table) for table in halves(width, padded))
    hand = lax.axis_index("hand").astype(jnp.int32).reshape(1)
    pack_rows = 2 * (turn_sequences + round_up(points, 8))
    stat_rows = 3 * infosets + 8
    total_rows = 2 * infosets + 8

    def shape(*dims, dtype=F32):
        return jax.ShapeDtypeStruct(dims, dtype)

    def swap(value):
        return lax.ppermute(value, "hand", [(0, 1), (1, 0)])

    def hop_total(value, hop, gate):
        came = lax.ppermute(value, "river", [(at, at ^ hop) for at in range(river_count)])
        if gate is not None:
            came, _ = lax.optimization_barrier((came, gate))
        return value + came

    def reduced(value, gates):
        gates = list(gates)
        if river_count & (river_count - 1):
            value = lax.psum(value, "river")
        else:
            hop = 1
            while hop < river_count:
                value = hop_total(value, hop, gates.pop(0) if gates else None)
                hop *= 2
        far = swap(value)
        if gates:
            far, _ = lax.optimization_barrier((far, gates[0]))
        return value, far

    def boards(rows, size=group, start=0):
        return pl.BlockSpec((size, rows, padded), lambda at, *_: (at + start, 0, 0))

    vmem = pl.BlockSpec(memory_space=pltpu.VMEM)

    def operand(item, first, size):
        if isinstance(item, list):
            length = slots // len(item)
            return item[first // length], vmem, first % length
        return item, boards(item.shape[1], size, first // size), None

    def call(kernel, name, scalars, steps, in_specs, out_specs, out_shape, scratch, args, micros, aliases=None, vmem=VMEM_BYTES):
        estimate = pl.CostEstimate(flops=int(micros * 1e9), bytes_accessed=0, transcendentals=0)
        return pl.pallas_call(
            kernel,
            grid_spec=pltpu.PrefetchScalarGridSpec(
                num_scalar_prefetch=scalars, grid=steps, in_specs=in_specs, out_specs=out_specs, scratch_shapes=scratch),
            out_shape=out_shape, compiler_params=pltpu.CompilerParams(vmem_limit_bytes=vmem),
            cost_estimate=estimate, input_output_aliases=aliases or {}, name=name,
        )(*args)

    card_block = pl.BlockSpec((1, 8, both), lambda at, ref: (ref[0], 0, 0))
    tree_blocks = [whole(river_children.shape), whole(river_parents.shape)]
    half_block = lambda rows, at_row=0: pl.BlockSpec((rows, padded), lambda at, *_: (at_row, 0))
    operator_sizes = ((2 * sequences + infosets, 4 * sequences), (2 * sequences, 2 * sequences), (sequences, 2 * infosets))
    link_scratch = pltpu.VMEM((infosets, padded), F32)
    flow_scratch = pltpu.VMEM((group, infosets, padded), F32)
    step_scratch = pltpu.VMEM((8, LANES), F32)
    plan_scratch = pltpu.VMEM((sequences, padded), F32)
    any_block = pl.BlockSpec(memory_space=pl.ANY)

    rank_far = swap(hand_rank)
    rival_far = swap(rival_river)

    def stats_kernel_here(hand_ref, *refs):
        stats_kernel(slots, group, "river", *refs)

    def prepare_kernel_here(hand_ref, *refs):
        prepare_kernel(slots, group, "river", *refs)

    sums, pack = call(
        stats_kernel_here, "stats", 1, (slots // group,),
        [smem(), smem(), card_block, half_block(slots), boards(sequences), boards(infosets),
         boards(sequences), boards(infosets), half_block(turn_sequences), half_block(points),
         half_block(turn_sequences), half_block(points)] + tree_blocks,
        [whole((stat_rows, padded)), whole((pack_rows, padded))],
        [shape(stat_rows, padded), shape(pack_rows, padded)],
        [pltpu.VMEM((slots, 1, padded), F32), plan_scratch],
        (hand, loads, turn_cards, cards, hand_rank, mover_river, mover_river_price, rival_river, rival_river_price,
         mover_turn, mover_turn_price, rival_turn, rival_turn_price, river_children, river_parents), 5,
        vmem=56 * 2**20)
    gather_block = pl.BlockSpec((1, both, LANES), lambda at, ref: (ref[0], 0, 0))
    spread_block = pl.BlockSpec((1, LANES, both), lambda at, ref: (ref[0], 0, 0))
    prepared = [shape(slots, 1, both), shape(slots, 1, padded, dtype=BF16), shape(slots // group, both, group),
                shape(both, padded, dtype=BF16), shape(LANES, padded, dtype=BF16)] + [shape(2, *size, dtype=BF16) for size in operator_sizes]
    near_block = pl.BlockSpec((1, LANES, padded), lambda at, ref: (ref[0], 0, 0))
    tables = call(
        prepare_kernel_here, "prepare", 1, (1,),
        [smem(), smem(), card_block, gather_block, spread_block, half_block(slots), half_block(slots), near_block,
         whole(showdown_pot.shape), whole(river_fold.shape)] + tree_blocks,
        [vmem] * len(prepared), prepared, [],
        (hand, loads, turn_cards, cards, gather, spread, hand_rank, rank_far, near, showdown_pot, river_fold,
         river_children, river_parents), 2)
    live = tables[0]

    def gradients(y, y_far, u, pack):
        out = []
        for first in range(0, slots, group):
            arrays, specs, bases = zip(*(operand(item, first, group) for item in (y, y_far, u)))
            args = (*arrays, *tables, pack, river_parents)
            out.append(call(
                functools.partial(mover_gradient_kernel, group, first, bases, turn_sequences), "mover_gradient", 0, (1,),
                [*specs] + [vmem] * (len(args) - 3), [vmem] * 2,
                [shape(group, sequences, padded), shape(group, infosets, padded)], [], args, group))
        return [item[0] for item in out], [item[1] for item in out]

    def mover_steps(last, norms, norm_row, x, v, grad, flow):
        outs = []
        for first in range(0, slots, span):
            arrays, specs, bases = zip(*(operand(item, first, span) for item in (x, v)))
            here = slice(first // group, first // group + parts)
            args = (*norms, *arrays, live, *grad[here], *flow[here])
            in_specs = [vmem] * 2 + [*specs] + [vmem] * (1 + 2 * parts)
            aliases = {}
            if last:
                out_specs = [boards(sequences, span, first // span), boards(infosets, span, first // span), vmem]
                out_shape = [shape(slots, sequences, width), shape(slots, infosets, width), shape(span, sequences, padded)]
                if first:
                    aliases = {len(args): 0, len(args) + 1: 1}
                    in_specs += [any_block] * 2
                    args += tuple(outs[-1][:2])
            else:
                out_specs = [vmem] * 4
                out_shape = [shape(span, sequences, padded), shape(span, infosets, padded),
                             shape(span, sequences, padded), shape(8, padded)]
                if first:
                    in_specs += [vmem]
                    args += (outs[-1][3],)
            outs.append(call(functools.partial(mover_step_kernel, group, first, bases, count, norm_row, parts, last),
                             "mover_step", 0, (1,), in_specs, out_specs, out_shape, [], args, parts, aliases))
        if last:
            return outs[-1][0], outs[-1][1], [item[2] for item in outs]
        return [item[0] for item in outs], [item[1] for item in outs], [item[2] for item in outs], outs[-1][3]

    def rival_steps(last, norms, norm_row, bar, bar_far, y, u, new_v, flow, bar_turn, parts_before):
        outs = []
        for first in range(0, slots, span):
            arrays, specs, bases = zip(*(operand(item, first, group) for item in (bar, bar_far, y, u, new_v)))
            here = slice(first // group, first // group + parts)
            args = (*norms, *arrays, *tables, bar_turn, river_children, river_parents, *flow[here])
            in_specs = [vmem] * 2 + [*specs] + [vmem] * (len(args) - 7)
            aliases = {}
            scratch = [link_scratch, flow_scratch, step_scratch]
            if last:
                out_specs = [boards(sequences, group, first // group), boards(infosets, group, first // group)]
                out_shape = [shape(slots, sequences, width), shape(slots, infosets, width)]
                if first:
                    aliases = {len(args): 0, len(args) + 1: 1}
                    in_specs += [any_block] * 2
                    args += tuple(outs[-1][:2])
            else:
                out_specs = [vmem] * 3
                out_shape = [shape(span, sequences, padded), shape(span, infosets, padded), shape(total_rows, padded)]
                scratch = scratch + [plan_scratch]
                before = (outs[-1][2],) if first else tuple(parts_before)
                in_specs += [vmem] * len(before)
                args += before
            outs.append(call(functools.partial(rival_step_kernel, group, first, bases, count, norm_row, parts, last),
                             "rival_step", 0, (parts,), in_specs, out_specs, out_shape, scratch, args, span, aliases))
        if last:
            return outs[-1]
        return [item[0] for item in outs], [item[1] for item in outs], outs[-1][2]

    turn_blocks = [smem(), card_block, gather_block, spread_block]
    turn_tables = (turn_cards, cards, gather, spread)
    turn_matrices = (turn_fold, turn_children, turn_parents, river_children, river_parents)

    def turn_call(first, data):
        if first:
            out_shape = [shape(pack_rows, both), shape(2 * infosets, both), shape(turn_sequences, both), shape(8, padded),
                         shape(8, LANES)]
        else:
            out_shape = [shape(turn_sequences, both), shape(turn_sequences, width), shape(points, width),
                         shape(turn_sequences, width), shape(points, width)]
        return call(
            functools.partial(turn_step_kernel, count, first, ("river", "hand")), "turn_step", 1, (1,),
            turn_blocks + [vmem] * len(data) + [whole(item.shape) for item in turn_matrices],
            [vmem] * 5 if first else [vmem] + [whole(item.shape) for item in out_shape[1:]],
            out_shape, [], (hand, *turn_tables, *data, *turn_matrices), 3)

    pack_far = swap(pack)
    grad, flow = gradients(rival_river, rival_far, rival_river_price, pack)
    norms = reduced(sums, [live] + flow[:3])
    x, v, bar, part = mover_steps(False, norms, 3 * infosets, mover_river, mover_river_price, grad, flow)
    bar_far = [swap(item) for item in bar]
    pack, kept, bar_turn, turn_norms, turn_steps = turn_call(True, (pack, pack_far, *norms))
    y, u, total = rival_steps(False, norms, 3 * infosets, bar, bar_far, rival_river, rival_river_price, v, flow, bar_turn,
                              (part, turn_norms))
    y_far = [swap(item) for item in y]
    grad, flow = gradients(y, y_far, u, pack)
    norms = reduced(total, flow)
    next_x, next_v, bar = mover_steps(True, norms, 2 * infosets, x, v, grad, flow)
    bar_far = [swap(item) for item in bar]
    bar_turn, next_xt, next_vt, next_yt, next_ut = turn_call(False, (pack, kept, bar_turn, turn_steps, *norms))
    next_y, next_u = rival_steps(True, norms, 2 * infosets, bar, bar_far, y, u, next_v, flow, bar_turn, None)
    return (next_xt, next_x, next_vt, next_v, next_yt, next_y, next_ut, next_u)


def solution(mesh):
    river = P(("groups", "river"), None, "hand")
    turn = P("groups", "hand")
    placed = (P(("groups", "river"), "hand"), P("groups"), P("groups"), P(), P(), P(), P(), P(), P(), P(),
              turn, river, turn, river, turn, river, turn, river)
    return jax.shard_map(local, mesh=mesh, in_specs=placed,
                         out_specs=(turn, river, turn, river, turn, river, turn, river), check_vma=False)
```

```python
import functools

import jax
import jax.numpy as jnp
import ml_dtypes
import numpy as np
from jax import lax
from jax.experimental import pallas as pl
from jax.experimental.pallas import tpu as pltpu
from jax.sharding import PartitionSpec as P

CARDS = 52
H = 1326
ITERS = 2
STEP_SCALE = 0.25
EPSILON = 1e-06
LANES = 128
TILE = 256
VMEM_BYTES = 20 * 2**20
STATS_BOARDS = 6
F32 = jnp.float32
BF16 = jnp.bfloat16


def round_up(value, unit):
    return -(-value // unit) * unit


def halves(width, padded):
    pairs = np.stack(np.triu_indices(CARDS, 1)).astype(np.int32)
    deck = np.arange(CARDS)
    incidence = (pairs[0][:, None] == deck) | (pairs[1][:, None] == deck)
    parts = pairs.shape[1] // width
    cards = np.full((parts, 8, 2 * padded), -1, np.int32)
    gather = np.zeros((parts, 2 * padded, LANES), np.float32)
    spread = np.zeros((parts, LANES, 2 * padded), np.float32)
    for part in range(parts):
        spread[part, np.arange(CARDS + 1), width + np.arange(CARDS + 1)] = 1.0
        for place, half in enumerate((part, 1 - part)):
            far = slice(half * width, (half + 1) * width)
            rows = slice(place * padded, place * padded + width)
            cards[part, :2, rows] = pairs[:, far]
            gather[part, rows, :CARDS] = incidence[far]
            gather[part, rows, CARDS] = 1.0
            spread[part, :CARDS, rows] = -incidence[far].T.astype(np.float32)
            spread[part, CARDS, rows] = 1.0
    near = np.zeros((parts, LANES, padded), np.float32)
    first = width - (padded - LANES)
    near[:, first:first + CARDS + 1, :width] = spread[:, :CARDS + 1, :width]
    exact = ml_dtypes.bfloat16
    return (cards, gather.astype(exact), spread.astype(exact), near.astype(exact))


def split_two(value):
    high = value.astype(BF16)
    return high, (value - high.astype(F32)).astype(BF16)


def exact_right(value, matrix):
    rows = value.shape[0]
    first = value.astype(BF16)
    rest = value - first.astype(F32)
    second = rest.astype(BF16)
    third = (rest - second.astype(F32)).astype(BF16)
    total = jnp.dot(jnp.concatenate([first, second, third], axis=0), matrix, preferred_element_type=F32)
    return total[:rows] + total[rows:2 * rows] + total[2 * rows:]


def exact_left(matrix, value):
    first = value.astype(BF16)
    rest = value - first.astype(F32)
    second = rest.astype(BF16)
    third = (rest - second.astype(F32)).astype(BF16)
    matrix = matrix.astype(BF16)
    return jnp.dot(jnp.concatenate([matrix] * 3, axis=1), jnp.concatenate([first, second, third], axis=0),
                   preferred_element_type=F32)


def pair_dot(left, right):
    rows = left.shape[0]
    left_high, left_low = split_two(left)
    right_high, right_low = split_two(right)
    total = jnp.dot(
        jnp.concatenate([jnp.concatenate([left_high] * 2, axis=1), jnp.concatenate([left_low] * 2, axis=1)], axis=0),
        jnp.concatenate([right_high, right_low], axis=0), preferred_element_type=F32)
    return total[:rows] + total[rows:]


def alive_rows(card_rows, turn_cards):
    one, two = card_rows[0:1], card_rows[1:2]
    held = one < 0
    for place in range(4):
        card = turn_cards[place]
        held = held | (one == card) | (two == card)
    return jnp.where(held, 0.0, 1.0).astype(F32)


def row_sums(value):
    return jnp.sum(value, axis=0, keepdims=True)


def steps_from(own_norms, far_norms, count):
    totals = jnp.sum(own_norms + far_norms, axis=1, keepdims=True)
    weight = jnp.sqrt((totals[1:2] / count + EPSILON) / (totals[0:1] / count + EPSILON))
    return STEP_SCALE / weight, STEP_SCALE * weight


def river_steps(children_ref, parents_ref):
    sequences = children_ref.shape[1]
    step = (children_ref[...] - parents_ref[:, :sequences]).astype(F32)
    return step, parents_ref[:, sequences:].astype(F32)


def river_link(parents_ref, sequences):
    return parents_ref[:, sequences:].astype(F32)


def stats_kernel(slots, group, river_axis, loads_ref, cards_now_ref, card_ref, rank_ref, x_ref, v_ref, y_ref, u_ref,
                 xt_ref, vt_ref, yt_ref, ut_ref, children_ref, parents_ref,
                 sums_ref, pack_ref, live_scratch, plan_scratch):
    at = pl.program_id(0)
    padded = live_scratch.shape[2]
    prices = v_ref.shape[1]
    nx, ny = 3 * prices, 3 * prices + 1
    river_here = lax.axis_index(river_axis)

    @pl.when(at == 0)
    def _():
        turn = alive_rows(card_ref[0, :, :padded], cards_now_ref)
        slot = lax.broadcasted_iota(jnp.int32, (slots, padded), 0)
        rank = rank_ref[...]
        live = jnp.where((rank >= 0) & (slot < loads_ref[river_here]) & (turn > 0), 1.0, 0.0)
        for board in range(slots):
            live_scratch[board] = live[board:board + 1]
        sums_ref[...] = jnp.zeros_like(sums_ref)
        plan_scratch[...] = jnp.zeros_like(plan_scratch)
        pack_ref[...] = jnp.zeros_like(pack_ref)
        first = jnp.where(river_here == 0, 1.0, 0.0)
        base = 0
        for rows, row in ((xt_ref, nx), (yt_ref, ny), (vt_ref, nx), (ut_ref, ny)):
            value = jnp.where(turn > 0, rows[...], 0.0)
            pack_ref[base:base + value.shape[0]] = value
            base += round_up(value.shape[0], 8)
            sums_ref[row:row + 1] += first * row_sums(value * value)

    mover = jnp.zeros((1, padded), F32)
    rival = jnp.zeros((1, padded), F32)
    for inner in range(group):
        live = live_scratch[at * group + inner] > 0
        x = jnp.where(live, x_ref[inner], 0.0)
        v = jnp.where(live, v_ref[inner], 0.0)
        y = jnp.where(live, y_ref[inner], 0.0)
        u = jnp.where(live, u_ref[inner], 0.0)
        mover = mover + row_sums(x * x) + row_sums(v * v)
        rival = rival + row_sums(y * y) + row_sums(u * u)
        sums_ref[0:prices] += u
        sums_ref[prices:2 * prices] += v
        plan_scratch[...] += y
    sums_ref[nx:nx + 1] += mover
    sums_ref[ny:ny + 1] += rival

    @pl.when(at == pl.num_programs(0) - 1)
    def _():
        step, _ = river_steps(children_ref, parents_ref)
        sums_ref[2 * prices:3 * prices] = exact_left(step, plan_scratch[...])


def prepare_kernel(slots, group, river_axis, loads_ref, cards_now_ref, card_ref, gather_ref, spread_ref, own_ref, far_ref,
                   near_table_ref, pot_ref, fold_ref, children_ref, parents_ref,
                   live_ref, row_ref, col_ref, compat_ref, near_ref, main_ref, folds_ref, back_ref):
    padded = row_ref.shape[2]
    rank = jnp.concatenate([own_ref[...], far_ref[...]], axis=1)
    turn = alive_rows(card_ref[0], cards_now_ref)
    slot = lax.broadcasted_iota(jnp.int32, rank.shape, 0)
    live = jnp.where((rank >= 0) & (slot < loads_ref[lax.axis_index(river_axis)]) & (turn > 0), 1.0, 0.0)
    safe = jnp.where(live > 0, rank, 0)
    code = (128 + (safe & 127)).astype(F32)
    high = safe >> 7
    for bit in range(6):
        code = code * jnp.where((high >> bit) & 1 == 1, float(2.0 ** (1 << bit)), 1.0)
    lane = lax.broadcasted_iota(jnp.int32, rank.shape, 1)
    width = H // 2
    own_code = jnp.where(lane[:, :padded] < width, code[:, :padded], 0.0)
    for board in range(slots):
        live_ref[board] = live[board:board + 1]
        row_ref[board] = own_code[board:board + 1].astype(BF16)
    depth = round_up(slots, 8)
    if depth > slots:
        code = jnp.concatenate([code, jnp.zeros((depth - slots, code.shape[1]), F32)], axis=0)
    turned = code.T
    for place in range(slots // group):
        col_ref[place] = turned[:, place * group:(place + 1) * group]
    free = jnp.dot(gather_ref[0], spread_ref[0][:, :padded], preferred_element_type=F32)
    compat_ref[...] = jnp.maximum(free, 0.0).astype(BF16)
    near_ref[...] = near_table_ref[0]
    for place in range(2):
        set_operators(place == 1, pot_ref, fold_ref, children_ref, parents_ref, main_ref.at[place], folds_ref.at[place],
                      back_ref.at[place])


def set_operators(transposed, pot_ref, fold_ref, children_ref, parents_ref, main_scratch, fold_scratch, back_scratch):
    pot = pot_ref[...] / H
    fold = fold_ref[...] / H
    if transposed:
        pot, fold = -pot.T, fold.T
    step, _ = river_steps(children_ref, parents_ref)
    sequences = pot.shape[0]
    infosets = step.shape[0]
    pot_high, pot_low = split_two(pot)
    fold_high, fold_low = split_two(fold)
    main_scratch[:sequences] = jnp.concatenate([pot_high, pot_high, fold_high, fold_high], axis=1)
    main_scratch[sequences:2 * sequences] = jnp.concatenate([pot_low, pot_low, fold_low, fold_low], axis=1)
    exact = step.astype(BF16)
    main_scratch[2 * sequences:2 * sequences + infosets] = jnp.concatenate(
        [jnp.zeros((infosets, 2 * sequences), BF16), exact, exact], axis=1)
    fold_scratch[:sequences] = jnp.concatenate([fold_high, fold_high], axis=1)
    fold_scratch[sequences:] = jnp.concatenate([fold_low, fold_low], axis=1)
    turned = step.T
    if transposed:
        turned = -turned
    turned = turned.astype(BF16)
    back_scratch[...] = jnp.concatenate([turned, turned], axis=1)


def payoffs(own_plans, far_plans, prices, columns, strengths, compat_ref, near_ref, main, folds, back_step):
    sequences, padded = own_plans[0].shape
    tiles = padded // TILE
    width = H // 2
    depths = [min(TILE, round_up(width - at, 16)) for at in range(0, width, TILE)]
    boards = range(len(own_plans))
    owns = [split_two(plan) for plan in own_plans]
    fars = [split_two(plan) for plan in far_plans]
    price_parts = [split_two(price) for price in prices]
    mixes = []
    for inner in boards:
        left = (jnp.concatenate(owns[inner], axis=0), jnp.concatenate(fars[inner], axis=0))
        row = strengths[inner]
        sums = [None] * tiles
        for place in range(2 * tiles):
            depth = depths[place % tiles]
            rows = slice(place * TILE, place * TILE + depth)
            column = jnp.broadcast_to(columns(rows, inner), (depth, LANES)).astype(BF16)
            column = jnp.concatenate([column, column], axis=1)
            piece = left[place // tiles][:, (place % tiles) * TILE:(place % tiles) * TILE + depth]
            for across in range(tiles):
                lanes = slice(across * TILE, (across + 1) * TILE)
                bound = compat_ref[rows, lanes]
                signs = jnp.minimum(jnp.maximum(column - row[:, lanes], -bound), bound)
                part = jnp.dot(piece, signs, preferred_element_type=F32)
                sums[across] = part if sums[across] is None else sums[across] + part
        mixes.append(split_two(jnp.concatenate([item[:sequences] + item[sequences:] for item in sums], axis=1)))
    cards = []
    for inner in boards:
        tail = jnp.concatenate([item[:, padded - LANES:] for item in mixes[inner]], axis=0)
        folded = jnp.dot(folds, tail, preferred_element_type=F32)
        cards.extend(split_two(folded[:sequences] + folded[sequences:]))
    backs = [jnp.dot(back_step, jnp.concatenate(price_parts[inner], axis=0), preferred_element_type=F32) for inner in boards]
    products = [jnp.dot(main, jnp.concatenate(mixes[inner] + owns[inner], axis=0), preferred_element_type=F32)
                for inner in boards]
    nearby = jnp.dot(jnp.concatenate(cards, axis=0), near_ref[...], preferred_element_type=F32)
    done = []
    for inner in boards:
        base = 2 * inner * sequences
        close = nearby[base:base + sequences] + nearby[base + sequences:base + 2 * sequences]
        product = products[inner]
        done.append((product[:sequences] + product[sequences:2 * sequences] + backs[inner] + close, product[2 * sequences:]))
    return done


def pick(ref, base, at, inner, group):
    return ref[inner] if base is None else ref[base + at * group + inner]


def group_payoffs(group, start, side, at, plans, fars, prices, live_ref, row_ref, col_ref, compat_ref, near_ref,
                  main_ref, folds_ref, back_ref):
    strengths = [row_ref[start + at * group + inner] for inner in range(group)]

    def columns(rows, inner):
        return col_ref[start // group + at, rows, inner:inner + 1]

    return payoffs(plans, fars, prices, columns, strengths, compat_ref, near_ref, main_ref[side], folds_ref[side],
                   back_ref[side])


def mover_gradient_kernel(group, start, bases, turn_row, y_ref, far_ref, u_ref, live_ref, row_ref, col_ref, compat_ref,
                          near_ref, main_ref, folds_ref, back_ref, pack_ref, parents_ref, grad_ref, flow_ref):
    _, sequences, padded = grad_ref.shape
    link = river_link(parents_ref, sequences)
    turn_flow = exact_left(link, pack_ref[turn_row:turn_row + link.shape[1], :padded])
    own_plans, far_plans, prices, lives = [], [], [], []
    for inner in range(group):
        live = live_ref[start + inner]
        near_live = live[:, :padded]
        lives.append(near_live)
        own_plans.append(jnp.where(near_live > 0, pick(y_ref, bases[0], 0, inner, group), 0.0))
        far_plans.append(jnp.where(live[:, padded:] > 0, pick(far_ref, bases[1], 0, inner, group), 0.0))
        prices.append(jnp.where(near_live > 0, pick(u_ref, bases[2], 0, inner, group), 0.0))
    done = group_payoffs(group, start, 0, 0, own_plans, far_plans, prices, live_ref, row_ref, col_ref, compat_ref, near_ref,
                         main_ref, folds_ref, back_ref)
    for inner, (gradient, flow) in enumerate(done):
        grad_ref[inner] = gradient
        flow_ref[inner] = lives[inner] * (flow - turn_flow)


def mover_step_kernel(group, start, bases, count, norm_row, parts, last, own_norm_ref, far_norm_ref, x_ref, v_ref, live_ref,
                      *rest):
    grads, flows = rest[:parts], rest[parts:2 * parts]
    if last:
        new_x_ref, new_v_ref, bar_ref = rest[-3:]
    else:
        new_x_ref, new_v_ref, bar_ref, total_ref = rest[-4:]
        total_ref[...] = rest[2 * parts][...] if start else jnp.zeros_like(total_ref)
    padded = bar_ref.shape[2]
    primal, _ = steps_from(own_norm_ref[norm_row:norm_row + 8], far_norm_ref[norm_row:norm_row + 8], count)

    def work(part):
        for inner in range(group):
            board = part * group + inner
            place = inner if last else board
            live = live_ref[start + board][:, :padded]
            x = jnp.where(live > 0, pick(x_ref, bases[0], 0, board, group), 0.0)
            v = jnp.where(live > 0, pick(v_ref, bases[1], 0, board, group), 0.0)
            new_x = live * jnp.maximum(x - primal * grads[part][inner], 0.0)
            new_v = v + primal * flows[part][inner]
            new_x_ref[place] = new_x
            new_v_ref[place] = new_v
            bar_ref[board] = 2.0 * new_x - x
            if not last:
                total_ref[0:1] += row_sums(new_x * new_x) + row_sums(new_v * new_v)

    for part in range(parts):
        if last:
            pl.when(pl.program_id(0) == part)(functools.partial(work, part))
        else:
            work(part)


def rival_step_kernel(group, start, bases, count, norm_row, parts, last, own_norm_ref, far_norm_ref, bar_ref, far_ref, y_ref,
                      u_ref, new_v_ref, live_ref, row_ref, col_ref, compat_ref, near_ref, main_ref, folds_ref, back_ref,
                      bart_ref, children_ref, parents_ref, *rest):
    flows = rest[:parts]
    rest = rest[parts:]
    at = pl.program_id(0)
    if last:
        new_y_ref, new_u_ref, link_scratch, flow_scratch, step_scratch = rest[-5:]
    else:
        new_y_ref, new_u_ref, total_ref, link_scratch, flow_scratch, step_scratch, plan_scratch = rest[-7:]
    padded = live_ref.shape[2] // 2
    infosets = u_ref.shape[1]
    nx, ny = 2 * infosets, 2 * infosets + 1

    @pl.when(at == 0)
    def _():
        primal, dual = steps_from(own_norm_ref[norm_row:norm_row + 8], far_norm_ref[norm_row:norm_row + 8], count)
        step_scratch[0:1, :] = jnp.broadcast_to(primal, (1, LANES))
        step_scratch[1:2, :] = jnp.broadcast_to(dual, (1, LANES))
        link_scratch[...] = exact_left(river_link(parents_ref, bar_ref.shape[1]), bart_ref[:, :padded])
        if not last:
            plan_scratch[...] = jnp.zeros_like(plan_scratch)
            if start:
                total_ref[...] = rest[0][...]
            else:
                total_ref[...] = jnp.zeros_like(total_ref)
                total_ref[nx:ny + 1] = rest[0][0:2] + rest[1][0:2]

    for part in range(parts):
        @pl.when(at == part)
        def _():
            flow_scratch[...] = flows[part][...]

    primal = step_scratch[0:1, 0:1]
    dual = step_scratch[1:2, 0:1]
    own_plans, far_plans, prices = [], [], []
    for inner in range(group):
        own_plans.append(pick(bar_ref, bases[0], at, inner, group))
        far_plans.append(pick(far_ref, bases[1], at, inner, group))
        prices.append(pick(new_v_ref, bases[4], at, inner, group) + primal * flow_scratch[inner])
    done = group_payoffs(group, start, 1, at, own_plans, far_plans, prices, live_ref, row_ref, col_ref, compat_ref, near_ref,
                         main_ref, folds_ref, back_ref)
    for inner, (gradient, flow) in enumerate(done):
        live = live_ref[start + at * group + inner][:, :padded]
        y = jnp.where(live > 0, pick(y_ref, bases[2], at, inner, group), 0.0)
        u = jnp.where(live > 0, pick(u_ref, bases[3], at, inner, group), 0.0)
        flow = live * flow
        new_y = live * jnp.maximum(y + dual * gradient, 0.0)
        new_u = u + dual * (flow - live * link_scratch[...])
        place = inner if last else at * group + inner
        new_y_ref[place] = new_y
        new_u_ref[place] = new_u
        if not last:
            plan_scratch[...] += new_y
            total_ref[0:infosets] += flow
            total_ref[ny:ny + 1] += row_sums(new_y * new_y) + row_sums(new_u * new_u)

    if not last:
        @pl.when(at == pl.num_programs(0) - 1)
        def _():
            step, _ = river_steps(children_ref, parents_ref)
            total_ref[infosets:2 * infosets] += exact_left(step, plan_scratch[...])


def turn_places(sequences, points):
    return 0, 2 * sequences, sequences, 2 * sequences + round_up(points, 8)


def turn_mix(turn, plan, gather_ref, spread_ref):
    return turn * (exact_right(exact_right(plan, gather_ref[0]), spread_ref[0]) + plan)


def turn_tree(turn_children_ref, turn_parents_ref):
    parents = turn_parents_ref[...].astype(F32)
    return turn_children_ref[...].astype(F32) - parents, 1.0 - jnp.sum(parents, axis=1, keepdims=True)


def turn_start_kernel(first, hand_ref, cards_now_ref, card_ref, gather_ref, spread_ref, *rest):
    if first:
        own_ref, far_ref = rest[:2]
        pack = jnp.concatenate([own_ref[...], far_ref[...]], axis=1)
    else:
        pack_ref, old_bar_ref = rest[:2]
        pack = pack_ref[...]
    turn_fold_ref, turn_children_ref, turn_parents_ref, children_ref, parents_ref = rest[2:7]
    grad_ref, flow_ref, link_ref, extra_ref = rest[7:]
    turn = alive_rows(card_ref[0], cards_now_ref)
    link = river_link(parents_ref, children_ref.shape[1])
    step, root = turn_tree(turn_children_ref, turn_parents_ref)
    fold = turn_fold_ref[...]
    sequences, points = fold.shape[0], step.shape[0]
    _, _, y_at, u_at = turn_places(sequences, points)
    y = pack[y_at:y_at + sequences]
    u = pack[u_at:u_at + points]
    grad_ref[...] = pair_dot(fold, turn_mix(turn, y, gather_ref, spread_ref)) / H + turn * exact_left(step.T, u)
    flow_ref[...] = turn * (exact_left(step, y) - root)
    link_ref[...] = exact_left(link, y)
    extra_ref[...] = pack if first else exact_left(link, old_bar_ref[...])


def turn_step_kernel(count, first, names, hand_ref, cards_now_ref, card_ref, gather_ref, spread_ref, *rest):
    pack_ref, grad_ref, flow_ref, link_ref = rest[:4]
    if first:
        sums_ref, sums_far_ref = rest[4:6]
        rest = rest[6:]
    else:
        bar_link_ref, kept_ref, old_steps_ref, sums_ref, sums_far_ref = rest[4:9]
        rest = rest[9:]
    turn_fold_ref, turn_children_ref, turn_parents_ref, children_ref, parents_ref = rest[:5]
    rest = rest[5:]
    turn = alive_rows(card_ref[0], cards_now_ref)
    link_turned = river_link(parents_ref, children_ref.shape[1]).T
    turn_step, turn_root = turn_tree(turn_children_ref, turn_parents_ref)
    fold = turn_fold_ref[...]
    meetings = (CARDS - 6) * turn
    sequences = fold.shape[0]
    points = turn_step.shape[0]
    starts = turn_places(sequences, points)
    infosets = link_turned.shape[1]
    norm_row = (3 if first else 2) * infosets
    primal, dual = steps_from(sums_ref[norm_row:norm_row + 8], sums_far_ref[norm_row:norm_row + 8], count)
    sums = jnp.concatenate([sums_ref[:norm_row], sums_far_ref[:norm_row]], axis=1)
    pack = pack_ref[...]
    if first:
        price_sum = sums[:infosets]
        kept = sums[infosets:2 * infosets]
        plan_sum = sums[2 * infosets:]
    else:
        price_sum = kept_ref[:infosets] + old_steps_ref[1:2, 0:1] * (sums[:infosets] - meetings * bar_link_ref[...])
        kept = kept_ref[infosets:]
        plan_sum = sums[infosets:]
    x = pack[starts[0]:starts[0] + sequences]
    v = pack[starts[1]:starts[1] + points]
    y = pack[starts[2]:starts[2] + sequences]
    u = pack[starts[3]:starts[3] + points]

    grad = grad_ref[...] - turn * exact_left(link_turned, price_sum)
    new_x = turn * jnp.maximum(x - primal * grad, 0.0)
    new_v = v + primal * flow_ref[...]
    bar = 2.0 * new_x - x
    price_bar = 2.0 * new_v - v
    drift = primal * (plan_sum - meetings * link_ref[...])
    rise = pair_dot(fold.T, turn_mix(turn, bar, gather_ref, spread_ref)) / H - turn * (
        exact_left(turn_step.T, price_bar) - exact_left(link_turned, kept + 2.0 * drift))
    new_y = turn * jnp.maximum(y + dual * rise, 0.0)
    new_u = u + dual * (turn * (exact_left(turn_step, bar) - turn_root))
    if first:
        out_pack_ref, out_kept_ref, bar_ref, out_norms_ref, steps_ref = rest
        steps_ref[0:1] = jnp.broadcast_to(primal, (1, LANES))
        steps_ref[1:2] = jnp.broadcast_to(dual, (1, LANES))
        out_pack_ref[...] = jnp.zeros_like(out_pack_ref)
        for start, value in zip(starts, (new_x, new_v, new_y, new_u)):
            out_pack_ref[start:start + value.shape[0]] = value
        out_kept_ref[:infosets] = price_sum
        out_kept_ref[infosets:] = kept + drift
        bar_ref[...] = bar
        river_name, hand_name = names
        flag = jnp.where((lax.axis_index(river_name) == 0) & (hand_ref[0] == 0), 1.0, 0.0)
        out_norms_ref[...] = jnp.zeros_like(out_norms_ref)
        mover = row_sums(new_x * new_x) + row_sums(new_v * new_v)
        rival = row_sums(new_y * new_y) + row_sums(new_u * new_u)
        half = mover.shape[1] // 2
        out_norms_ref[0:1] = flag * (mover[:, :half] + mover[:, half:])
        out_norms_ref[1:2] = flag * (rival[:, :half] + rival[:, half:])
    else:
        bar_ref = rest[0]
        bar_ref[...] = bar
        for out_ref, value in zip(rest[1:], (new_x, new_v, new_y, new_u)):
            out_ref[...] = value[:, :out_ref.shape[1]]


def whole(shape):
    return pl.BlockSpec(shape, lambda *at: (0,) * len(shape))


def smem():
    return pl.BlockSpec(memory_space=pltpu.SMEM)


def local(hand_rank, loads, turn_cards, turn_children, turn_parents, river_children, river_parents, showdown_pot, river_fold,
          turn_fold, mover_turn, mover_river, mover_turn_price, mover_river_price, rival_turn, rival_river,
          rival_turn_price, rival_river_price):
    slots, sequences, width = mover_river.shape
    infosets = mover_river_price.shape[1]
    turn_sequences = mover_turn.shape[0]
    points = mover_turn_price.shape[0]
    river_count = lax.axis_size("river")
    padded = round_up(width + CARDS + 1, TILE)
    both = 2 * padded
    count = float((turn_sequences + points) * H + river_count * slots * (sequences + infosets) * H)
    group = next(size for size in (3, 2, 1) if slots % size == 0)
    chunks = slots // group
    parts = 2 if chunks % 2 == 0 else 1
    stats_group = STATS_BOARDS if slots % STATS_BOARDS == 0 else group
    span = parts * group
    cards, gather, spread, near = (jnp.asarray(table) for table in halves(width, padded))
    hand = lax.axis_index("hand").astype(jnp.int32).reshape(1)
    pack_rows = 2 * (turn_sequences + round_up(points, 8))
    stat_rows = 3 * infosets + 8
    total_rows = 2 * infosets + 8

    def shape(*dims, dtype=F32):
        return jax.ShapeDtypeStruct(dims, dtype)

    def swap(value):
        return lax.ppermute(value, "hand", [(0, 1), (1, 0)])

    def hop_total(value, hop, gate):
        came = lax.ppermute(value, "river", [(at, at ^ hop) for at in range(river_count)])
        if gate is not None:
            came, _ = lax.optimization_barrier((came, gate))
        return value + came

    def boards(rows, size=group, start=0):
        return pl.BlockSpec((size, rows, padded), lambda at, *_: (at + start, 0, 0))

    vmem = pl.BlockSpec(memory_space=pltpu.VMEM)

    def operand(item, first, size):
        if isinstance(item, list):
            length = slots // len(item)
            return item[first // length], vmem, first % length
        return item, boards(item.shape[1], size, first // size), None

    def call(kernel, name, scalars, steps, in_specs, out_specs, out_shape, scratch, args, micros, aliases=None, vmem=VMEM_BYTES):
        estimate = pl.CostEstimate(flops=int(micros * 1e9), bytes_accessed=0, transcendentals=0)
        return pl.pallas_call(
            kernel,
            grid_spec=pltpu.PrefetchScalarGridSpec(
                num_scalar_prefetch=scalars, grid=steps, in_specs=in_specs, out_specs=out_specs, scratch_shapes=scratch),
            out_shape=out_shape, compiler_params=pltpu.CompilerParams(vmem_limit_bytes=vmem),
            cost_estimate=estimate, input_output_aliases=aliases or {}, name=name,
        )(*args)

    card_block = pl.BlockSpec((1, 8, both), lambda at, ref: (ref[0], 0, 0))
    tree_blocks = [whole(river_children.shape), whole(river_parents.shape)]
    half_block = lambda rows, at_row=0: pl.BlockSpec((rows, padded), lambda at, *_: (at_row, 0))
    operator_sizes = ((2 * sequences + infosets, 4 * sequences), (2 * sequences, 2 * sequences), (sequences, 2 * infosets))
    link_scratch = pltpu.VMEM((infosets, padded), F32)
    flow_scratch = pltpu.VMEM((group, infosets, padded), F32)
    step_scratch = pltpu.VMEM((8, LANES), F32)
    plan_scratch = pltpu.VMEM((sequences, padded), F32)
    any_block = pl.BlockSpec(memory_space=pl.ANY)

    rank_far = swap(hand_rank)
    rival_far = swap(rival_river)

    def stats_kernel_here(hand_ref, *refs):
        stats_kernel(slots, stats_group, "river", *refs)

    def prepare_kernel_here(hand_ref, *refs):
        prepare_kernel(slots, group, "river", *refs)

    sums, pack = call(
        stats_kernel_here, "stats", 1, (slots // stats_group,),
        [smem(), smem(), card_block, half_block(slots), boards(sequences, stats_group), boards(infosets, stats_group),
         boards(sequences, stats_group), boards(infosets, stats_group), half_block(turn_sequences), half_block(points),
         half_block(turn_sequences), half_block(points)] + tree_blocks,
        [whole((stat_rows, padded)), whole((pack_rows, padded))],
        [shape(stat_rows, padded), shape(pack_rows, padded)],
        [pltpu.VMEM((slots, 1, padded), F32), plan_scratch],
        (hand, loads, turn_cards, cards, hand_rank, mover_river, mover_river_price, rival_river, rival_river_price,
         mover_turn, mover_turn_price, rival_turn, rival_turn_price, river_children, river_parents), 5,
        vmem=56 * 2**20)
    gather_block = pl.BlockSpec((1, both, LANES), lambda at, ref: (ref[0], 0, 0))
    spread_block = pl.BlockSpec((1, LANES, both), lambda at, ref: (ref[0], 0, 0))
    prepared = [shape(slots, 1, both), shape(slots, 1, padded, dtype=BF16), shape(slots // group, both, group),
                shape(both, padded, dtype=BF16), shape(LANES, padded, dtype=BF16)] + [shape(2, *size, dtype=BF16) for size in operator_sizes]
    near_block = pl.BlockSpec((1, LANES, padded), lambda at, ref: (ref[0], 0, 0))
    tables = call(
        prepare_kernel_here, "prepare", 1, (1,),
        [smem(), smem(), card_block, gather_block, spread_block, half_block(slots), half_block(slots), near_block,
         whole(showdown_pot.shape), whole(river_fold.shape)] + tree_blocks,
        [vmem] * len(prepared), prepared, [],
        (hand, loads, turn_cards, cards, gather, spread, hand_rank, rank_far, near, showdown_pot, river_fold,
         river_children, river_parents), 2)
    live = tables[0]

    def gradients(value, early, y, y_far, u, pack, beside, stage):
        out = []
        hops = [1 << at for at in range(max(river_count - 1, 1).bit_length())]
        if river_count & (river_count - 1):
            value = lax.psum(value, "river")
            hops = []
        extra = None
        for place in range(max(len(hops), 1)):
            near_now = tables[4]
            if place:
                near_now, _ = lax.optimization_barrier((near_now, value))
            gate = []
            if place == min(stage, len(hops) - 1) or not hops:
                extra = beside(early, value)
                gate.extend(extra)
            while len(out) * group < slots and (len(out) <= place or place >= len(hops) - 1):
                first = len(out) * group
                arrays, specs, bases = zip(*(operand(item, first, group) for item in (y, y_far, u)))
                args = (*arrays, *tables[:4], near_now, *tables[5:], pack, river_parents)
                out.append(call(
                    functools.partial(mover_gradient_kernel, group, first, bases, turn_sequences), "mover_gradient", 0, (1,),
                    [*specs] + [vmem] * (len(args) - 3), [vmem] * 2,
                    [shape(group, sequences, padded), shape(group, infosets, padded)], [], args, group))
                gate.append(out[-1][1])
            if hops:
                value = hop_total(value, hops[place], gate)
                if place == 0:
                    value, early = lax.optimization_barrier((value, early))
        return [item[0] for item in out], [item[1] for item in out], (value, swap(value)), extra

    def mover_steps(last, norms, norm_row, x, v, grad, flow):
        outs = []
        for first in range(0, slots, span):
            arrays, specs, bases = zip(*(operand(item, first, span) for item in (x, v)))
            here = slice(first // group, first // group + parts)
            args = (*norms, *arrays, live, *grad[here], *flow[here])
            in_specs = [vmem] * 2 + [*specs] + [vmem] * (1 + 2 * parts)
            aliases = {}
            if last:
                out_specs = [boards(sequences, group, first // group), boards(infosets, group, first // group), vmem]
                out_shape = [shape(slots, sequences, width), shape(slots, infosets, width), shape(span, sequences, padded)]
                if first:
                    aliases = {len(args): 0, len(args) + 1: 1}
                    in_specs += [any_block] * 2
                    args += tuple(outs[-1][:2])
            else:
                out_specs = [vmem] * 4
                out_shape = [shape(span, sequences, padded), shape(span, infosets, padded),
                             shape(span, sequences, padded), shape(8, padded)]
                if first:
                    in_specs += [vmem]
                    args += (outs[-1][3],)
            outs.append(call(functools.partial(mover_step_kernel, group, first, bases, count, norm_row, parts, last),
                             "mover_step", 0, (parts if last else 1,), in_specs, out_specs, out_shape, [], args, parts, aliases))
        if last:
            return outs[-1][0], outs[-1][1], [item[2] for item in outs]
        return [item[0] for item in outs], [item[1] for item in outs], [item[2] for item in outs], outs[-1][3]

    def rival_steps(last, norms, norm_row, bar, bar_far, y, u, new_v, flow, bar_turn, parts_before):
        outs = []
        for first in range(0, slots, span):
            arrays, specs, bases = zip(*(operand(item, first, group) for item in (bar, bar_far, y, u, new_v)))
            here = slice(first // group, first // group + parts)
            args = (*norms, *arrays, *tables, bar_turn, river_children, river_parents, *flow[here])
            in_specs = [vmem] * 2 + [*specs] + [vmem] * (len(args) - 7)
            aliases = {}
            scratch = [link_scratch, flow_scratch, step_scratch]
            if last:
                out_specs = [boards(sequences, group, first // group), boards(infosets, group, first // group)]
                out_shape = [shape(slots, sequences, width), shape(slots, infosets, width)]
                if first:
                    aliases = {len(args): 0, len(args) + 1: 1}
                    in_specs += [any_block] * 2
                    args += tuple(outs[-1][:2])
            else:
                out_specs = [vmem] * 3
                out_shape = [shape(span, sequences, padded), shape(span, infosets, padded), shape(total_rows, padded)]
                scratch = scratch + [plan_scratch]
                before = (outs[-1][2],) if first else tuple(parts_before)
                in_specs += [vmem] * len(before)
                args += before
            outs.append(call(functools.partial(rival_step_kernel, group, first, bases, count, norm_row, parts, last),
                             "rival_step", 0, (parts,), in_specs, out_specs, out_shape, scratch, args, span, aliases))
        if last:
            return outs[-1]
        return [item[0] for item in outs], [item[1] for item in outs], outs[-1][2]

    turn_blocks = [smem(), card_block, gather_block, spread_block]
    turn_tables = (turn_cards, cards, gather, spread)
    turn_matrices = (turn_fold, turn_children, turn_parents, river_children, river_parents)

    def turn_call(first, data):
        if first:
            out_shape = [shape(pack_rows, both), shape(2 * infosets, both), shape(turn_sequences, both), shape(8, padded),
                         shape(8, LANES)]
        else:
            out_shape = [shape(turn_sequences, both), shape(turn_sequences, width), shape(points, width),
                         shape(turn_sequences, width), shape(points, width)]
        return call(
            functools.partial(turn_step_kernel, count, first, ("river", "hand")), "turn_step", 1, (1,),
            turn_blocks + [vmem] * len(data) + [whole(item.shape) for item in turn_matrices],
            [vmem] * 5 if first else [vmem] + [whole(item.shape) for item in out_shape[1:]],
            out_shape, [], (hand, *turn_tables, *data, *turn_matrices), 2)

    def turn_start(first, data):
        out_shape = [shape(turn_sequences, both), shape(points, both), shape(infosets, both),
                     shape(pack_rows if first else infosets, both)]
        return call(
            functools.partial(turn_start_kernel, first), "turn_start", 1, (1,),
            turn_blocks + [vmem] * 2 + [whole(item.shape) for item in turn_matrices], [vmem] * 4, out_shape, [],
            (hand, *turn_tables, *data, *turn_matrices), 1)

    def first_start(far, value):
        near_now, _ = lax.optimization_barrier((pack, value))
        return turn_start(True, (near_now, far))

    grad, flow, norms, starts = gradients(sums, swap(pack), rival_river, rival_far, rival_river_price, pack, first_start, 2)
    x, v, bar, part = mover_steps(False, norms, 3 * infosets, mover_river, mover_river_price, grad, flow)
    bar_far = [swap(item) for item in bar]
    pack, kept, bar_turn, turn_norms, turn_steps = turn_call(True, (starts[3], *starts[:3], *norms))
    y, u, total = rival_steps(False, norms, 3 * infosets, bar, bar_far, rival_river, rival_river_price, v, flow, bar_turn,
                              (part, turn_norms))
    y_far = [swap(item) for item in y]

    def second_start(far, value):
        now, _ = lax.optimization_barrier((pack, value))
        return turn_start(False, (now, bar_turn))

    grad, flow, norms, starts = gradients(total, y_far[0], y, y_far, u, pack, second_start, 1)
    next_x, next_v, bar = mover_steps(True, norms, 2 * infosets, x, v, grad, flow)
    bar_far = [swap(item) for item in bar]
    bar_turn, next_xt, next_vt, next_yt, next_ut = turn_call(False, (pack, *starts, kept, turn_steps, *norms))
    next_y, next_u = rival_steps(True, norms, 2 * infosets, bar, bar_far, y, u, next_v, flow, bar_turn, None)
    return (next_xt, next_x, next_vt, next_v, next_yt, next_y, next_ut, next_u)


def solution(mesh):
    river = P(("groups", "river"), None, "hand")
    turn = P("groups", "hand")
    placed = (P(("groups", "river"), "hand"), P("groups"), P("groups"), P(), P(), P(), P(), P(), P(), P(),
              turn, river, turn, river, turn, river, turn, river)
    return jax.shard_map(local, mesh=mesh, in_specs=placed,
                         out_specs=(turn, river, turn, river, turn, river, turn, river), check_vma=False)
```

```python
import functools

import jax
import jax.numpy as jnp
import ml_dtypes
import numpy as np
from jax import lax
from jax.experimental import pallas as pl
from jax.experimental.pallas import tpu as pltpu
from jax.sharding import PartitionSpec as P

CARDS = 52
H = 1326
ITERS = 2
STEP_SCALE = 0.25
EPSILON = 1e-06
LANES = 128
TILE = 256
VMEM_BYTES = 20 * 2**20
STATS_BOARDS = 6
F32 = jnp.float32
BF16 = jnp.bfloat16


def round_up(value, unit):
    return -(-value // unit) * unit


def halves(width, padded):
    pairs = np.stack(np.triu_indices(CARDS, 1)).astype(np.int32)
    deck = np.arange(CARDS)
    incidence = (pairs[0][:, None] == deck) | (pairs[1][:, None] == deck)
    parts = pairs.shape[1] // width
    cards = np.full((parts, 8, 2 * padded), -1, np.int32)
    gather = np.zeros((parts, 2 * padded, LANES), np.float32)
    spread = np.zeros((parts, LANES, 2 * padded), np.float32)
    for part in range(parts):
        spread[part, np.arange(CARDS + 1), width + np.arange(CARDS + 1)] = 1.0
        for place, half in enumerate((part, 1 - part)):
            far = slice(half * width, (half + 1) * width)
            rows = slice(place * padded, place * padded + width)
            cards[part, :2, rows] = pairs[:, far]
            gather[part, rows, :CARDS] = incidence[far]
            gather[part, rows, CARDS] = 1.0
            spread[part, :CARDS, rows] = -incidence[far].T.astype(np.float32)
            spread[part, CARDS, rows] = 1.0
    near = np.zeros((parts, LANES, padded), np.float32)
    first = width - (padded - LANES)
    near[:, first:first + CARDS + 1, :width] = spread[:, :CARDS + 1, :width]
    exact = ml_dtypes.bfloat16
    return (cards, gather.astype(exact), spread.astype(exact), near.astype(exact))


def split_two(value):
    high = value.astype(BF16)
    return high, (value - high.astype(F32)).astype(BF16)


def exact_right(value, matrix):
    rows = value.shape[0]
    first = value.astype(BF16)
    rest = value - first.astype(F32)
    second = rest.astype(BF16)
    third = (rest - second.astype(F32)).astype(BF16)
    total = jnp.dot(jnp.concatenate([first, second, third], axis=0), matrix, preferred_element_type=F32)
    return total[:rows] + total[rows:2 * rows] + total[2 * rows:]


def exact_left(matrix, value):
    first = value.astype(BF16)
    rest = value - first.astype(F32)
    second = rest.astype(BF16)
    third = (rest - second.astype(F32)).astype(BF16)
    matrix = matrix.astype(BF16)
    return jnp.dot(jnp.concatenate([matrix] * 3, axis=1), jnp.concatenate([first, second, third], axis=0),
                   preferred_element_type=F32)


def pair_dot(left, right):
    rows = left.shape[0]
    left_high, left_low = split_two(left)
    right_high, right_low = split_two(right)
    total = jnp.dot(
        jnp.concatenate([jnp.concatenate([left_high] * 2, axis=1), jnp.concatenate([left_low] * 2, axis=1)], axis=0),
        jnp.concatenate([right_high, right_low], axis=0), preferred_element_type=F32)
    return total[:rows] + total[rows:]


def alive_rows(card_rows, turn_cards):
    one, two = card_rows[0:1], card_rows[1:2]
    held = one < 0
    for place in range(4):
        card = turn_cards[place]
        held = held | (one == card) | (two == card)
    return jnp.where(held, 0.0, 1.0).astype(F32)


def row_sums(value):
    return jnp.sum(value, axis=0, keepdims=True)


def add_squares(sums_ref, row, squares):
    last = sums_ref.shape[1] - 1
    sums_ref[row:row + 1, last:] += jnp.sum(squares, axis=1, keepdims=True)


def steps_from(own_ref, far_ref, count):
    last = own_ref.shape[1] - 1
    totals = own_ref[0:2, last:] + far_ref[0:2, last:]
    weight = jnp.sqrt((totals[1:2] / count + EPSILON) / (totals[0:1] / count + EPSILON))
    return STEP_SCALE / weight, STEP_SCALE * weight


def river_steps(children_ref, parents_ref):
    sequences = children_ref.shape[1]
    step = (children_ref[...] - parents_ref[:, :sequences]).astype(F32)
    return step, parents_ref[:, sequences:].astype(F32)


def river_link(parents_ref, sequences):
    return parents_ref[:, sequences:].astype(F32)


def stats_kernel(slots, group, river_axis, loads_ref, cards_now_ref, card_ref, rank_ref, x_ref, v_ref, y_ref, u_ref,
                 xt_ref, vt_ref, yt_ref, ut_ref, children_ref, parents_ref,
                 sums_ref, pack_ref, live_scratch, plan_scratch):
    at = pl.program_id(0)
    padded = live_scratch.shape[2]
    prices = v_ref.shape[1]
    river_here = lax.axis_index(river_axis)

    @pl.when(at == 0)
    def _():
        turn = alive_rows(card_ref[0, :, :padded], cards_now_ref)
        slot = lax.broadcasted_iota(jnp.int32, (slots, padded), 0)
        rank = rank_ref[...]
        live = jnp.where((rank >= 0) & (slot < loads_ref[river_here]) & (turn > 0), 1.0, 0.0)
        for board in range(slots):
            live_scratch[board] = live[board:board + 1]
        sums_ref[...] = jnp.zeros_like(sums_ref)
        plan_scratch[...] = jnp.zeros_like(plan_scratch)
        pack_ref[...] = jnp.zeros_like(pack_ref)
        first = jnp.where(river_here == 0, 1.0, 0.0)
        base = 0
        for rows, row in ((xt_ref, 0), (yt_ref, 1), (vt_ref, 0), (ut_ref, 1)):
            value = jnp.where(turn > 0, rows[...], 0.0)
            pack_ref[base:base + value.shape[0]] = value
            base += round_up(value.shape[0], 8)
            add_squares(sums_ref, row, first * row_sums(value * value))

    mover = jnp.zeros((1, padded), F32)
    rival = jnp.zeros((1, padded), F32)
    for inner in range(group):
        live = live_scratch[at * group + inner] > 0
        x = jnp.where(live, x_ref[inner], 0.0)
        v = jnp.where(live, v_ref[inner], 0.0)
        y = jnp.where(live, y_ref[inner], 0.0)
        u = jnp.where(live, u_ref[inner], 0.0)
        mover = mover + row_sums(x * x) + row_sums(v * v)
        rival = rival + row_sums(y * y) + row_sums(u * u)
        sums_ref[0:prices] += u
        sums_ref[prices:2 * prices] += v
        plan_scratch[...] += y
    add_squares(sums_ref, 0, mover)
    add_squares(sums_ref, 1, rival)

    @pl.when(at == pl.num_programs(0) - 1)
    def _():
        step, _ = river_steps(children_ref, parents_ref)
        sums_ref[2 * prices:3 * prices] = exact_left(step, plan_scratch[...])


def prepare_kernel(slots, group, river_axis, loads_ref, cards_now_ref, card_ref, gather_ref, spread_ref, own_ref, far_ref,
                   near_table_ref, pot_ref, fold_ref, children_ref, parents_ref,
                   live_ref, row_ref, col_ref, compat_ref, near_ref, main_ref, folds_ref, back_ref):
    padded = row_ref.shape[2]
    rank = jnp.concatenate([own_ref[...], far_ref[...]], axis=1)
    turn = alive_rows(card_ref[0], cards_now_ref)
    slot = lax.broadcasted_iota(jnp.int32, rank.shape, 0)
    live = jnp.where((rank >= 0) & (slot < loads_ref[lax.axis_index(river_axis)]) & (turn > 0), 1.0, 0.0)
    safe = jnp.where(live > 0, rank, 0)
    code = (128 + (safe & 127)).astype(F32)
    high = safe >> 7
    for bit in range(6):
        code = code * jnp.where((high >> bit) & 1 == 1, float(2.0 ** (1 << bit)), 1.0)
    lane = lax.broadcasted_iota(jnp.int32, rank.shape, 1)
    width = H // 2
    own_code = jnp.where(lane[:, :padded] < width, code[:, :padded], 0.0)
    for board in range(slots):
        live_ref[board] = live[board:board + 1]
        row_ref[board] = own_code[board:board + 1].astype(BF16)
    depth = round_up(slots, 8)
    if depth > slots:
        code = jnp.concatenate([code, jnp.zeros((depth - slots, code.shape[1]), F32)], axis=0)
    turned = code.T
    for place in range(slots // group):
        col_ref[place] = turned[:, place * group:(place + 1) * group]
    free = jnp.dot(gather_ref[0], spread_ref[0][:, :padded], preferred_element_type=F32)
    compat_ref[...] = jnp.maximum(free, 0.0).astype(BF16)
    near_ref[...] = near_table_ref[0]
    for place in range(2):
        set_operators(place == 1, pot_ref, fold_ref, children_ref, parents_ref, main_ref.at[place], folds_ref.at[place],
                      back_ref.at[place])


def set_operators(transposed, pot_ref, fold_ref, children_ref, parents_ref, main_scratch, fold_scratch, back_scratch):
    pot = pot_ref[...] / H
    fold = fold_ref[...] / H
    if transposed:
        pot, fold = -pot.T, fold.T
    step, _ = river_steps(children_ref, parents_ref)
    sequences = pot.shape[0]
    infosets = step.shape[0]
    pot_high, pot_low = split_two(pot)
    fold_high, fold_low = split_two(fold)
    main_scratch[:sequences] = jnp.concatenate([pot_high, pot_high, fold_high, fold_high], axis=1)
    main_scratch[sequences:2 * sequences] = jnp.concatenate([pot_low, pot_low, fold_low, fold_low], axis=1)
    exact = step.astype(BF16)
    main_scratch[2 * sequences:2 * sequences + infosets] = jnp.concatenate(
        [jnp.zeros((infosets, 2 * sequences), BF16), exact, exact], axis=1)
    fold_scratch[:sequences] = jnp.concatenate([fold_high, fold_high], axis=1)
    fold_scratch[sequences:] = jnp.concatenate([fold_low, fold_low], axis=1)
    turned = step.T
    if transposed:
        turned = -turned
    turned = turned.astype(BF16)
    back_scratch[...] = jnp.concatenate([turned, turned], axis=1)


def payoffs(own_plans, far_plans, prices, columns, strengths, compat_ref, near_ref, main, folds, back_step):
    sequences, padded = own_plans[0].shape
    tiles = padded // TILE
    width = H // 2
    depths = [min(TILE, round_up(width - at, 16)) for at in range(0, width, TILE)]
    boards = range(len(own_plans))
    owns = [split_two(plan) for plan in own_plans]
    fars = [split_two(plan) for plan in far_plans]
    price_parts = [split_two(price) for price in prices]
    mixes = []
    for inner in boards:
        left = (jnp.concatenate(owns[inner], axis=0), jnp.concatenate(fars[inner], axis=0))
        row = strengths[inner]
        sums = [None] * tiles
        for place in range(2 * tiles):
            depth = depths[place % tiles]
            rows = slice(place * TILE, place * TILE + depth)
            column = jnp.broadcast_to(columns(rows, inner), (depth, LANES)).astype(BF16)
            column = jnp.concatenate([column, column], axis=1)
            piece = left[place // tiles][:, (place % tiles) * TILE:(place % tiles) * TILE + depth]
            for across in range(tiles):
                lanes = slice(across * TILE, (across + 1) * TILE)
                bound = compat_ref[rows, lanes]
                signs = jnp.minimum(jnp.maximum(column - row[:, lanes], -bound), bound)
                part = jnp.dot(piece, signs, preferred_element_type=F32)
                sums[across] = part if sums[across] is None else sums[across] + part
        mixes.append(split_two(jnp.concatenate([item[:sequences] + item[sequences:] for item in sums], axis=1)))
    cards = []
    for inner in boards:
        tail = jnp.concatenate([item[:, padded - LANES:] for item in mixes[inner]], axis=0)
        folded = jnp.dot(folds, tail, preferred_element_type=F32)
        cards.extend(split_two(folded[:sequences] + folded[sequences:]))
    backs = [jnp.dot(back_step, jnp.concatenate(price_parts[inner], axis=0), preferred_element_type=F32) for inner in boards]
    products = [jnp.dot(main, jnp.concatenate(mixes[inner] + owns[inner], axis=0), preferred_element_type=F32)
                for inner in boards]
    nearby = jnp.dot(jnp.concatenate(cards, axis=0), near_ref[...], preferred_element_type=F32)
    done = []
    for inner in boards:
        base = 2 * inner * sequences
        close = nearby[base:base + sequences] + nearby[base + sequences:base + 2 * sequences]
        product = products[inner]
        done.append((product[:sequences] + product[sequences:2 * sequences] + backs[inner] + close, product[2 * sequences:]))
    return done


def pick(ref, base, at, inner, group):
    return ref[inner] if base is None else ref[base + at * group + inner]


def group_payoffs(group, start, side, at, plans, fars, prices, live_ref, row_ref, col_ref, compat_ref, near_ref,
                  main_ref, folds_ref, back_ref):
    strengths = [row_ref[start + at * group + inner] for inner in range(group)]

    def columns(rows, inner):
        return col_ref[start // group + at, rows, inner:inner + 1]

    return payoffs(plans, fars, prices, columns, strengths, compat_ref, near_ref, main_ref[side], folds_ref[side],
                   back_ref[side])


def mover_gradient_kernel(group, start, bases, turn_row, y_ref, far_ref, u_ref, live_ref, row_ref, col_ref, compat_ref,
                          near_ref, main_ref, folds_ref, back_ref, pack_ref, parents_ref, grad_ref, flow_ref):
    _, sequences, padded = grad_ref.shape
    link = river_link(parents_ref, sequences)
    turn_flow = exact_left(link, pack_ref[turn_row:turn_row + link.shape[1], :padded])
    own_plans, far_plans, prices, lives = [], [], [], []
    for inner in range(group):
        live = live_ref[start + inner]
        near_live = live[:, :padded]
        lives.append(near_live)
        own_plans.append(jnp.where(near_live > 0, pick(y_ref, bases[0], 0, inner, group), 0.0))
        far_plans.append(jnp.where(live[:, padded:] > 0, pick(far_ref, bases[1], 0, inner, group), 0.0))
        prices.append(jnp.where(near_live > 0, pick(u_ref, bases[2], 0, inner, group), 0.0))
    done = group_payoffs(group, start, 0, 0, own_plans, far_plans, prices, live_ref, row_ref, col_ref, compat_ref, near_ref,
                         main_ref, folds_ref, back_ref)
    for inner, (gradient, flow) in enumerate(done):
        grad_ref[inner] = gradient
        flow_ref[inner] = lives[inner] * (flow - turn_flow)


def mover_step_kernel(group, start, bases, count, parts, last, own_norm_ref, far_norm_ref, x_ref, v_ref, live_ref,
                      *rest):
    grads, flows = rest[:parts], rest[parts:2 * parts]
    if last:
        new_x_ref, new_v_ref, bar_ref = rest[-3:]
    else:
        new_x_ref, new_v_ref, bar_ref, total_ref = rest[-4:]
        total_ref[...] = rest[2 * parts][...] if start else jnp.zeros_like(total_ref)
    padded = bar_ref.shape[2]
    primal, _ = steps_from(own_norm_ref, far_norm_ref, count)

    def work(part):
        for inner in range(group):
            board = part * group + inner
            place = inner if last else board
            live = live_ref[start + board][:, :padded]
            x = jnp.where(live > 0, pick(x_ref, bases[0], 0, board, group), 0.0)
            v = jnp.where(live > 0, pick(v_ref, bases[1], 0, board, group), 0.0)
            new_x = live * jnp.maximum(x - primal * grads[part][inner], 0.0)
            new_v = v + primal * flows[part][inner]
            new_x_ref[place] = new_x
            new_v_ref[place] = new_v
            bar_ref[board] = 2.0 * new_x - x
            if not last:
                total_ref[0:1] += row_sums(new_x * new_x) + row_sums(new_v * new_v)

    for part in range(parts):
        if last:
            pl.when(pl.program_id(0) == part)(functools.partial(work, part))
        else:
            work(part)


def rival_step_kernel(group, start, bases, count, parts, last, own_norm_ref, far_norm_ref, bar_ref, far_ref, y_ref,
                      u_ref, new_v_ref, live_ref, row_ref, col_ref, compat_ref, near_ref, main_ref, folds_ref, back_ref,
                      bart_ref, children_ref, parents_ref, *rest):
    flows = rest[:parts]
    rest = rest[parts:]
    at = pl.program_id(0)
    if last:
        new_y_ref, new_u_ref, link_scratch, flow_scratch, step_scratch = rest[-5:]
    else:
        new_y_ref, new_u_ref, total_ref, link_scratch, flow_scratch, step_scratch, plan_scratch = rest[-7:]
    padded = live_ref.shape[2] // 2
    infosets = u_ref.shape[1]
    @pl.when(at == 0)
    def _():
        primal, dual = steps_from(own_norm_ref, far_norm_ref, count)
        step_scratch[0:1, :] = jnp.broadcast_to(primal, (1, LANES))
        step_scratch[1:2, :] = jnp.broadcast_to(dual, (1, LANES))
        link_scratch[...] = exact_left(river_link(parents_ref, bar_ref.shape[1]), bart_ref[:, :padded])
        if not last:
            plan_scratch[...] = jnp.zeros_like(plan_scratch)
            if start:
                total_ref[...] = rest[0][...]
            else:
                total_ref[...] = jnp.zeros_like(total_ref)
                for row in range(2):
                    add_squares(total_ref, row, rest[0][row:row + 1] + rest[1][row:row + 1])

    for part in range(parts):
        @pl.when(at == part)
        def _():
            flow_scratch[...] = flows[part][...]

    primal = step_scratch[0:1, 0:1]
    dual = step_scratch[1:2, 0:1]
    own_plans, far_plans, prices = [], [], []
    for inner in range(group):
        own_plans.append(pick(bar_ref, bases[0], at, inner, group))
        far_plans.append(pick(far_ref, bases[1], at, inner, group))
        prices.append(pick(new_v_ref, bases[4], at, inner, group) + primal * flow_scratch[inner])
    done = group_payoffs(group, start, 1, at, own_plans, far_plans, prices, live_ref, row_ref, col_ref, compat_ref, near_ref,
                         main_ref, folds_ref, back_ref)
    squares = jnp.zeros((1, padded), F32)
    for inner, (gradient, flow) in enumerate(done):
        live = live_ref[start + at * group + inner][:, :padded]
        y = jnp.where(live > 0, pick(y_ref, bases[2], at, inner, group), 0.0)
        u = jnp.where(live > 0, pick(u_ref, bases[3], at, inner, group), 0.0)
        flow = live * flow
        new_y = live * jnp.maximum(y + dual * gradient, 0.0)
        new_u = u + dual * (flow - live * link_scratch[...])
        place = inner if last else at * group + inner
        new_y_ref[place] = new_y
        new_u_ref[place] = new_u
        if not last:
            plan_scratch[...] += new_y
            total_ref[0:infosets] += flow
            squares = squares + row_sums(new_y * new_y) + row_sums(new_u * new_u)

    if not last:
        add_squares(total_ref, 1, squares)

        @pl.when(at == pl.num_programs(0) - 1)
        def _():
            step, _ = river_steps(children_ref, parents_ref)
            total_ref[infosets:2 * infosets] += exact_left(step, plan_scratch[...])


def turn_places(sequences, points):
    return 0, 2 * sequences, sequences, 2 * sequences + round_up(points, 8)


def turn_mix(turn, plan, gather_ref, spread_ref):
    return turn * (exact_right(exact_right(plan, gather_ref[0]), spread_ref[0]) + plan)


def turn_tree(turn_children_ref, turn_parents_ref):
    parents = turn_parents_ref[...].astype(F32)
    return turn_children_ref[...].astype(F32) - parents, 1.0 - jnp.sum(parents, axis=1, keepdims=True)


def turn_start_kernel(first, hand_ref, cards_now_ref, card_ref, gather_ref, spread_ref, *rest):
    if first:
        own_ref, far_ref = rest[:2]
        pack = jnp.concatenate([own_ref[...], far_ref[...]], axis=1)
    else:
        pack_ref, old_bar_ref = rest[:2]
        pack = pack_ref[...]
    turn_fold_ref, turn_children_ref, turn_parents_ref, children_ref, parents_ref = rest[2:7]
    grad_ref, flow_ref, link_ref, extra_ref = rest[7:]
    turn = alive_rows(card_ref[0], cards_now_ref)
    link = river_link(parents_ref, children_ref.shape[1])
    step, root = turn_tree(turn_children_ref, turn_parents_ref)
    fold = turn_fold_ref[...]
    sequences, points = fold.shape[0], step.shape[0]
    _, _, y_at, u_at = turn_places(sequences, points)
    y = pack[y_at:y_at + sequences]
    u = pack[u_at:u_at + points]
    grad_ref[...] = pair_dot(fold, turn_mix(turn, y, gather_ref, spread_ref)) / H + turn * exact_left(step.T, u)
    flow_ref[...] = turn * (exact_left(step, y) - root)
    link_ref[...] = exact_left(link, y)
    extra_ref[...] = pack if first else exact_left(link, old_bar_ref[...])


def turn_step_kernel(count, first, names, hand_ref, cards_now_ref, card_ref, gather_ref, spread_ref, *rest):
    pack_ref, grad_ref, flow_ref, link_ref = rest[:4]
    if first:
        sums_ref, sums_far_ref = rest[4:6]
        rest = rest[6:]
    else:
        bar_link_ref, kept_ref, old_steps_ref, sums_ref, sums_far_ref = rest[4:9]
        rest = rest[9:]
    turn_fold_ref, turn_children_ref, turn_parents_ref, children_ref, parents_ref = rest[:5]
    rest = rest[5:]
    turn = alive_rows(card_ref[0], cards_now_ref)
    link_turned = river_link(parents_ref, children_ref.shape[1]).T
    turn_step, turn_root = turn_tree(turn_children_ref, turn_parents_ref)
    fold = turn_fold_ref[...]
    meetings = (CARDS - 6) * turn
    sequences = fold.shape[0]
    points = turn_step.shape[0]
    starts = turn_places(sequences, points)
    infosets = link_turned.shape[1]
    primal, dual = steps_from(sums_ref, sums_far_ref, count)
    sums = jnp.concatenate([sums_ref[...], sums_far_ref[...]], axis=1)
    pack = pack_ref[...]
    if first:
        price_sum = sums[:infosets]
        kept = sums[infosets:2 * infosets]
        plan_sum = sums[2 * infosets:]
    else:
        price_sum = kept_ref[:infosets] + old_steps_ref[1:2, 0:1] * (sums[:infosets] - meetings * bar_link_ref[...])
        kept = kept_ref[infosets:]
        plan_sum = sums[infosets:]
    x = pack[starts[0]:starts[0] + sequences]
    v = pack[starts[1]:starts[1] + points]
    y = pack[starts[2]:starts[2] + sequences]
    u = pack[starts[3]:starts[3] + points]

    grad = grad_ref[...] - turn * exact_left(link_turned, price_sum)
    new_x = turn * jnp.maximum(x - primal * grad, 0.0)
    new_v = v + primal * flow_ref[...]
    bar = 2.0 * new_x - x
    price_bar = 2.0 * new_v - v
    drift = primal * (plan_sum - meetings * link_ref[...])
    rise = pair_dot(fold.T, turn_mix(turn, bar, gather_ref, spread_ref)) / H - turn * (
        exact_left(turn_step.T, price_bar) - exact_left(link_turned, kept + 2.0 * drift))
    new_y = turn * jnp.maximum(y + dual * rise, 0.0)
    new_u = u + dual * (turn * (exact_left(turn_step, bar) - turn_root))
    if first:
        out_pack_ref, out_kept_ref, bar_ref, out_norms_ref, steps_ref = rest
        steps_ref[0:1] = jnp.broadcast_to(primal, (1, LANES))
        steps_ref[1:2] = jnp.broadcast_to(dual, (1, LANES))
        out_pack_ref[...] = jnp.zeros_like(out_pack_ref)
        for start, value in zip(starts, (new_x, new_v, new_y, new_u)):
            out_pack_ref[start:start + value.shape[0]] = value
        out_kept_ref[:infosets] = price_sum
        out_kept_ref[infosets:] = kept + drift
        bar_ref[...] = bar
        river_name, hand_name = names
        flag = jnp.where((lax.axis_index(river_name) == 0) & (hand_ref[0] == 0), 1.0, 0.0)
        out_norms_ref[...] = jnp.zeros_like(out_norms_ref)
        mover = row_sums(new_x * new_x) + row_sums(new_v * new_v)
        rival = row_sums(new_y * new_y) + row_sums(new_u * new_u)
        half = mover.shape[1] // 2
        out_norms_ref[0:1] = flag * (mover[:, :half] + mover[:, half:])
        out_norms_ref[1:2] = flag * (rival[:, :half] + rival[:, half:])
    else:
        bar_ref = rest[0]
        bar_ref[...] = bar
        for out_ref, value in zip(rest[1:], (new_x, new_v, new_y, new_u)):
            out_ref[...] = value[:, :out_ref.shape[1]]


def whole(shape):
    return pl.BlockSpec(shape, lambda *at: (0,) * len(shape))


def smem():
    return pl.BlockSpec(memory_space=pltpu.SMEM)


def local(hand_rank, loads, turn_cards, turn_children, turn_parents, river_children, river_parents, showdown_pot, river_fold,
          turn_fold, mover_turn, mover_river, mover_turn_price, mover_river_price, rival_turn, rival_river,
          rival_turn_price, rival_river_price):
    slots, sequences, width = mover_river.shape
    infosets = mover_river_price.shape[1]
    turn_sequences = mover_turn.shape[0]
    points = mover_turn_price.shape[0]
    river_count = lax.axis_size("river")
    padded = round_up(width + CARDS + 1, TILE)
    both = 2 * padded
    count = float((turn_sequences + points) * H + river_count * slots * (sequences + infosets) * H)
    group = next(size for size in (3, 2, 1) if slots % size == 0)
    chunks = slots // group
    parts = 2 if chunks % 2 == 0 else 1
    stats_group = STATS_BOARDS if slots % STATS_BOARDS == 0 else group
    span = parts * group
    cards, gather, spread, near = (jnp.asarray(table) for table in halves(width, padded))
    hand = lax.axis_index("hand").astype(jnp.int32).reshape(1)
    pack_rows = 2 * (turn_sequences + round_up(points, 8))
    stat_rows = 3 * infosets
    total_rows = 2 * infosets

    def shape(*dims, dtype=F32):
        return jax.ShapeDtypeStruct(dims, dtype)

    def swap(value):
        return lax.ppermute(value, "hand", [(0, 1), (1, 0)])

    def hop_total(value, hop, gate):
        came = lax.ppermute(value, "river", [(at, at ^ hop) for at in range(river_count)])
        if gate is not None:
            came, _ = lax.optimization_barrier((came, gate))
        return value + came

    def boards(rows, size=group, start=0):
        return pl.BlockSpec((size, rows, padded), lambda at, *_: (at + start, 0, 0))

    vmem = pl.BlockSpec(memory_space=pltpu.VMEM)

    def operand(item, first, size):
        if isinstance(item, list):
            length = slots // len(item)
            return item[first // length], vmem, first % length
        return item, boards(item.shape[1], size, first // size), None

    def call(kernel, name, scalars, steps, in_specs, out_specs, out_shape, scratch, args, micros, aliases=None, vmem=VMEM_BYTES):
        estimate = pl.CostEstimate(flops=int(micros * 1e9), bytes_accessed=0, transcendentals=0)
        return pl.pallas_call(
            kernel,
            grid_spec=pltpu.PrefetchScalarGridSpec(
                num_scalar_prefetch=scalars, grid=steps, in_specs=in_specs, out_specs=out_specs, scratch_shapes=scratch),
            out_shape=out_shape, compiler_params=pltpu.CompilerParams(vmem_limit_bytes=vmem),
            cost_estimate=estimate, input_output_aliases=aliases or {}, name=name,
        )(*args)

    card_block = pl.BlockSpec((1, 8, both), lambda at, ref: (ref[0], 0, 0))
    tree_blocks = [whole(river_children.shape), whole(river_parents.shape)]
    half_block = lambda rows, at_row=0: pl.BlockSpec((rows, padded), lambda at, *_: (at_row, 0))
    operator_sizes = ((2 * sequences + infosets, 4 * sequences), (2 * sequences, 2 * sequences), (sequences, 2 * infosets))
    link_scratch = pltpu.VMEM((infosets, padded), F32)
    flow_scratch = pltpu.VMEM((group, infosets, padded), F32)
    step_scratch = pltpu.VMEM((8, LANES), F32)
    plan_scratch = pltpu.VMEM((sequences, padded), F32)
    any_block = pl.BlockSpec(memory_space=pl.ANY)

    rank_far = swap(hand_rank)
    rival_far = swap(rival_river)

    def stats_kernel_here(hand_ref, *refs):
        stats_kernel(slots, stats_group, "river", *refs)

    def prepare_kernel_here(hand_ref, *refs):
        prepare_kernel(slots, group, "river", *refs)

    sums, pack = call(
        stats_kernel_here, "stats", 1, (slots // stats_group,),
        [smem(), smem(), card_block, half_block(slots), boards(sequences, stats_group), boards(infosets, stats_group),
         boards(sequences, stats_group), boards(infosets, stats_group), half_block(turn_sequences), half_block(points),
         half_block(turn_sequences), half_block(points)] + tree_blocks,
        [whole((stat_rows, padded)), whole((pack_rows, padded))],
        [shape(stat_rows, padded), shape(pack_rows, padded)],
        [pltpu.VMEM((slots, 1, padded), F32), plan_scratch],
        (hand, loads, turn_cards, cards, hand_rank, mover_river, mover_river_price, rival_river, rival_river_price,
         mover_turn, mover_turn_price, rival_turn, rival_turn_price, river_children, river_parents), 5,
        vmem=56 * 2**20)
    gather_block = pl.BlockSpec((1, both, LANES), lambda at, ref: (ref[0], 0, 0))
    spread_block = pl.BlockSpec((1, LANES, both), lambda at, ref: (ref[0], 0, 0))
    prepared = [shape(slots, 1, both), shape(slots, 1, padded, dtype=BF16), shape(slots // group, both, group),
                shape(both, padded, dtype=BF16), shape(LANES, padded, dtype=BF16)] + [shape(2, *size, dtype=BF16) for size in operator_sizes]
    near_block = pl.BlockSpec((1, LANES, padded), lambda at, ref: (ref[0], 0, 0))
    tables = call(
        prepare_kernel_here, "prepare", 1, (1,),
        [smem(), smem(), card_block, gather_block, spread_block, half_block(slots), half_block(slots), near_block,
         whole(showdown_pot.shape), whole(river_fold.shape)] + tree_blocks,
        [vmem] * len(prepared), prepared, [],
        (hand, loads, turn_cards, cards, gather, spread, hand_rank, rank_far, near, showdown_pot, river_fold,
         river_children, river_parents), 2)
    live = tables[0]

    def gradients(value, early, y, y_far, u, pack, beside, stage):
        out = []
        hops = [1 << at for at in range(max(river_count - 1, 1).bit_length())]
        if river_count & (river_count - 1):
            value = lax.psum(value, "river")
            hops = []
        extra = None
        for place in range(max(len(hops), 1)):
            near_now = tables[4]
            if place:
                near_now, _ = lax.optimization_barrier((near_now, value))
            gate = []
            if place == min(stage, len(hops) - 1) or not hops:
                extra = beside(early, value)
                gate.extend(extra)
            while len(out) * group < slots and (len(out) <= place or place >= len(hops) - 1):
                first = len(out) * group
                arrays, specs, bases = zip(*(operand(item, first, group) for item in (y, y_far, u)))
                args = (*arrays, *tables[:4], near_now, *tables[5:], pack, river_parents)
                out.append(call(
                    functools.partial(mover_gradient_kernel, group, first, bases, turn_sequences), "mover_gradient", 0, (1,),
                    [*specs] + [vmem] * (len(args) - 3), [vmem] * 2,
                    [shape(group, sequences, padded), shape(group, infosets, padded)], [], args, group))
                gate.append(out[-1][1])
            if hops:
                value = hop_total(value, hops[place], gate)
                if place == 0:
                    value, early = lax.optimization_barrier((value, early))
        return [item[0] for item in out], [item[1] for item in out], (value, swap(value)), extra

    def mover_steps(last, norms, x, v, grad, flow):
        outs = []
        for first in range(0, slots, span):
            arrays, specs, bases = zip(*(operand(item, first, span) for item in (x, v)))
            here = slice(first // group, first // group + parts)
            args = (*norms, *arrays, live, *grad[here], *flow[here])
            in_specs = [vmem] * 2 + [*specs] + [vmem] * (1 + 2 * parts)
            aliases = {}
            if last:
                out_specs = [boards(sequences, group, first // group), boards(infosets, group, first // group), vmem]
                out_shape = [shape(slots, sequences, width), shape(slots, infosets, width), shape(span, sequences, padded)]
                if first:
                    aliases = {len(args): 0, len(args) + 1: 1}
                    in_specs += [any_block] * 2
                    args += tuple(outs[-1][:2])
            else:
                out_specs = [vmem] * 4
                out_shape = [shape(span, sequences, padded), shape(span, infosets, padded),
                             shape(span, sequences, padded), shape(8, padded)]
                if first:
                    in_specs += [vmem]
                    args += (outs[-1][3],)
            outs.append(call(functools.partial(mover_step_kernel, group, first, bases, count, parts, last),
                             "mover_step", 0, (parts if last else 1,), in_specs, out_specs, out_shape, [], args, parts, aliases))
        if last:
            return outs[-1][0], outs[-1][1], [item[2] for item in outs]
        return [item[0] for item in outs], [item[1] for item in outs], [item[2] for item in outs], outs[-1][3]

    def rival_steps(last, norms, bar, bar_far, y, u, new_v, flow, bar_turn, parts_before):
        outs = []
        for first in range(0, slots, span):
            arrays, specs, bases = zip(*(operand(item, first, group) for item in (bar, bar_far, y, u, new_v)))
            here = slice(first // group, first // group + parts)
            args = (*norms, *arrays, *tables, bar_turn, river_children, river_parents, *flow[here])
            in_specs = [vmem] * 2 + [*specs] + [vmem] * (len(args) - 7)
            aliases = {}
            scratch = [link_scratch, flow_scratch, step_scratch]
            if last:
                out_specs = [boards(sequences, group, first // group), boards(infosets, group, first // group)]
                out_shape = [shape(slots, sequences, width), shape(slots, infosets, width)]
                if first:
                    aliases = {len(args): 0, len(args) + 1: 1}
                    in_specs += [any_block] * 2
                    args += tuple(outs[-1][:2])
            else:
                out_specs = [vmem] * 3
                out_shape = [shape(span, sequences, padded), shape(span, infosets, padded), shape(total_rows, padded)]
                scratch = scratch + [plan_scratch]
                before = (outs[-1][2],) if first else tuple(parts_before)
                in_specs += [vmem] * len(before)
                args += before
            outs.append(call(functools.partial(rival_step_kernel, group, first, bases, count, parts, last),
                             "rival_step", 0, (parts,), in_specs, out_specs, out_shape, scratch, args, span, aliases))
        if last:
            return outs[-1]
        return [item[0] for item in outs], [item[1] for item in outs], outs[-1][2]

    turn_blocks = [smem(), card_block, gather_block, spread_block]
    turn_tables = (turn_cards, cards, gather, spread)
    turn_matrices = (turn_fold, turn_children, turn_parents, river_children, river_parents)

    def turn_call(first, data):
        if first:
            out_shape = [shape(pack_rows, both), shape(2 * infosets, both), shape(turn_sequences, both), shape(8, padded),
                         shape(8, LANES)]
        else:
            out_shape = [shape(turn_sequences, both), shape(turn_sequences, width), shape(points, width),
                         shape(turn_sequences, width), shape(points, width)]
        return call(
            functools.partial(turn_step_kernel, count, first, ("river", "hand")), "turn_step", 1, (1,),
            turn_blocks + [vmem] * len(data) + [whole(item.shape) for item in turn_matrices],
            [vmem] * 5 if first else [vmem] + [whole(item.shape) for item in out_shape[1:]],
            out_shape, [], (hand, *turn_tables, *data, *turn_matrices), 2)

    def turn_start(first, data):
        out_shape = [shape(turn_sequences, both), shape(points, both), shape(infosets, both),
                     shape(pack_rows if first else infosets, both)]
        return call(
            functools.partial(turn_start_kernel, first), "turn_start", 1, (1,),
            turn_blocks + [vmem] * 2 + [whole(item.shape) for item in turn_matrices], [vmem] * 4, out_shape, [],
            (hand, *turn_tables, *data, *turn_matrices), 1)

    def first_start(far, value):
        near_now, _ = lax.optimization_barrier((pack, value))
        return turn_start(True, (near_now, far))

    grad, flow, norms, starts = gradients(sums, swap(pack), rival_river, rival_far, rival_river_price, pack, first_start, 2)
    x, v, bar, part = mover_steps(False, norms, mover_river, mover_river_price, grad, flow)
    bar_far = [swap(item) for item in bar]
    pack, kept, bar_turn, turn_norms, turn_steps = turn_call(True, (starts[3], *starts[:3], *norms))
    y, u, total = rival_steps(False, norms, bar, bar_far, rival_river, rival_river_price, v, flow, bar_turn,
                              (part, turn_norms))
    y_far = [swap(item) for item in y]

    def second_start(far, value):
        now, _ = lax.optimization_barrier((pack, value))
        return turn_start(False, (now, bar_turn))

    grad, flow, norms, starts = gradients(total, y_far[0], y, y_far, u, pack, second_start, 1)
    next_x, next_v, bar = mover_steps(True, norms, x, v, grad, flow)
    bar_far = [swap(item) for item in bar]
    bar_turn, next_xt, next_vt, next_yt, next_ut = turn_call(False, (pack, *starts, kept, turn_steps, *norms))
    next_y, next_u = rival_steps(True, norms, bar, bar_far, y, u, next_v, flow, bar_turn, None)
    return (next_xt, next_x, next_vt, next_v, next_yt, next_y, next_ut, next_u)


def solution(mesh):
    river = P(("groups", "river"), None, "hand")
    turn = P("groups", "hand")
    placed = (P(("groups", "river"), "hand"), P("groups"), P("groups"), P(), P(), P(), P(), P(), P(), P(),
              turn, river, turn, river, turn, river, turn, river)
    return jax.shard_map(local, mesh=mesh, in_specs=placed,
                         out_specs=(turn, river, turn, river, turn, river, turn, river), check_vma=False)
```

```python
import functools

import jax
import jax.numpy as jnp
import ml_dtypes
import numpy as np
from jax import lax
from jax.experimental import pallas as pl
from jax.experimental.pallas import tpu as pltpu
from jax.sharding import PartitionSpec as P

CARDS = 52
H = 1326
ITERS = 2
STEP_SCALE = 0.25
EPSILON = 1e-06
LANES = 128
TILE = 256
VMEM_BYTES = 20 * 2**20
STATS_BOARDS = 6
F32 = jnp.float32
BF16 = jnp.bfloat16


def round_up(value, unit):
    return -(-value // unit) * unit


def halves(width, padded):
    pairs = np.stack(np.triu_indices(CARDS, 1)).astype(np.int32)
    deck = np.arange(CARDS)
    incidence = (pairs[0][:, None] == deck) | (pairs[1][:, None] == deck)
    parts = pairs.shape[1] // width
    cards = np.full((parts, 8, 2 * padded), -1, np.int32)
    gather = np.zeros((parts, 2 * padded, LANES), np.float32)
    spread = np.zeros((parts, LANES, 2 * padded), np.float32)
    for part in range(parts):
        spread[part, np.arange(CARDS + 1), width + np.arange(CARDS + 1)] = 1.0
        for place, half in enumerate((part, 1 - part)):
            far = slice(half * width, (half + 1) * width)
            rows = slice(place * padded, place * padded + width)
            cards[part, :2, rows] = pairs[:, far]
            gather[part, rows, :CARDS] = incidence[far]
            gather[part, rows, CARDS] = 1.0
            spread[part, :CARDS, rows] = -incidence[far].T.astype(np.float32)
            spread[part, CARDS, rows] = 1.0
    near = np.zeros((parts, LANES, padded), np.float32)
    first = width - (padded - LANES)
    near[:, first:first + CARDS + 1, :width] = spread[:, :CARDS + 1, :width]
    exact = ml_dtypes.bfloat16
    return (cards, gather.astype(exact), spread.astype(exact), near.astype(exact))


def split_two(value):
    high = value.astype(BF16)
    return high, (value - high.astype(F32)).astype(BF16)


def exact_right(value, matrix):
    rows = value.shape[0]
    first = value.astype(BF16)
    rest = value - first.astype(F32)
    second = rest.astype(BF16)
    third = (rest - second.astype(F32)).astype(BF16)
    total = jnp.dot(jnp.concatenate([first, second, third], axis=0), matrix, preferred_element_type=F32)
    return total[:rows] + total[rows:2 * rows] + total[2 * rows:]


def exact_left(matrix, value):
    first = value.astype(BF16)
    rest = value - first.astype(F32)
    second = rest.astype(BF16)
    third = (rest - second.astype(F32)).astype(BF16)
    matrix = matrix.astype(BF16)
    return jnp.dot(jnp.concatenate([matrix] * 3, axis=1), jnp.concatenate([first, second, third], axis=0),
                   preferred_element_type=F32)


def pair_dot(left, right):
    rows = left.shape[0]
    left_high, left_low = split_two(left)
    right_high, right_low = split_two(right)
    total = jnp.dot(
        jnp.concatenate([jnp.concatenate([left_high] * 2, axis=1), jnp.concatenate([left_low] * 2, axis=1)], axis=0),
        jnp.concatenate([right_high, right_low], axis=0), preferred_element_type=F32)
    return total[:rows] + total[rows:]


def alive_rows(card_rows, turn_cards):
    one, two = card_rows[0:1], card_rows[1:2]
    held = one < 0
    for place in range(4):
        card = turn_cards[place]
        held = held | (one == card) | (two == card)
    return jnp.where(held, 0.0, 1.0).astype(F32)


def row_sums(value):
    return jnp.sum(value, axis=0, keepdims=True)


def add_squares(sums_ref, row, squares):
    last = sums_ref.shape[1] - 1
    sums_ref[row:row + 1, last:] += jnp.sum(squares, axis=1, keepdims=True)


def steps_from(own_ref, far_ref, count):
    last = own_ref.shape[1] - 1
    totals = own_ref[0:2, last:] + far_ref[0:2, last:]
    weight = jnp.sqrt((totals[1:2] / count + EPSILON) / (totals[0:1] / count + EPSILON))
    return STEP_SCALE / weight, STEP_SCALE * weight


def river_steps(children_ref, parents_ref):
    sequences = children_ref.shape[1]
    step = (children_ref[...] - parents_ref[:, :sequences]).astype(F32)
    return step, parents_ref[:, sequences:].astype(F32)


def river_link(parents_ref, sequences):
    return parents_ref[:, sequences:].astype(F32)


def stats_kernel(slots, group, river_axis, loads_ref, cards_now_ref, card_ref, rank_ref, x_ref, v_ref, y_ref, u_ref,
                 xt_ref, vt_ref, yt_ref, ut_ref, children_ref, parents_ref,
                 sums_ref, pack_ref, live_scratch, plan_scratch):
    at = pl.program_id(0)
    padded = live_scratch.shape[2]
    prices = v_ref.shape[1]
    river_here = lax.axis_index(river_axis)

    @pl.when(at == 0)
    def _():
        turn = alive_rows(card_ref[0, :, :padded], cards_now_ref)
        slot = lax.broadcasted_iota(jnp.int32, (slots, padded), 0)
        rank = rank_ref[...]
        live = jnp.where((rank >= 0) & (slot < loads_ref[river_here]) & (turn > 0), 1.0, 0.0)
        for board in range(slots):
            live_scratch[board] = live[board:board + 1]
        sums_ref[...] = jnp.zeros_like(sums_ref)
        plan_scratch[...] = jnp.zeros_like(plan_scratch)
        pack_ref[...] = jnp.zeros_like(pack_ref)
        first = jnp.where(river_here == 0, 1.0, 0.0)
        base = 0
        for rows, row in ((xt_ref, 0), (yt_ref, 1), (vt_ref, 0), (ut_ref, 1)):
            value = jnp.where(turn > 0, rows[...], 0.0)
            pack_ref[base:base + value.shape[0]] = value
            base += round_up(value.shape[0], 8)
            add_squares(sums_ref, row, first * row_sums(value * value))

    mover = jnp.zeros((1, padded), F32)
    rival = jnp.zeros((1, padded), F32)
    for inner in range(group):
        live = live_scratch[at * group + inner] > 0
        x = jnp.where(live, x_ref[inner], 0.0)
        v = jnp.where(live, v_ref[inner], 0.0)
        y = jnp.where(live, y_ref[inner], 0.0)
        u = jnp.where(live, u_ref[inner], 0.0)
        mover = mover + row_sums(x * x) + row_sums(v * v)
        rival = rival + row_sums(y * y) + row_sums(u * u)
        sums_ref[0:prices] += u
        sums_ref[prices:2 * prices] += v
        plan_scratch[...] += y
    add_squares(sums_ref, 0, mover)
    add_squares(sums_ref, 1, rival)

    @pl.when(at == pl.num_programs(0) - 1)
    def _():
        step, _ = river_steps(children_ref, parents_ref)
        sums_ref[2 * prices:3 * prices] = exact_left(step, plan_scratch[...])


def prepare_kernel(slots, group, river_axis, loads_ref, cards_now_ref, card_ref, gather_ref, spread_ref, own_ref, far_ref,
                   near_table_ref, pot_ref, fold_ref, children_ref, parents_ref,
                   live_ref, row_ref, col_ref, compat_ref, near_ref, main_ref, folds_ref, back_ref):
    padded = row_ref.shape[2]
    rank = jnp.concatenate([own_ref[...], far_ref[...]], axis=1)
    turn = alive_rows(card_ref[0], cards_now_ref)
    slot = lax.broadcasted_iota(jnp.int32, rank.shape, 0)
    live = jnp.where((rank >= 0) & (slot < loads_ref[lax.axis_index(river_axis)]) & (turn > 0), 1.0, 0.0)
    safe = jnp.where(live > 0, rank, 0)
    code = (128 + (safe & 127)).astype(F32)
    high = safe >> 7
    for bit in range(6):
        code = code * jnp.where((high >> bit) & 1 == 1, float(2.0 ** (1 << bit)), 1.0)
    lane = lax.broadcasted_iota(jnp.int32, rank.shape, 1)
    width = H // 2
    own_code = jnp.where(lane[:, :padded] < width, code[:, :padded], 0.0)
    for board in range(slots):
        live_ref[board] = live[board:board + 1]
        row_ref[board] = own_code[board:board + 1].astype(BF16)
    depth = round_up(slots, 8)
    if depth > slots:
        code = jnp.concatenate([code, jnp.zeros((depth - slots, code.shape[1]), F32)], axis=0)
    turned = code.T
    for place in range(slots // group):
        col_ref[place] = turned[:, place * group:(place + 1) * group]
    free = jnp.dot(gather_ref[0], spread_ref[0][:, :padded], preferred_element_type=F32)
    compat_ref[...] = jnp.maximum(free, 0.0).astype(BF16)
    near_ref[...] = near_table_ref[0]
    for place in range(2):
        set_operators(place == 1, pot_ref, fold_ref, children_ref, parents_ref, main_ref.at[place], folds_ref.at[place],
                      back_ref.at[place])


def set_operators(transposed, pot_ref, fold_ref, children_ref, parents_ref, main_scratch, fold_scratch, back_scratch):
    pot = pot_ref[...] / H
    fold = fold_ref[...] / H
    if transposed:
        pot, fold = -pot.T, fold.T
    step, _ = river_steps(children_ref, parents_ref)
    sequences = pot.shape[0]
    infosets = step.shape[0]
    pot_high, pot_low = split_two(pot)
    fold_high, fold_low = split_two(fold)
    main_scratch[:sequences] = jnp.concatenate([pot_high, pot_high, fold_high, fold_high], axis=1)
    main_scratch[sequences:2 * sequences] = jnp.concatenate([pot_low, pot_low, fold_low, fold_low], axis=1)
    exact = step.astype(BF16)
    main_scratch[2 * sequences:2 * sequences + infosets] = jnp.concatenate(
        [jnp.zeros((infosets, 2 * sequences), BF16), exact, exact], axis=1)
    fold_scratch[:sequences] = jnp.concatenate([fold_high, fold_high], axis=1)
    fold_scratch[sequences:] = jnp.concatenate([fold_low, fold_low], axis=1)
    turned = step.T
    if transposed:
        turned = -turned
    turned = turned.astype(BF16)
    back_scratch[...] = jnp.concatenate([turned, turned], axis=1)


def payoffs(own_plans, far_plans, prices, columns, strengths, compat_ref, near_ref, main, folds, back_step):
    sequences, padded = own_plans[0].shape
    tiles = padded // TILE
    width = H // 2
    depths = [min(TILE, round_up(width - at, 16)) for at in range(0, width, TILE)]
    boards = range(len(own_plans))
    owns = [split_two(plan) for plan in own_plans]
    fars = [split_two(plan) for plan in far_plans]
    price_parts = [split_two(price) for price in prices]
    mixes = []
    for inner in boards:
        left = (jnp.concatenate(owns[inner], axis=0), jnp.concatenate(fars[inner], axis=0))
        row = strengths[inner]
        sums = [None] * tiles
        for place in range(2 * tiles):
            depth = depths[place % tiles]
            rows = slice(place * TILE, place * TILE + depth)
            column = jnp.broadcast_to(columns(rows, inner), (depth, LANES)).astype(BF16)
            column = jnp.concatenate([column, column], axis=1)
            piece = left[place // tiles][:, (place % tiles) * TILE:(place % tiles) * TILE + depth]
            for across in range(tiles):
                lanes = slice(across * TILE, (across + 1) * TILE)
                bound = compat_ref[rows, lanes]
                signs = jnp.minimum(jnp.maximum(column - row[:, lanes], -bound), bound)
                part = jnp.dot(piece, signs, preferred_element_type=F32)
                sums[across] = part if sums[across] is None else sums[across] + part
        mixes.append(split_two(jnp.concatenate([item[:sequences] + item[sequences:] for item in sums], axis=1)))
    cards = []
    for inner in boards:
        tail = jnp.concatenate([item[:, padded - LANES:] for item in mixes[inner]], axis=0)
        folded = jnp.dot(folds, tail, preferred_element_type=F32)
        cards.extend(split_two(folded[:sequences] + folded[sequences:]))
    backs = [jnp.dot(back_step, jnp.concatenate(price_parts[inner], axis=0), preferred_element_type=F32) for inner in boards]
    products = [jnp.dot(main, jnp.concatenate(mixes[inner] + owns[inner], axis=0), preferred_element_type=F32)
                for inner in boards]
    nearby = jnp.dot(jnp.concatenate(cards, axis=0), near_ref[...], preferred_element_type=F32)
    done = []
    for inner in boards:
        base = 2 * inner * sequences
        close = nearby[base:base + sequences] + nearby[base + sequences:base + 2 * sequences]
        product = products[inner]
        done.append((product[:sequences] + product[sequences:2 * sequences] + backs[inner] + close, product[2 * sequences:]))
    return done


def pick(ref, base, at, inner, group):
    return ref[inner] if base is None else ref[base + at * group + inner]


def group_payoffs(group, start, side, at, plans, fars, prices, live_ref, row_ref, col_ref, compat_ref, near_ref,
                  main_ref, folds_ref, back_ref):
    strengths = [row_ref[start + at * group + inner] for inner in range(group)]

    def columns(rows, inner):
        return col_ref[start // group + at, rows, inner:inner + 1]

    return payoffs(plans, fars, prices, columns, strengths, compat_ref, near_ref, main_ref[side], folds_ref[side],
                   back_ref[side])


def mover_gradient_kernel(group, start, bases, turn_row, y_ref, far_ref, u_ref, live_ref, row_ref, col_ref, compat_ref,
                          near_ref, main_ref, folds_ref, back_ref, pack_ref, parents_ref, grad_ref, flow_ref):
    _, sequences, padded = grad_ref.shape
    link = river_link(parents_ref, sequences)
    turn_flow = exact_left(link, pack_ref[turn_row:turn_row + link.shape[1], :padded])
    own_plans, far_plans, prices, lives = [], [], [], []
    for inner in range(group):
        live = live_ref[start + inner]
        near_live = live[:, :padded]
        lives.append(near_live)
        own_plans.append(jnp.where(near_live > 0, pick(y_ref, bases[0], 0, inner, group), 0.0))
        far_plans.append(jnp.where(live[:, padded:] > 0, pick(far_ref, bases[1], 0, inner, group), 0.0))
        prices.append(jnp.where(near_live > 0, pick(u_ref, bases[2], 0, inner, group), 0.0))
    done = group_payoffs(group, start, 0, 0, own_plans, far_plans, prices, live_ref, row_ref, col_ref, compat_ref, near_ref,
                         main_ref, folds_ref, back_ref)
    for inner, (gradient, flow) in enumerate(done):
        grad_ref[inner] = gradient
        flow_ref[inner] = lives[inner] * (flow - turn_flow)


def mover_step_kernel(group, start, bases, count, parts, last, own_norm_ref, far_norm_ref, x_ref, v_ref, live_ref,
                      *rest):
    grads, flows = rest[:parts], rest[parts:2 * parts]
    if last:
        new_x_ref, new_v_ref, bar_ref = rest[-3:]
    else:
        new_x_ref, new_v_ref, bar_ref, total_ref = rest[-4:]
        total_ref[...] = rest[2 * parts][...] if start else jnp.zeros_like(total_ref)
    padded = bar_ref.shape[2]
    primal, _ = steps_from(own_norm_ref, far_norm_ref, count)

    def work(part):
        for inner in range(group):
            board = part * group + inner
            place = inner if last else board
            live = live_ref[start + board][:, :padded]
            x = jnp.where(live > 0, pick(x_ref, bases[0], 0, board, group), 0.0)
            v = jnp.where(live > 0, pick(v_ref, bases[1], 0, board, group), 0.0)
            new_x = live * jnp.maximum(x - primal * grads[part][inner], 0.0)
            new_v = v + primal * flows[part][inner]
            new_x_ref[place] = new_x
            new_v_ref[place] = new_v
            bar_ref[board] = 2.0 * new_x - x
            if not last:
                total_ref[0:1] += row_sums(new_x * new_x) + row_sums(new_v * new_v)

    for part in range(parts):
        if last:
            pl.when(pl.program_id(0) == part)(functools.partial(work, part))
        else:
            work(part)


def rival_step_kernel(group, start, bases, count, parts, last, own_norm_ref, far_norm_ref, bar_ref, far_ref, y_ref,
                      u_ref, new_v_ref, live_ref, row_ref, col_ref, compat_ref, near_ref, main_ref, folds_ref, back_ref,
                      bart_ref, children_ref, parents_ref, *rest):
    flows = rest[:parts]
    rest = rest[parts:]
    at = pl.program_id(0)
    if last:
        new_y_ref, new_u_ref, link_scratch, flow_scratch, step_scratch = rest[-5:]
    else:
        new_y_ref, new_u_ref, total_ref, link_scratch, flow_scratch, step_scratch, plan_scratch = rest[-7:]
    padded = live_ref.shape[2] // 2
    infosets = u_ref.shape[1]
    @pl.when(at == 0)
    def _():
        primal, dual = steps_from(own_norm_ref, far_norm_ref, count)
        step_scratch[0:1, :] = jnp.broadcast_to(primal, (1, LANES))
        step_scratch[1:2, :] = jnp.broadcast_to(dual, (1, LANES))
        link_scratch[...] = exact_left(river_link(parents_ref, bar_ref.shape[1]), bart_ref[:, :padded])
        if not last:
            plan_scratch[...] = jnp.zeros_like(plan_scratch)
            if start:
                total_ref[...] = rest[0][...]
            else:
                total_ref[...] = jnp.zeros_like(total_ref)
                for row in range(2):
                    add_squares(total_ref, row, rest[0][row:row + 1] + rest[1][row:row + 1])

    for part in range(parts):
        @pl.when(at == part)
        def _():
            flow_scratch[...] = flows[part][...]

    primal = step_scratch[0:1, 0:1]
    dual = step_scratch[1:2, 0:1]
    own_plans, far_plans, prices = [], [], []
    for inner in range(group):
        own_plans.append(pick(bar_ref, bases[0], at, inner, group))
        far_plans.append(pick(far_ref, bases[1], at, inner, group))
        prices.append(pick(new_v_ref, bases[4], at, inner, group) + primal * flow_scratch[inner])
    done = group_payoffs(group, start, 1, at, own_plans, far_plans, prices, live_ref, row_ref, col_ref, compat_ref, near_ref,
                         main_ref, folds_ref, back_ref)
    squares = jnp.zeros((1, padded), F32)
    for inner, (gradient, flow) in enumerate(done):
        live = live_ref[start + at * group + inner][:, :padded]
        y = jnp.where(live > 0, pick(y_ref, bases[2], at, inner, group), 0.0)
        u = jnp.where(live > 0, pick(u_ref, bases[3], at, inner, group), 0.0)
        flow = live * flow
        new_y = live * jnp.maximum(y + dual * gradient, 0.0)
        new_u = u + dual * (flow - live * link_scratch[...])
        place = inner if last else at * group + inner
        new_y_ref[place] = new_y
        new_u_ref[place] = new_u
        if not last:
            plan_scratch[...] += new_y
            total_ref[0:infosets] += flow
            squares = squares + row_sums(new_y * new_y) + row_sums(new_u * new_u)

    if not last:
        add_squares(total_ref, 1, squares)

        @pl.when(at == pl.num_programs(0) - 1)
        def _():
            step, _ = river_steps(children_ref, parents_ref)
            total_ref[infosets:2 * infosets] += exact_left(step, plan_scratch[...])


def turn_places(sequences, points):
    return 0, 2 * sequences, sequences, 2 * sequences + round_up(points, 8)


def turn_mix(turn, plan, gather_ref, spread_ref):
    return turn * (exact_right(exact_right(plan, gather_ref[0]), spread_ref[0]) + plan)


def turn_tree(turn_children_ref, turn_parents_ref):
    parents = turn_parents_ref[...].astype(F32)
    return turn_children_ref[...].astype(F32) - parents, 1.0 - jnp.sum(parents, axis=1, keepdims=True)


def turn_start_kernel(first, hand_ref, cards_now_ref, card_ref, gather_ref, spread_ref, *rest):
    if first:
        own_ref, far_ref = rest[:2]
        pack = jnp.concatenate([own_ref[...], far_ref[...]], axis=1)
    else:
        pack_ref, old_bar_ref = rest[:2]
        pack = pack_ref[...]
    turn_fold_ref, turn_children_ref, turn_parents_ref, children_ref, parents_ref = rest[2:7]
    grad_ref, flow_ref, link_ref, extra_ref = rest[7:]
    turn = alive_rows(card_ref[0], cards_now_ref)
    link = river_link(parents_ref, children_ref.shape[1])
    step, root = turn_tree(turn_children_ref, turn_parents_ref)
    fold = turn_fold_ref[...]
    sequences, points = fold.shape[0], step.shape[0]
    _, _, y_at, u_at = turn_places(sequences, points)
    y = pack[y_at:y_at + sequences]
    u = pack[u_at:u_at + points]
    grad_ref[...] = pair_dot(fold, turn_mix(turn, y, gather_ref, spread_ref)) / H + turn * exact_left(step.T, u)
    flow_ref[...] = turn * (exact_left(step, y) - root)
    link_ref[...] = exact_left(link, y)
    extra_ref[...] = pack if first else exact_left(link, old_bar_ref[...])


def turn_step_kernel(count, first, names, hand_ref, cards_now_ref, card_ref, gather_ref, spread_ref, *rest):
    pack_ref, grad_ref, flow_ref, link_ref = rest[:4]
    if first:
        sums_ref, sums_far_ref = rest[4:6]
        rest = rest[6:]
    else:
        bar_link_ref, kept_ref, old_steps_ref, sums_ref, sums_far_ref = rest[4:9]
        rest = rest[9:]
    turn_fold_ref, turn_children_ref, turn_parents_ref, children_ref, parents_ref = rest[:5]
    rest = rest[5:]
    turn = alive_rows(card_ref[0], cards_now_ref)
    link_turned = river_link(parents_ref, children_ref.shape[1]).T
    turn_step, turn_root = turn_tree(turn_children_ref, turn_parents_ref)
    fold = turn_fold_ref[...]
    meetings = (CARDS - 6) * turn
    sequences = fold.shape[0]
    points = turn_step.shape[0]
    starts = turn_places(sequences, points)
    infosets = link_turned.shape[1]
    primal, dual = steps_from(sums_ref, sums_far_ref, count)
    sums = jnp.concatenate([sums_ref[...], sums_far_ref[...]], axis=1)
    pack = pack_ref[...]
    if first:
        price_sum = sums[:infosets]
        kept = sums[infosets:2 * infosets]
        plan_sum = sums[2 * infosets:]
    else:
        price_sum = kept_ref[:infosets] + old_steps_ref[1:2, 0:1] * (sums[:infosets] - meetings * bar_link_ref[...])
        kept = kept_ref[infosets:]
        plan_sum = sums[infosets:]
    x = pack[starts[0]:starts[0] + sequences]
    v = pack[starts[1]:starts[1] + points]
    y = pack[starts[2]:starts[2] + sequences]
    u = pack[starts[3]:starts[3] + points]

    grad = grad_ref[...] - turn * exact_left(link_turned, price_sum)
    new_x = turn * jnp.maximum(x - primal * grad, 0.0)
    new_v = v + primal * flow_ref[...]
    bar = 2.0 * new_x - x
    price_bar = 2.0 * new_v - v
    drift = primal * (plan_sum - meetings * link_ref[...])
    rise = pair_dot(fold.T, turn_mix(turn, bar, gather_ref, spread_ref)) / H - turn * (
        exact_left(turn_step.T, price_bar) - exact_left(link_turned, kept + 2.0 * drift))
    new_y = turn * jnp.maximum(y + dual * rise, 0.0)
    new_u = u + dual * (turn * (exact_left(turn_step, bar) - turn_root))
    if first:
        out_pack_ref, out_kept_ref, bar_ref, out_norms_ref, steps_ref = rest
        steps_ref[0:1] = jnp.broadcast_to(primal, (1, LANES))
        steps_ref[1:2] = jnp.broadcast_to(dual, (1, LANES))
        out_pack_ref[...] = jnp.zeros_like(out_pack_ref)
        for start, value in zip(starts, (new_x, new_v, new_y, new_u)):
            out_pack_ref[start:start + value.shape[0]] = value
        out_kept_ref[:infosets] = price_sum
        out_kept_ref[infosets:] = kept + drift
        bar_ref[...] = bar
        river_name, hand_name = names
        flag = jnp.where((lax.axis_index(river_name) == 0) & (hand_ref[0] == 0), 1.0, 0.0)
        out_norms_ref[...] = jnp.zeros_like(out_norms_ref)
        mover = row_sums(new_x * new_x) + row_sums(new_v * new_v)
        rival = row_sums(new_y * new_y) + row_sums(new_u * new_u)
        half = mover.shape[1] // 2
        out_norms_ref[0:1] = flag * (mover[:, :half] + mover[:, half:])
        out_norms_ref[1:2] = flag * (rival[:, :half] + rival[:, half:])
    else:
        bar_ref = rest[0]
        bar_ref[...] = bar
        for out_ref, value in zip(rest[1:], (new_x, new_v, new_y, new_u)):
            out_ref[...] = value[:, :out_ref.shape[1]]


def whole(shape):
    return pl.BlockSpec(shape, lambda *at: (0,) * len(shape))


def smem():
    return pl.BlockSpec(memory_space=pltpu.SMEM)


def local(hand_rank, loads, turn_cards, turn_children, turn_parents, river_children, river_parents, showdown_pot, river_fold,
          turn_fold, mover_turn, mover_river, mover_turn_price, mover_river_price, rival_turn, rival_river,
          rival_turn_price, rival_river_price):
    slots, sequences, width = mover_river.shape
    infosets = mover_river_price.shape[1]
    turn_sequences = mover_turn.shape[0]
    points = mover_turn_price.shape[0]
    river_count = lax.axis_size("river")
    padded = round_up(width + CARDS + 1, TILE)
    both = 2 * padded
    count = float((turn_sequences + points) * H + river_count * slots * (sequences + infosets) * H)
    group = next(size for size in (3, 2, 1) if slots % size == 0)
    chunks = slots // group
    parts = 2 if chunks % 2 == 0 else 1
    stats_group = STATS_BOARDS if slots % STATS_BOARDS == 0 else group
    span = parts * group
    cards, gather, spread, near = (jnp.asarray(table) for table in halves(width, padded))
    hand = lax.axis_index("hand").astype(jnp.int32).reshape(1)
    pack_rows = 2 * (turn_sequences + round_up(points, 8))
    stat_rows = 3 * infosets
    total_rows = 2 * infosets

    def shape(*dims, dtype=F32):
        return jax.ShapeDtypeStruct(dims, dtype)

    def swap(value):
        return lax.ppermute(value, "hand", [(0, 1), (1, 0)])

    def hop_total(value, hop, gate):
        came = lax.ppermute(value, "river", [(at, at ^ hop) for at in range(river_count)])
        if gate is not None:
            came, _ = lax.optimization_barrier((came, gate))
        return value + came

    def boards(rows, size=group, start=0):
        return pl.BlockSpec((size, rows, padded), lambda at, *_: (at + start, 0, 0))

    vmem = pl.BlockSpec(memory_space=pltpu.VMEM)

    def operand(item, first, size):
        if isinstance(item, list):
            length = slots // len(item)
            return item[first // length], vmem, first % length
        return item, boards(item.shape[1], size, first // size), None

    def call(kernel, name, scalars, steps, in_specs, out_specs, out_shape, scratch, args, micros, aliases=None, vmem=VMEM_BYTES):
        estimate = pl.CostEstimate(flops=int(micros * 1e9), bytes_accessed=0, transcendentals=0)
        return pl.pallas_call(
            kernel,
            grid_spec=pltpu.PrefetchScalarGridSpec(
                num_scalar_prefetch=scalars, grid=steps, in_specs=in_specs, out_specs=out_specs, scratch_shapes=scratch),
            out_shape=out_shape, compiler_params=pltpu.CompilerParams(vmem_limit_bytes=vmem),
            cost_estimate=estimate, input_output_aliases=aliases or {}, name=name,
        )(*args)

    card_block = pl.BlockSpec((1, 8, both), lambda at, ref: (ref[0], 0, 0))
    tree_blocks = [whole(river_children.shape), whole(river_parents.shape)]
    half_block = lambda rows, at_row=0: pl.BlockSpec((rows, padded), lambda at, *_: (at_row, 0))
    operator_sizes = ((2 * sequences + infosets, 4 * sequences), (2 * sequences, 2 * sequences), (sequences, 2 * infosets))
    link_scratch = pltpu.VMEM((infosets, padded), F32)
    flow_scratch = pltpu.VMEM((group, infosets, padded), F32)
    step_scratch = pltpu.VMEM((8, LANES), F32)
    plan_scratch = pltpu.VMEM((sequences, padded), F32)
    any_block = pl.BlockSpec(memory_space=pl.ANY)

    rank_far = swap(hand_rank)
    rival_far = swap(rival_river)

    def stats_kernel_here(hand_ref, *refs):
        stats_kernel(slots, stats_group, "river", *refs)

    def prepare_kernel_here(hand_ref, *refs):
        prepare_kernel(slots, group, "river", *refs)

    sums, pack = call(
        stats_kernel_here, "stats", 1, (slots // stats_group,),
        [smem(), smem(), card_block, half_block(slots), boards(sequences, stats_group), boards(infosets, stats_group),
         boards(sequences, stats_group), boards(infosets, stats_group), half_block(turn_sequences), half_block(points),
         half_block(turn_sequences), half_block(points)] + tree_blocks,
        [whole((stat_rows, padded)), whole((pack_rows, padded))],
        [shape(stat_rows, padded), shape(pack_rows, padded)],
        [pltpu.VMEM((slots, 1, padded), F32), plan_scratch],
        (hand, loads, turn_cards, cards, hand_rank, mover_river, mover_river_price, rival_river, rival_river_price,
         mover_turn, mover_turn_price, rival_turn, rival_turn_price, river_children, river_parents), 5,
        vmem=56 * 2**20)
    gather_block = pl.BlockSpec((1, both, LANES), lambda at, ref: (ref[0], 0, 0))
    spread_block = pl.BlockSpec((1, LANES, both), lambda at, ref: (ref[0], 0, 0))
    prepared = [shape(slots, 1, both), shape(slots, 1, padded, dtype=BF16), shape(slots // group, both, group),
                shape(both, padded, dtype=BF16), shape(LANES, padded, dtype=BF16)] + [shape(2, *size, dtype=BF16) for size in operator_sizes]
    near_block = pl.BlockSpec((1, LANES, padded), lambda at, ref: (ref[0], 0, 0))
    tables = call(
        prepare_kernel_here, "prepare", 1, (1,),
        [smem(), smem(), card_block, gather_block, spread_block, half_block(slots), half_block(slots), near_block,
         whole(showdown_pot.shape), whole(river_fold.shape)] + tree_blocks,
        [vmem] * len(prepared), prepared, [],
        (hand, loads, turn_cards, cards, gather, spread, hand_rank, rank_far, near, showdown_pot, river_fold,
         river_children, river_parents), 2)
    live = tables[0]

    def gradients(value, early, y, y_far, u, pack, beside, stage):
        out = []
        hops = [1 << at for at in range(max(river_count - 1, 1).bit_length())]
        if river_count & (river_count - 1):
            value = lax.psum(value, "river")
            hops = []
        extra = None
        for place in range(max(len(hops), 1)):
            near_now = tables[4]
            if place:
                near_now, _ = lax.optimization_barrier((near_now, value))
            gate = []
            if place == min(stage, len(hops) - 1) or not hops:
                extra = beside(early, value)
                gate.extend(extra)
            while len(out) * group < slots and (len(out) <= place or place >= len(hops) - 1):
                first = len(out) * group
                arrays, specs, bases = zip(*(operand(item, first, group) for item in (y, y_far, u)))
                args = (*arrays, *tables[:4], near_now, *tables[5:], pack, river_parents)
                out.append(call(
                    functools.partial(mover_gradient_kernel, group, first, bases, turn_sequences), "mover_gradient", 0, (1,),
                    [*specs] + [vmem] * (len(args) - 3), [vmem] * 2,
                    [shape(group, sequences, padded), shape(group, infosets, padded)], [], args, group))
                gate.append(out[-1][1])
            if hops:
                value = hop_total(value, hops[place], gate)
                if place == 0:
                    value, early = lax.optimization_barrier((value, early))
        return [item[0] for item in out], [item[1] for item in out], (value, swap(value)), extra

    def mover_steps(last, norms, x, v, grad, flow):
        outs = []
        for first in range(0, slots, span):
            arrays, specs, bases = zip(*(operand(item, first, span) for item in (x, v)))
            here = slice(first // group, first // group + parts)
            args = (*norms, *arrays, live, *grad[here], *flow[here])
            in_specs = [vmem] * 2 + [*specs] + [vmem] * (1 + 2 * parts)
            aliases = {}
            if last:
                out_specs = [boards(sequences, group, first // group), boards(infosets, group, first // group), vmem]
                out_shape = [shape(slots, sequences, width), shape(slots, infosets, width), shape(span, sequences, padded)]
                if first:
                    aliases = {len(args): 0, len(args) + 1: 1}
                    in_specs += [any_block] * 2
                    args += tuple(outs[-1][:2])
            else:
                out_specs = [vmem] * 4
                out_shape = [shape(span, sequences, padded), shape(span, infosets, padded),
                             shape(span, sequences, padded), shape(8, padded)]
                if first:
                    in_specs += [vmem]
                    args += (outs[-1][3],)
            outs.append(call(functools.partial(mover_step_kernel, group, first, bases, count, parts, last),
                             "mover_step", 0, (parts if last else 1,), in_specs, out_specs, out_shape, [], args, parts, aliases))
        if last:
            return outs[-1][0], outs[-1][1], [item[2] for item in outs]
        return [item[0] for item in outs], [item[1] for item in outs], [item[2] for item in outs], outs[-1][3]

    def rival_steps(last, norms, bar, bar_far, y, u, new_v, flow, bar_turn, parts_before):
        outs = []
        for first in range(0, slots, span):
            arrays, specs, bases = zip(*(operand(item, first, group) for item in (bar, bar_far, y, u, new_v)))
            here = slice(first // group, first // group + parts)
            args = (*norms, *arrays, *tables, bar_turn, river_children, river_parents, *flow[here])
            in_specs = [vmem] * 2 + [*specs] + [vmem] * (len(args) - 7)
            aliases = {}
            scratch = [link_scratch, flow_scratch, step_scratch]
            if last:
                out_specs = [boards(sequences, group, first // group), boards(infosets, group, first // group)]
                out_shape = [shape(slots, sequences, width), shape(slots, infosets, width)]
                if first:
                    aliases = {len(args): 0, len(args) + 1: 1}
                    in_specs += [any_block] * 2
                    args += tuple(outs[-1][:2])
            else:
                out_specs = [vmem] * 3
                out_shape = [shape(span, sequences, padded), shape(span, infosets, padded), shape(total_rows, padded)]
                scratch = scratch + [plan_scratch]
                before = (outs[-1][2],) if first else tuple(parts_before)
                in_specs += [vmem] * len(before)
                args += before
            outs.append(call(functools.partial(rival_step_kernel, group, first, bases, count, parts, last),
                             "rival_step", 0, (parts,), in_specs, out_specs, out_shape, scratch, args, span, aliases))
        if last:
            return outs[-1]
        return [item[0] for item in outs], [item[1] for item in outs], outs[-1][2]

    turn_blocks = [smem(), card_block, gather_block, spread_block]
    turn_tables = (turn_cards, cards, gather, spread)
    turn_matrices = (turn_fold, turn_children, turn_parents, river_children, river_parents)

    def turn_call(first, data):
        if first:
            out_shape = [shape(pack_rows, both), shape(2 * infosets, both), shape(turn_sequences, both), shape(8, padded),
                         shape(8, LANES)]
        else:
            out_shape = [shape(turn_sequences, both), shape(turn_sequences, width), shape(points, width),
                         shape(turn_sequences, width), shape(points, width)]
        return call(
            functools.partial(turn_step_kernel, count, first, ("river", "hand")), "turn_step", 1, (1,),
            turn_blocks + [vmem] * len(data) + [whole(item.shape) for item in turn_matrices],
            [vmem] * 5 if first else [vmem] + [whole(item.shape) for item in out_shape[1:]],
            out_shape, [], (hand, *turn_tables, *data, *turn_matrices), 2)

    def turn_start(first, data):
        out_shape = [shape(turn_sequences, both), shape(points, both), shape(infosets, both),
                     shape(pack_rows if first else infosets, both)]
        return call(
            functools.partial(turn_start_kernel, first), "turn_start", 1, (1,),
            turn_blocks + [vmem] * 2 + [whole(item.shape) for item in turn_matrices], [vmem] * 4, out_shape, [],
            (hand, *turn_tables, *data, *turn_matrices), 1)

    def first_start(far, value):
        near_now, _ = lax.optimization_barrier((pack, value))
        return turn_start(True, (near_now, far))

    grad, flow, norms, starts = gradients(sums, swap(pack), rival_river, rival_far, rival_river_price, pack, first_start, 2)
    x, v, bar, part = mover_steps(False, norms, mover_river, mover_river_price, grad, flow)
    bar_far = [swap(item) for item in bar]
    pack, kept, bar_turn, turn_norms, turn_steps = turn_call(True, (starts[3], *starts[:3], *norms))
    y, u, total = rival_steps(False, norms, bar, bar_far, rival_river, rival_river_price, v, flow, bar_turn,
                              (part, turn_norms))
    y_far = [swap(item) for item in y]

    def second_start(far, value):
        now, _ = lax.optimization_barrier((pack, value))
        return turn_start(False, (now, bar_turn))

    grad, flow, norms, starts = gradients(total, y_far[0], y, y_far, u, pack, second_start, 0)
    next_x, next_v, bar = mover_steps(True, norms, x, v, grad, flow)
    bar_far = [swap(item) for item in bar]
    bar_turn, next_xt, next_vt, next_yt, next_ut = turn_call(False, (pack, *starts, kept, turn_steps, *norms))
    next_y, next_u = rival_steps(True, norms, bar, bar_far, y, u, next_v, flow, bar_turn, None)
    return (next_xt, next_x, next_vt, next_v, next_yt, next_y, next_ut, next_u)


def solution(mesh):
    river = P(("groups", "river"), None, "hand")
    turn = P("groups", "hand")
    placed = (P(("groups", "river"), "hand"), P("groups"), P("groups"), P(), P(), P(), P(), P(), P(), P(),
              turn, river, turn, river, turn, river, turn, river)
    return jax.shard_map(local, mesh=mesh, in_specs=placed,
                         out_specs=(turn, river, turn, river, turn, river, turn, river), check_vma=False)
```

```python
import functools

import jax
import jax.numpy as jnp
import ml_dtypes
import numpy as np
from jax import lax
from jax.experimental import pallas as pl
from jax.experimental.pallas import tpu as pltpu
from jax.sharding import PartitionSpec as P

CARDS = 52
H = 1326
ITERS = 2
STEP_SCALE = 0.25
EPSILON = 1e-06
LANES = 128
TILE = 256
VMEM_BYTES = 20 * 2**20
STATS_BOARDS = 6
F32 = jnp.float32
BF16 = jnp.bfloat16


def round_up(value, unit):
    return -(-value // unit) * unit


def halves(width, padded):
    pairs = np.stack(np.triu_indices(CARDS, 1)).astype(np.int32)
    deck = np.arange(CARDS)
    incidence = (pairs[0][:, None] == deck) | (pairs[1][:, None] == deck)
    parts = pairs.shape[1] // width
    cards = np.full((parts, 8, 2 * padded), -1, np.int32)
    gather = np.zeros((parts, 2 * padded, LANES), np.float32)
    spread = np.zeros((parts, LANES, 2 * padded), np.float32)
    for part in range(parts):
        spread[part, np.arange(CARDS + 1), width + np.arange(CARDS + 1)] = 1.0
        for place, half in enumerate((part, 1 - part)):
            far = slice(half * width, (half + 1) * width)
            rows = slice(place * padded, place * padded + width)
            cards[part, :2, rows] = pairs[:, far]
            gather[part, rows, :CARDS] = incidence[far]
            gather[part, rows, CARDS] = 1.0
            spread[part, :CARDS, rows] = -incidence[far].T.astype(np.float32)
            spread[part, CARDS, rows] = 1.0
    near = np.zeros((parts, LANES, padded), np.float32)
    first = width - (padded - LANES)
    near[:, first:first + CARDS + 1, :width] = spread[:, :CARDS + 1, :width]
    exact = ml_dtypes.bfloat16
    return (cards, gather.astype(exact), spread.astype(exact), near.astype(exact))


def split_two(value):
    high = value.astype(BF16)
    return high, (value - high.astype(F32)).astype(BF16)


def exact_right(value, matrix):
    rows = value.shape[0]
    first = value.astype(BF16)
    rest = value - first.astype(F32)
    second = rest.astype(BF16)
    third = (rest - second.astype(F32)).astype(BF16)
    total = jnp.dot(jnp.concatenate([first, second, third], axis=0), matrix, preferred_element_type=F32)
    return total[:rows] + total[rows:2 * rows] + total[2 * rows:]


def exact_left(matrix, value):
    first = value.astype(BF16)
    rest = value - first.astype(F32)
    second = rest.astype(BF16)
    third = (rest - second.astype(F32)).astype(BF16)
    matrix = matrix.astype(BF16)
    return jnp.dot(jnp.concatenate([matrix] * 3, axis=1), jnp.concatenate([first, second, third], axis=0),
                   preferred_element_type=F32)


def pair_dot(left, right):
    rows = left.shape[0]
    left_high, left_low = split_two(left)
    right_high, right_low = split_two(right)
    total = jnp.dot(
        jnp.concatenate([jnp.concatenate([left_high] * 2, axis=1), jnp.concatenate([left_low] * 2, axis=1)], axis=0),
        jnp.concatenate([right_high, right_low], axis=0), preferred_element_type=F32)
    return total[:rows] + total[rows:]


def alive_rows(card_rows, turn_cards):
    one, two = card_rows[0:1], card_rows[1:2]
    held = one < 0
    for place in range(4):
        card = turn_cards[place]
        held = held | (one == card) | (two == card)
    return jnp.where(held, 0.0, 1.0).astype(F32)


def row_sums(value):
    return jnp.sum(value, axis=0, keepdims=True)


def add_squares(sums_ref, row, squares):
    last = sums_ref.shape[1] - 1
    sums_ref[row:row + 1, last:] += jnp.sum(squares, axis=1, keepdims=True)


def steps_from(own_ref, far_ref, count):
    last = own_ref.shape[1] - 1
    totals = own_ref[0:2, last:] + far_ref[0:2, last:]
    weight = jnp.sqrt((totals[1:2] / count + EPSILON) / (totals[0:1] / count + EPSILON))
    return STEP_SCALE / weight, STEP_SCALE * weight


def river_steps(children_ref, parents_ref):
    sequences = children_ref.shape[1]
    step = (children_ref[...] - parents_ref[:, :sequences]).astype(F32)
    return step, parents_ref[:, sequences:].astype(F32)


def river_link(parents_ref, sequences):
    return parents_ref[:, sequences:].astype(F32)


def stats_kernel(slots, group, river_axis, loads_ref, cards_now_ref, card_ref, rank_ref, x_ref, v_ref, y_ref, u_ref,
                 xt_ref, vt_ref, yt_ref, ut_ref, children_ref, parents_ref,
                 sums_ref, pack_ref, live_scratch, plan_scratch):
    at = pl.program_id(0)
    padded = live_scratch.shape[2]
    prices = v_ref.shape[1]
    river_here = lax.axis_index(river_axis)

    @pl.when(at == 0)
    def _():
        turn = alive_rows(card_ref[0, :, :padded], cards_now_ref)
        slot = lax.broadcasted_iota(jnp.int32, (slots, padded), 0)
        rank = rank_ref[...]
        live = jnp.where((rank >= 0) & (slot < loads_ref[river_here]) & (turn > 0), 1.0, 0.0)
        for board in range(slots):
            live_scratch[board] = live[board:board + 1]
        sums_ref[...] = jnp.zeros_like(sums_ref)
        plan_scratch[...] = jnp.zeros_like(plan_scratch)
        pack_ref[...] = jnp.zeros_like(pack_ref)
        first = jnp.where(river_here == 0, 1.0, 0.0)
        base = 0
        for rows, row in ((xt_ref, 0), (yt_ref, 1), (vt_ref, 0), (ut_ref, 1)):
            value = jnp.where(turn > 0, rows[...], 0.0)
            pack_ref[base:base + value.shape[0]] = value
            base += round_up(value.shape[0], 8)
            add_squares(sums_ref, row, first * row_sums(value * value))

    mover = jnp.zeros((1, padded), F32)
    rival = jnp.zeros((1, padded), F32)
    for inner in range(group):
        live = live_scratch[at * group + inner] > 0
        x = jnp.where(live, x_ref[inner], 0.0)
        v = jnp.where(live, v_ref[inner], 0.0)
        y = jnp.where(live, y_ref[inner], 0.0)
        u = jnp.where(live, u_ref[inner], 0.0)
        mover = mover + row_sums(x * x) + row_sums(v * v)
        rival = rival + row_sums(y * y) + row_sums(u * u)
        sums_ref[0:prices] += u
        sums_ref[prices:2 * prices] += v
        plan_scratch[...] += y
    add_squares(sums_ref, 0, mover)
    add_squares(sums_ref, 1, rival)

    @pl.when(at == pl.num_programs(0) - 1)
    def _():
        step, _ = river_steps(children_ref, parents_ref)
        sums_ref[2 * prices:3 * prices] = exact_left(step, plan_scratch[...])


def prepare_kernel(slots, group, river_axis, loads_ref, cards_now_ref, card_ref, gather_ref, spread_ref, own_ref, far_ref,
                   near_table_ref, pot_ref, fold_ref, children_ref, parents_ref,
                   live_ref, row_ref, col_ref, compat_ref, near_ref, main_ref, folds_ref, back_ref):
    padded = row_ref.shape[2]
    rank = jnp.concatenate([own_ref[...], far_ref[...]], axis=1)
    turn = alive_rows(card_ref[0], cards_now_ref)
    slot = lax.broadcasted_iota(jnp.int32, rank.shape, 0)
    live = jnp.where((rank >= 0) & (slot < loads_ref[lax.axis_index(river_axis)]) & (turn > 0), 1.0, 0.0)
    safe = jnp.where(live > 0, rank, 0)
    code = (128 + (safe & 127)).astype(F32)
    high = safe >> 7
    for bit in range(6):
        code = code * jnp.where((high >> bit) & 1 == 1, float(2.0 ** (1 << bit)), 1.0)
    lane = lax.broadcasted_iota(jnp.int32, rank.shape, 1)
    width = H // 2
    own_code = jnp.where(lane[:, :padded] < width, code[:, :padded], 0.0)
    for board in range(slots):
        live_ref[board] = live[board:board + 1]
        row_ref[board] = own_code[board:board + 1].astype(BF16)
    depth = round_up(slots, 8)
    if depth > slots:
        code = jnp.concatenate([code, jnp.zeros((depth - slots, code.shape[1]), F32)], axis=0)
    turned = code.T
    for place in range(slots // group):
        col_ref[place] = turned[:, place * group:(place + 1) * group]
    free = jnp.dot(gather_ref[0], spread_ref[0][:, :padded], preferred_element_type=F32)
    compat_ref[0] = jnp.maximum(free, 0.0).astype(BF16)
    compat_ref[1] = jnp.minimum(-free, 0.0).astype(BF16)
    near_ref[...] = near_table_ref[0]
    for place in range(2):
        set_operators(place == 1, pot_ref, fold_ref, children_ref, parents_ref, main_ref.at[place], folds_ref.at[place],
                      back_ref.at[place])


def set_operators(transposed, pot_ref, fold_ref, children_ref, parents_ref, main_scratch, fold_scratch, back_scratch):
    pot = pot_ref[...] / H
    fold = fold_ref[...] / H
    if transposed:
        pot, fold = -pot.T, fold.T
    step, _ = river_steps(children_ref, parents_ref)
    sequences = pot.shape[0]
    infosets = step.shape[0]
    pot_high, pot_low = split_two(pot)
    fold_high, fold_low = split_two(fold)
    main_scratch[:sequences] = jnp.concatenate([pot_high, pot_high, fold_high, fold_high], axis=1)
    main_scratch[sequences:2 * sequences] = jnp.concatenate([pot_low, pot_low, fold_low, fold_low], axis=1)
    exact = step.astype(BF16)
    main_scratch[2 * sequences:2 * sequences + infosets] = jnp.concatenate(
        [jnp.zeros((infosets, 2 * sequences), BF16), exact, exact], axis=1)
    fold_scratch[:sequences] = jnp.concatenate([fold_high, fold_high], axis=1)
    fold_scratch[sequences:] = jnp.concatenate([fold_low, fold_low], axis=1)
    turned = step.T
    if transposed:
        turned = -turned
    turned = turned.astype(BF16)
    back_scratch[...] = jnp.concatenate([turned, turned], axis=1)


def payoffs(own_plans, far_plans, prices, columns, strengths, compat_ref, near_ref, main, folds, back_step):
    sequences, padded = own_plans[0].shape
    tiles = padded // TILE
    width = H // 2
    depths = [min(TILE, round_up(width - at, 16)) for at in range(0, width, TILE)]
    boards = range(len(own_plans))
    owns = [split_two(plan) for plan in own_plans]
    fars = [split_two(plan) for plan in far_plans]
    price_parts = [split_two(price) for price in prices]
    mixes = []
    for inner in boards:
        left = (jnp.concatenate(owns[inner], axis=0), jnp.concatenate(fars[inner], axis=0))
        row = strengths[inner]
        sums = [None] * tiles
        for place in range(2 * tiles):
            depth = depths[place % tiles]
            rows = slice(place * TILE, place * TILE + depth)
            column = jnp.broadcast_to(columns(rows, inner), (depth, LANES)).astype(BF16)
            column = jnp.concatenate([column, column], axis=1)
            piece = left[place // tiles][:, (place % tiles) * TILE:(place % tiles) * TILE + depth]
            for across in range(tiles):
                lanes = slice(across * TILE, (across + 1) * TILE)
                bound = compat_ref[0, rows, lanes]
                signs = jnp.minimum(jnp.maximum(column - row[:, lanes], compat_ref[1, rows, lanes]), bound)
                part = jnp.dot(piece, signs, preferred_element_type=F32)
                sums[across] = part if sums[across] is None else sums[across] + part
        mixes.append(split_two(jnp.concatenate([item[:sequences] + item[sequences:] for item in sums], axis=1)))
    cards = []
    for inner in boards:
        tail = jnp.concatenate([item[:, padded - LANES:] for item in mixes[inner]], axis=0)
        folded = jnp.dot(folds, tail, preferred_element_type=F32)
        cards.extend(split_two(folded[:sequences] + folded[sequences:]))
    backs = [jnp.dot(back_step, jnp.concatenate(price_parts[inner], axis=0), preferred_element_type=F32) for inner in boards]
    products = [jnp.dot(main, jnp.concatenate(mixes[inner] + owns[inner], axis=0), preferred_element_type=F32)
                for inner in boards]
    nearby = jnp.dot(jnp.concatenate(cards, axis=0), near_ref[...], preferred_element_type=F32)
    done = []
    for inner in boards:
        base = 2 * inner * sequences
        close = nearby[base:base + sequences] + nearby[base + sequences:base + 2 * sequences]
        product = products[inner]
        done.append((product[:sequences] + product[sequences:2 * sequences] + backs[inner] + close, product[2 * sequences:]))
    return done


def pick(ref, base, at, inner, group):
    return ref[inner] if base is None else ref[base + at * group + inner]


def group_payoffs(group, start, side, at, plans, fars, prices, live_ref, row_ref, col_ref, compat_ref, near_ref,
                  main_ref, folds_ref, back_ref):
    strengths = [row_ref[start + at * group + inner] for inner in range(group)]

    def columns(rows, inner):
        return col_ref[start // group + at, rows, inner:inner + 1]

    return payoffs(plans, fars, prices, columns, strengths, compat_ref, near_ref, main_ref[side], folds_ref[side],
                   back_ref[side])


def mover_gradient_kernel(group, start, bases, turn_row, y_ref, far_ref, u_ref, live_ref, row_ref, col_ref, compat_ref,
                          near_ref, main_ref, folds_ref, back_ref, pack_ref, parents_ref, grad_ref, flow_ref):
    _, sequences, padded = grad_ref.shape
    link = river_link(parents_ref, sequences)
    turn_flow = exact_left(link, pack_ref[turn_row:turn_row + link.shape[1], :padded])
    own_plans, far_plans, prices, lives = [], [], [], []
    for inner in range(group):
        live = live_ref[start + inner]
        near_live = live[:, :padded]
        lives.append(near_live)
        own_plans.append(jnp.where(near_live > 0, pick(y_ref, bases[0], 0, inner, group), 0.0))
        far_plans.append(jnp.where(live[:, padded:] > 0, pick(far_ref, bases[1], 0, inner, group), 0.0))
        prices.append(jnp.where(near_live > 0, pick(u_ref, bases[2], 0, inner, group), 0.0))
    done = group_payoffs(group, start, 0, 0, own_plans, far_plans, prices, live_ref, row_ref, col_ref, compat_ref, near_ref,
                         main_ref, folds_ref, back_ref)
    for inner, (gradient, flow) in enumerate(done):
        grad_ref[inner] = gradient
        flow_ref[inner] = lives[inner] * (flow - turn_flow)


def mover_step_kernel(group, start, bases, count, parts, last, own_norm_ref, far_norm_ref, x_ref, v_ref, live_ref,
                      *rest):
    grads, flows = rest[:parts], rest[parts:2 * parts]
    if last:
        new_x_ref, new_v_ref, bar_ref = rest[-3:]
    else:
        new_x_ref, new_v_ref, bar_ref, total_ref = rest[-4:]
        total_ref[...] = rest[2 * parts][...] if start else jnp.zeros_like(total_ref)
    padded = bar_ref.shape[2]
    primal, _ = steps_from(own_norm_ref, far_norm_ref, count)

    def work(part):
        for inner in range(group):
            board = part * group + inner
            place = inner if last else board
            live = live_ref[start + board][:, :padded]
            x = jnp.where(live > 0, pick(x_ref, bases[0], 0, board, group), 0.0)
            v = jnp.where(live > 0, pick(v_ref, bases[1], 0, board, group), 0.0)
            new_x = live * jnp.maximum(x - primal * grads[part][inner], 0.0)
            new_v = v + primal * flows[part][inner]
            new_x_ref[place] = new_x
            new_v_ref[place] = new_v
            bar_ref[board] = 2.0 * new_x - x
            if not last:
                total_ref[0:1] += row_sums(new_x * new_x) + row_sums(new_v * new_v)

    for part in range(parts):
        if last:
            pl.when(pl.program_id(0) == part)(functools.partial(work, part))
        else:
            work(part)


def rival_step_kernel(group, start, bases, count, parts, last, own_norm_ref, far_norm_ref, bar_ref, far_ref, y_ref,
                      u_ref, new_v_ref, live_ref, row_ref, col_ref, compat_ref, near_ref, main_ref, folds_ref, back_ref,
                      bart_ref, children_ref, parents_ref, *rest):
    flows = rest[:parts]
    rest = rest[parts:]
    at = pl.program_id(0)
    if last:
        new_y_ref, new_u_ref, link_scratch, flow_scratch, step_scratch = rest[-5:]
    else:
        new_y_ref, new_u_ref, total_ref, link_scratch, flow_scratch, step_scratch, plan_scratch = rest[-7:]
    padded = live_ref.shape[2] // 2
    infosets = u_ref.shape[1]
    @pl.when(at == 0)
    def _():
        primal, dual = steps_from(own_norm_ref, far_norm_ref, count)
        step_scratch[0:1, :] = jnp.broadcast_to(primal, (1, LANES))
        step_scratch[1:2, :] = jnp.broadcast_to(dual, (1, LANES))
        link_scratch[...] = exact_left(river_link(parents_ref, bar_ref.shape[1]), bart_ref[:, :padded])
        if not last:
            plan_scratch[...] = jnp.zeros_like(plan_scratch)
            if start:
                total_ref[...] = rest[0][...]
            else:
                total_ref[...] = jnp.zeros_like(total_ref)
                for row in range(2):
                    add_squares(total_ref, row, rest[0][row:row + 1] + rest[1][row:row + 1])

    for part in range(parts):
        @pl.when(at == part)
        def _():
            flow_scratch[...] = flows[part][...]

    primal = step_scratch[0:1, 0:1]
    dual = step_scratch[1:2, 0:1]
    own_plans, far_plans, prices = [], [], []
    for inner in range(group):
        own_plans.append(pick(bar_ref, bases[0], at, inner, group))
        far_plans.append(pick(far_ref, bases[1], at, inner, group))
        prices.append(pick(new_v_ref, bases[4], at, inner, group) + primal * flow_scratch[inner])
    done = group_payoffs(group, start, 1, at, own_plans, far_plans, prices, live_ref, row_ref, col_ref, compat_ref, near_ref,
                         main_ref, folds_ref, back_ref)
    squares = jnp.zeros((1, padded), F32)
    for inner, (gradient, flow) in enumerate(done):
        live = live_ref[start + at * group + inner][:, :padded]
        y = jnp.where(live > 0, pick(y_ref, bases[2], at, inner, group), 0.0)
        u = jnp.where(live > 0, pick(u_ref, bases[3], at, inner, group), 0.0)
        flow = live * flow
        new_y = live * jnp.maximum(y + dual * gradient, 0.0)
        new_u = u + dual * (flow - live * link_scratch[...])
        place = inner if last else at * group + inner
        new_y_ref[place] = new_y
        new_u_ref[place] = new_u
        if not last:
            plan_scratch[...] += new_y
            total_ref[0:infosets] += flow
            squares = squares + row_sums(new_y * new_y) + row_sums(new_u * new_u)

    if not last:
        add_squares(total_ref, 1, squares)

        @pl.when(at == pl.num_programs(0) - 1)
        def _():
            step, _ = river_steps(children_ref, parents_ref)
            total_ref[infosets:2 * infosets] += exact_left(step, plan_scratch[...])


def turn_places(sequences, points):
    return 0, 2 * sequences, sequences, 2 * sequences + round_up(points, 8)


def turn_mix(turn, plan, gather_ref, spread_ref):
    return turn * (exact_right(exact_right(plan, gather_ref[0]), spread_ref[0]) + plan)


def turn_tree(turn_children_ref, turn_parents_ref):
    parents = turn_parents_ref[...].astype(F32)
    return turn_children_ref[...].astype(F32) - parents, 1.0 - jnp.sum(parents, axis=1, keepdims=True)


def turn_start_kernel(first, hand_ref, cards_now_ref, card_ref, gather_ref, spread_ref, *rest):
    if first:
        own_ref, far_ref = rest[:2]
        pack = jnp.concatenate([own_ref[...], far_ref[...]], axis=1)
    else:
        pack_ref, old_bar_ref = rest[:2]
        pack = pack_ref[...]
    turn_fold_ref, turn_children_ref, turn_parents_ref, children_ref, parents_ref = rest[2:7]
    grad_ref, flow_ref, link_ref, extra_ref = rest[7:]
    turn = alive_rows(card_ref[0], cards_now_ref)
    link = river_link(parents_ref, children_ref.shape[1])
    step, root = turn_tree(turn_children_ref, turn_parents_ref)
    fold = turn_fold_ref[...]
    sequences, points = fold.shape[0], step.shape[0]
    _, _, y_at, u_at = turn_places(sequences, points)
    y = pack[y_at:y_at + sequences]
    u = pack[u_at:u_at + points]
    grad_ref[...] = pair_dot(fold, turn_mix(turn, y, gather_ref, spread_ref)) / H + turn * exact_left(step.T, u)
    flow_ref[...] = turn * (exact_left(step, y) - root)
    link_ref[...] = exact_left(link, y)
    extra_ref[...] = pack if first else exact_left(link, old_bar_ref[...])


def turn_step_kernel(count, first, names, hand_ref, cards_now_ref, card_ref, gather_ref, spread_ref, *rest):
    pack_ref, grad_ref, flow_ref, link_ref = rest[:4]
    if first:
        sums_ref, sums_far_ref = rest[4:6]
        rest = rest[6:]
    else:
        bar_link_ref, kept_ref, old_steps_ref, sums_ref, sums_far_ref = rest[4:9]
        rest = rest[9:]
    turn_fold_ref, turn_children_ref, turn_parents_ref, children_ref, parents_ref = rest[:5]
    rest = rest[5:]
    turn = alive_rows(card_ref[0], cards_now_ref)
    link_turned = river_link(parents_ref, children_ref.shape[1]).T
    turn_step, turn_root = turn_tree(turn_children_ref, turn_parents_ref)
    fold = turn_fold_ref[...]
    meetings = (CARDS - 6) * turn
    sequences = fold.shape[0]
    points = turn_step.shape[0]
    starts = turn_places(sequences, points)
    infosets = link_turned.shape[1]
    primal, dual = steps_from(sums_ref, sums_far_ref, count)
    sums = jnp.concatenate([sums_ref[...], sums_far_ref[...]], axis=1)
    pack = pack_ref[...]
    if first:
        price_sum = sums[:infosets]
        kept = sums[infosets:2 * infosets]
        plan_sum = sums[2 * infosets:]
    else:
        price_sum = kept_ref[:infosets] + old_steps_ref[1:2, 0:1] * (sums[:infosets] - meetings * bar_link_ref[...])
        kept = kept_ref[infosets:]
        plan_sum = sums[infosets:]
    x = pack[starts[0]:starts[0] + sequences]
    v = pack[starts[1]:starts[1] + points]
    y = pack[starts[2]:starts[2] + sequences]
    u = pack[starts[3]:starts[3] + points]

    grad = grad_ref[...] - turn * exact_left(link_turned, price_sum)
    new_x = turn * jnp.maximum(x - primal * grad, 0.0)
    new_v = v + primal * flow_ref[...]
    bar = 2.0 * new_x - x
    price_bar = 2.0 * new_v - v
    drift = primal * (plan_sum - meetings * link_ref[...])
    rise = pair_dot(fold.T, turn_mix(turn, bar, gather_ref, spread_ref)) / H - turn * (
        exact_left(turn_step.T, price_bar) - exact_left(link_turned, kept + 2.0 * drift))
    new_y = turn * jnp.maximum(y + dual * rise, 0.0)
    new_u = u + dual * (turn * (exact_left(turn_step, bar) - turn_root))
    if first:
        out_pack_ref, out_kept_ref, bar_ref, out_norms_ref, steps_ref = rest
        steps_ref[0:1] = jnp.broadcast_to(primal, (1, LANES))
        steps_ref[1:2] = jnp.broadcast_to(dual, (1, LANES))
        out_pack_ref[...] = jnp.zeros_like(out_pack_ref)
        for start, value in zip(starts, (new_x, new_v, new_y, new_u)):
            out_pack_ref[start:start + value.shape[0]] = value
        out_kept_ref[:infosets] = price_sum
        out_kept_ref[infosets:] = kept + drift
        bar_ref[...] = bar
        river_name, hand_name = names
        flag = jnp.where((lax.axis_index(river_name) == 0) & (hand_ref[0] == 0), 1.0, 0.0)
        out_norms_ref[...] = jnp.zeros_like(out_norms_ref)
        mover = row_sums(new_x * new_x) + row_sums(new_v * new_v)
        rival = row_sums(new_y * new_y) + row_sums(new_u * new_u)
        half = mover.shape[1] // 2
        out_norms_ref[0:1] = flag * (mover[:, :half] + mover[:, half:])
        out_norms_ref[1:2] = flag * (rival[:, :half] + rival[:, half:])
    else:
        bar_ref = rest[0]
        bar_ref[...] = bar
        for out_ref, value in zip(rest[1:], (new_x, new_v, new_y, new_u)):
            out_ref[...] = value[:, :out_ref.shape[1]]


def whole(shape):
    return pl.BlockSpec(shape, lambda *at: (0,) * len(shape))


def smem():
    return pl.BlockSpec(memory_space=pltpu.SMEM)


def local(hand_rank, loads, turn_cards, turn_children, turn_parents, river_children, river_parents, showdown_pot, river_fold,
          turn_fold, mover_turn, mover_river, mover_turn_price, mover_river_price, rival_turn, rival_river,
          rival_turn_price, rival_river_price):
    slots, sequences, width = mover_river.shape
    infosets = mover_river_price.shape[1]
    turn_sequences = mover_turn.shape[0]
    points = mover_turn_price.shape[0]
    river_count = lax.axis_size("river")
    padded = round_up(width + CARDS + 1, TILE)
    both = 2 * padded
    count = float((turn_sequences + points) * H + river_count * slots * (sequences + infosets) * H)
    group = next(size for size in (3, 2, 1) if slots % size == 0)
    chunks = slots // group
    parts = 2 if chunks % 2 == 0 else 1
    stats_group = STATS_BOARDS if slots % STATS_BOARDS == 0 else group
    span = parts * group
    cards, gather, spread, near = (jnp.asarray(table) for table in halves(width, padded))
    hand = lax.axis_index("hand").astype(jnp.int32).reshape(1)
    pack_rows = 2 * (turn_sequences + round_up(points, 8))
    stat_rows = 3 * infosets
    total_rows = 2 * infosets

    def shape(*dims, dtype=F32):
        return jax.ShapeDtypeStruct(dims, dtype)

    def swap(value):
        return lax.ppermute(value, "hand", [(0, 1), (1, 0)])

    def hop_total(value, hop, gate):
        came = lax.ppermute(value, "river", [(at, at ^ hop) for at in range(river_count)])
        if gate is not None:
            came, _ = lax.optimization_barrier((came, gate))
        return value + came

    def boards(rows, size=group, start=0):
        return pl.BlockSpec((size, rows, padded), lambda at, *_: (at + start, 0, 0))

    vmem = pl.BlockSpec(memory_space=pltpu.VMEM)

    def operand(item, first, size):
        if isinstance(item, list):
            length = slots // len(item)
            return item[first // length], vmem, first % length
        return item, boards(item.shape[1], size, first // size), None

    def call(kernel, name, scalars, steps, in_specs, out_specs, out_shape, scratch, args, micros, aliases=None, vmem=VMEM_BYTES):
        estimate = pl.CostEstimate(flops=int(micros * 1e9), bytes_accessed=0, transcendentals=0)
        return pl.pallas_call(
            kernel,
            grid_spec=pltpu.PrefetchScalarGridSpec(
                num_scalar_prefetch=scalars, grid=steps, in_specs=in_specs, out_specs=out_specs, scratch_shapes=scratch),
            out_shape=out_shape, compiler_params=pltpu.CompilerParams(vmem_limit_bytes=vmem),
            cost_estimate=estimate, input_output_aliases=aliases or {}, name=name,
        )(*args)

    card_block = pl.BlockSpec((1, 8, both), lambda at, ref: (ref[0], 0, 0))
    tree_blocks = [whole(river_children.shape), whole(river_parents.shape)]
    half_block = lambda rows, at_row=0: pl.BlockSpec((rows, padded), lambda at, *_: (at_row, 0))
    operator_sizes = ((2 * sequences + infosets, 4 * sequences), (2 * sequences, 2 * sequences), (sequences, 2 * infosets))
    link_scratch = pltpu.VMEM((infosets, padded), F32)
    flow_scratch = pltpu.VMEM((group, infosets, padded), F32)
    step_scratch = pltpu.VMEM((8, LANES), F32)
    plan_scratch = pltpu.VMEM((sequences, padded), F32)
    any_block = pl.BlockSpec(memory_space=pl.ANY)

    rank_far = swap(hand_rank)
    rival_far = swap(rival_river)

    def stats_kernel_here(hand_ref, *refs):
        stats_kernel(slots, stats_group, "river", *refs)

    def prepare_kernel_here(hand_ref, *refs):
        prepare_kernel(slots, group, "river", *refs)

    sums, pack = call(
        stats_kernel_here, "stats", 1, (slots // stats_group,),
        [smem(), smem(), card_block, half_block(slots), boards(sequences, stats_group), boards(infosets, stats_group),
         boards(sequences, stats_group), boards(infosets, stats_group), half_block(turn_sequences), half_block(points),
         half_block(turn_sequences), half_block(points)] + tree_blocks,
        [whole((stat_rows, padded)), whole((pack_rows, padded))],
        [shape(stat_rows, padded), shape(pack_rows, padded)],
        [pltpu.VMEM((slots, 1, padded), F32), plan_scratch],
        (hand, loads, turn_cards, cards, hand_rank, mover_river, mover_river_price, rival_river, rival_river_price,
         mover_turn, mover_turn_price, rival_turn, rival_turn_price, river_children, river_parents), 5,
        vmem=56 * 2**20)
    gather_block = pl.BlockSpec((1, both, LANES), lambda at, ref: (ref[0], 0, 0))
    spread_block = pl.BlockSpec((1, LANES, both), lambda at, ref: (ref[0], 0, 0))
    prepared = [shape(slots, 1, both), shape(slots, 1, padded, dtype=BF16), shape(slots // group, both, group),
                shape(2, both, padded, dtype=BF16), shape(LANES, padded, dtype=BF16)] + [shape(2, *size, dtype=BF16) for size in operator_sizes]
    near_block = pl.BlockSpec((1, LANES, padded), lambda at, ref: (ref[0], 0, 0))
    tables = call(
        prepare_kernel_here, "prepare", 1, (1,),
        [smem(), smem(), card_block, gather_block, spread_block, half_block(slots), half_block(slots), near_block,
         whole(showdown_pot.shape), whole(river_fold.shape)] + tree_blocks,
        [vmem] * len(prepared), prepared, [],
        (hand, loads, turn_cards, cards, gather, spread, hand_rank, rank_far, near, showdown_pot, river_fold,
         river_children, river_parents), 2)
    live = tables[0]

    def gradients(value, early, y, y_far, u, pack, beside, stage):
        out = []
        hops = [1 << at for at in range(max(river_count - 1, 1).bit_length())]
        if river_count & (river_count - 1):
            value = lax.psum(value, "river")
            hops = []
        extra = None
        for place in range(max(len(hops), 1)):
            near_now = tables[4]
            if place:
                near_now, _ = lax.optimization_barrier((near_now, value))
            gate = []
            if place == min(stage, len(hops) - 1) or not hops:
                extra = beside(early, value)
                gate.extend(extra)
            while len(out) * group < slots and (len(out) <= place or place >= len(hops) - 1):
                first = len(out) * group
                arrays, specs, bases = zip(*(operand(item, first, group) for item in (y, y_far, u)))
                args = (*arrays, *tables[:4], near_now, *tables[5:], pack, river_parents)
                out.append(call(
                    functools.partial(mover_gradient_kernel, group, first, bases, turn_sequences), "mover_gradient", 0, (1,),
                    [*specs] + [vmem] * (len(args) - 3), [vmem] * 2,
                    [shape(group, sequences, padded), shape(group, infosets, padded)], [], args, group))
                gate.append(out[-1][1])
            if hops:
                value = hop_total(value, hops[place], gate)
                if place == 0:
                    value, early = lax.optimization_barrier((value, early))
        return [item[0] for item in out], [item[1] for item in out], (value, swap(value)), extra

    def mover_steps(last, norms, x, v, grad, flow):
        outs = []
        for first in range(0, slots, span):
            arrays, specs, bases = zip(*(operand(item, first, span) for item in (x, v)))
            here = slice(first // group, first // group + parts)
            args = (*norms, *arrays, live, *grad[here], *flow[here])
            in_specs = [vmem] * 2 + [*specs] + [vmem] * (1 + 2 * parts)
            aliases = {}
            if last:
                out_specs = [boards(sequences, group, first // group), boards(infosets, group, first // group), vmem]
                out_shape = [shape(slots, sequences, width), shape(slots, infosets, width), shape(span, sequences, padded)]
                if first:
                    aliases = {len(args): 0, len(args) + 1: 1}
                    in_specs += [any_block] * 2
                    args += tuple(outs[-1][:2])
            else:
                out_specs = [vmem] * 4
                out_shape = [shape(span, sequences, padded), shape(span, infosets, padded),
                             shape(span, sequences, padded), shape(8, padded)]
                if first:
                    in_specs += [vmem]
                    args += (outs[-1][3],)
            outs.append(call(functools.partial(mover_step_kernel, group, first, bases, count, parts, last),
                             "mover_step", 0, (parts if last else 1,), in_specs, out_specs, out_shape, [], args, parts, aliases))
        if last:
            return outs[-1][0], outs[-1][1], [item[2] for item in outs]
        return [item[0] for item in outs], [item[1] for item in outs], [item[2] for item in outs], outs[-1][3]

    def rival_steps(last, norms, bar, bar_far, y, u, new_v, flow, bar_turn, parts_before):
        outs = []
        for first in range(0, slots, span):
            arrays, specs, bases = zip(*(operand(item, first, group) for item in (bar, bar_far, y, u, new_v)))
            here = slice(first // group, first // group + parts)
            args = (*norms, *arrays, *tables, bar_turn, river_children, river_parents, *flow[here])
            in_specs = [vmem] * 2 + [*specs] + [vmem] * (len(args) - 7)
            aliases = {}
            scratch = [link_scratch, flow_scratch, step_scratch]
            if last:
                out_specs = [boards(sequences, group, first // group), boards(infosets, group, first // group)]
                out_shape = [shape(slots, sequences, width), shape(slots, infosets, width)]
                if first:
                    aliases = {len(args): 0, len(args) + 1: 1}
                    in_specs += [any_block] * 2
                    args += tuple(outs[-1][:2])
            else:
                out_specs = [vmem] * 3
                out_shape = [shape(span, sequences, padded), shape(span, infosets, padded), shape(total_rows, padded)]
                scratch = scratch + [plan_scratch]
                before = (outs[-1][2],) if first else tuple(parts_before)
                in_specs += [vmem] * len(before)
                args += before
            outs.append(call(functools.partial(rival_step_kernel, group, first, bases, count, parts, last),
                             "rival_step", 0, (parts,), in_specs, out_specs, out_shape, scratch, args, span, aliases))
        if last:
            return outs[-1]
        return [item[0] for item in outs], [item[1] for item in outs], outs[-1][2]

    turn_blocks = [smem(), card_block, gather_block, spread_block]
    turn_tables = (turn_cards, cards, gather, spread)
    turn_matrices = (turn_fold, turn_children, turn_parents, river_children, river_parents)

    def turn_call(first, data):
        if first:
            out_shape = [shape(pack_rows, both), shape(2 * infosets, both), shape(turn_sequences, both), shape(8, padded),
                         shape(8, LANES)]
        else:
            out_shape = [shape(turn_sequences, both), shape(turn_sequences, width), shape(points, width),
                         shape(turn_sequences, width), shape(points, width)]
        return call(
            functools.partial(turn_step_kernel, count, first, ("river", "hand")), "turn_step", 1, (1,),
            turn_blocks + [vmem] * len(data) + [whole(item.shape) for item in turn_matrices],
            [vmem] * 5 if first else [vmem] + [whole(item.shape) for item in out_shape[1:]],
            out_shape, [], (hand, *turn_tables, *data, *turn_matrices), 2)

    def turn_start(first, data):
        out_shape = [shape(turn_sequences, both), shape(points, both), shape(infosets, both),
                     shape(pack_rows if first else infosets, both)]
        return call(
            functools.partial(turn_start_kernel, first), "turn_start", 1, (1,),
            turn_blocks + [vmem] * 2 + [whole(item.shape) for item in turn_matrices], [vmem] * 4, out_shape, [],
            (hand, *turn_tables, *data, *turn_matrices), 1)

    def first_start(far, value):
        near_now, _ = lax.optimization_barrier((pack, value))
        return turn_start(True, (near_now, far))

    grad, flow, norms, starts = gradients(sums, swap(pack), rival_river, rival_far, rival_river_price, pack, first_start, 2)
    x, v, bar, part = mover_steps(False, norms, mover_river, mover_river_price, grad, flow)
    bar_far = [swap(item) for item in bar]
    pack, kept, bar_turn, turn_norms, turn_steps = turn_call(True, (starts[3], *starts[:3], *norms))
    y, u, total = rival_steps(False, norms, bar, bar_far, rival_river, rival_river_price, v, flow, bar_turn,
                              (part, turn_norms))
    y_far = [swap(item) for item in y]

    def second_start(far, value):
        now, _ = lax.optimization_barrier((pack, value))
        return turn_start(False, (now, bar_turn))

    grad, flow, norms, starts = gradients(total, y_far[0], y, y_far, u, pack, second_start, 0)
    next_x, next_v, bar = mover_steps(True, norms, x, v, grad, flow)
    bar_far = [swap(item) for item in bar]
    bar_turn, next_xt, next_vt, next_yt, next_ut = turn_call(False, (pack, *starts, kept, turn_steps, *norms))
    next_y, next_u = rival_steps(True, norms, bar, bar_far, y, u, next_v, flow, bar_turn, None)
    return (next_xt, next_x, next_vt, next_v, next_yt, next_y, next_ut, next_u)


def solution(mesh):
    river = P(("groups", "river"), None, "hand")
    turn = P("groups", "hand")
    placed = (P(("groups", "river"), "hand"), P("groups"), P("groups"), P(), P(), P(), P(), P(), P(), P(),
              turn, river, turn, river, turn, river, turn, river)
    return jax.shard_map(local, mesh=mesh, in_specs=placed,
                         out_specs=(turn, river, turn, river, turn, river, turn, river), check_vma=False)
```
